32 devices in a mesh: wide: 8 (over y, x, core), narrow: 4 (over z).
Axes of the slice: x: 2, y: 2, z: 4, core: 2. Of those that a mesh axis runs over, the one named last changes fastest.
Arguments:
- field: bfloat16 [512, 16384], P('narrow', 'wide'), may hold values from -6 to 6
- noise: bfloat16 [512, 16384], P('narrow', 'wide'), may hold values from -4 to 4
- norm_gain: bfloat16 [2, 2, 512], P(None, None, 'narrow'), may hold values from 0.5 to 1.5
- norm_bias: bfloat16 [2, 2, 512], P(None, None, 'narrow'), may hold values from -1.75 to 1.75
- mix_weight: bfloat16 [2, 2, 2, 512, 64], P(None, None, None, 'narrow'), may hold values from -0.5 to 0.5
- mix_bias: bfloat16 [2, 2, 2, 512], P(None, None, None, 'narrow'), may hold values from -1.75 to 1.75
- up_weight: bfloat16 [2, 512, 2048], P(None, None, 'narrow'), may hold values from -0.25 to 0.25
- up_bias: bfloat16 [2, 2048], P(None, 'narrow'), may hold values from -1.75 to 1.75
- down_weight: bfloat16 [2, 2048, 512], P(None, 'narrow'), may hold values from -0.125 to 0.125
- down_bias: bfloat16 [2, 512], P(None, 'narrow'), may hold values from -1.75 to 1.75
- out_grad: bfloat16 [512, 16384], P('narrow', 'wide'), may hold values from -6 to 6
Outputs:
- output: bfloat16 [512, 16384], P('narrow', 'wide')
- grad_field: float32 [512, 16384], P('narrow', 'wide')
- grad_norm_gain: float32 [2, 2, 512], P(None, None, 'narrow')
- grad_norm_bias: float32 [2, 2, 512], P(None, None, 'narrow')
- grad_mix_weight: float32 [2, 2, 2, 512, 64], P(None, None, None, 'narrow')
- grad_mix_bias: float32 [2, 2, 2, 512], P(None, None, None, 'narrow')
- grad_up_weight: float32 [2, 512, 2048], P(None, None, 'narrow')
- grad_up_bias: float32 [2, 2048], P(None, 'narrow')
- grad_down_weight: float32 [2, 2048, 512], P(None, 'narrow')
- grad_down_bias: float32 [2, 512], P(None, 'narrow')
The draws below stay inside these ranges and needn't reach their ends.
All inputs are finite; a program needn't handle non-finite values.
Results may differ from the reference program's by a relative error of at most 0.017.
Values may be sent and summed in bfloat16 or wider, within the bound.
No kernel may reach another device: no remote copies, remote signals or barrier semaphores. Data moves between devices by JAX's collectives and lax.ppermute only.
A program may use at most 128 MiB of HBM per device.

```python
import math
import jax
import jax.numpy as jnp
from jax import lax

D = 512
FF = 2048
BS = 64
MODES = 32
GRID = 64
LAYERS = 2
ITEMS = 4
CELLS = 16384


def draw_noise(key, part):
    key = jax.random.fold_in(key, 7)
    first_key, second_key = jax.random.split(key)
    base = jax.random.normal(first_key, (D, CELLS), jnp.float32)
    spread = jnp.exp(0.8 * jax.random.normal(second_key, (D, CELLS), jnp.float32))
    return jnp.clip(0.3 * base * spread, -4.0, 4.0).astype(jnp.bfloat16)


def draw_out_grad(key, part):
    key = jax.random.fold_in(key, 11)
    first_key, second_key = jax.random.split(key)
    base = jax.random.normal(first_key, (D, CELLS), jnp.float32)
    common = 0.8 * jax.random.normal(second_key, (1, CELLS), jnp.float32)
    return jnp.clip(base + common, -6.0, 6.0).astype(jnp.bfloat16)


def shard_levels(key, shape, cuts, least, top_value):
    def one(position, blocks):
        heights = jax.random.uniform(jax.random.fold_in(jax.random.fold_in(key, 6), position), (blocks,), jnp.float32, least / len(cuts), top_value / len(cuts))
        return jnp.repeat(jnp.exp(heights), shape[position] // blocks).reshape((-1,) + (1,) * (len(shape) - position - 1))

    level = one(*cuts[0])
    for cut in cuts[1:]:
        level = level * one(*cut)
    return level


def gaussian(key, dims, deviation, limit, pieces=(), kind=jnp.bfloat16):
    entries = deviation * jax.random.normal(key, dims, jnp.float32)
    if pieces:
        entries = entries * shard_levels(key, dims, pieces, -0.22, 0.18)
    return jnp.clip(entries, -limit, limit).astype(kind)


def setup_inputs(seed: int = 0) -> dict:
    streams_of = jax.random.split(jax.random.key(seed), 12)
    return {
        "field": gaussian(streams_of[0], (D, CELLS), 1.0, 6.0, ((0, 4), (1, 8))),
        "noise": draw_noise(jax.random.fold_in(streams_of[11], 71), 0),
        "norm_gain": jnp.clip(1.0 + 0.1 * jax.random.normal(streams_of[2], (LAYERS, 2, D), jnp.float32), 0.5, 1.5).astype(jnp.bfloat16),
        "norm_bias": gaussian(streams_of[3], (LAYERS, 2, D), 0.3, 1.75, ((2, 4),)),
        "mix_weight": gaussian(streams_of[4], (LAYERS, 2, 2, D, BS), (2 * BS) ** -0.5, 0.5, ((3, 4),)),
        "mix_bias": gaussian(streams_of[5], (LAYERS, 2, 2, D), 0.3, 1.75, ((3, 4),)),
        "up_weight": gaussian(streams_of[6], (LAYERS, D, FF), D ** -0.5, 0.25, ((2, 4),)),
        "up_bias": gaussian(streams_of[7], (LAYERS, FF), 0.3, 1.75, ((1, 4),)),
        "down_weight": gaussian(streams_of[8], (LAYERS, FF, D), FF ** -0.5, 0.125, ((1, 4),)),
        "down_bias": gaussian(streams_of[9], (LAYERS, D), 0.3, 1.75, ((1, 4),)),
        "out_grad": draw_out_grad(jax.random.fold_in(streams_of[11], 71), 0),
    }


eps = 1e-05
shrink = 0.1
highest = lax.Precision.HIGHEST

@jax.custom_vjp
def low(v):
    return lax.optimization_barrier(v.astype(jnp.bfloat16)).astype(jnp.float32)

@jax.custom_vjp
def low_back(v):
    return v

def low_keep(v):
    return (low(v), None)

def low_pass(kept, grad):
    return (grad,)

def back_keep(v):
    return (v, None)

def back_low(kept, grad):
    return (low(grad),)
low.defvjp(low_keep, low_pass)
low_back.defvjp(back_keep, back_low)

def spectral_table(first_row, row_count):
    cell_index = jnp.arange(row_count * GRID, dtype=jnp.int32)
    height = cell_index // GRID + first_row
    across = cell_index % GRID
    mode_index = jnp.arange(2 * MODES * MODES, dtype=jnp.int32)
    imaginary = mode_index // (MODES * MODES)
    along = mode_index // MODES % MODES
    freq_height = jnp.where(along < MODES // 2, along, along - MODES + GRID)
    freq_width = mode_index % MODES
    phase = (height[:, None] * freq_height[None, :] + across[:, None] * freq_width[None, :]) % GRID
    angle = phase.astype(jnp.float32) * (2.0 * math.pi / GRID)
    transform = jnp.where(imaginary[None, :] == 0, jnp.cos(angle), -jnp.sin(angle)) / GRID
    doubling = jnp.where(freq_width == 0, 1.0, 2.0).astype(jnp.float32)
    return (transform, doubling)

def normalize(values, gain, offset):
    center = values - lax.optimization_barrier(jnp.mean(values, axis=0))
    variance = lax.optimization_barrier(jnp.mean(center * center, axis=0))
    return center * lax.rsqrt(variance + eps) * gain[:, None] + offset[:, None]

def mixing_matrices(weight, offset):
    real_part = weight[0].reshape(-1, BS, BS)
    imag_part = weight[1].reshape(-1, BS, BS)
    top_rows = jnp.concatenate([real_part, imag_part], axis=2)
    bottom_rows = jnp.concatenate([-imag_part, real_part], axis=2)
    matrix = jnp.concatenate([top_rows, bottom_rows], axis=1)
    shifts = jnp.concatenate([offset[0].reshape(-1, BS), offset[1].reshape(-1, BS)], axis=1)
    return (matrix, shifts)

def to_blocks(spectrum):
    channels, item_count = (spectrum.shape[0], spectrum.shape[1])
    blocks = spectrum.reshape(channels // BS, BS, item_count, 2, MODES * MODES)
    return blocks.transpose(0, 3, 1, 2, 4).reshape(channels // BS, 2 * BS, item_count * MODES * MODES)

def from_blocks(blocks, item_count):
    block_count = blocks.shape[0]
    spectrum = blocks.reshape(block_count, 2, BS, item_count, MODES * MODES)
    return spectrum.transpose(0, 2, 3, 1, 4).reshape(block_count * BS, item_count, 2 * MODES * MODES)

def one_layer(state, gains, offsets, mix_weight, mix_bias, up_weight, up_bias, down_weight, down_bias, transform, doubling):
    normed_one = normalize(state, gains[0], offsets[0])
    item_cells = normed_one.reshape(D, ITEMS, GRID * GRID)
    spectrum = jnp.einsum('dic,ck->dik', item_cells, transform, precision=highest)
    spectrum_low = low(to_blocks(spectrum))
    matrix_one, shift_one = mixing_matrices(mix_weight[0], mix_bias[0])
    matrix_two, shift_two = mixing_matrices(mix_weight[1], mix_bias[1])
    mixed_one = low_back(jnp.einsum('bio,bim->bom', matrix_one, spectrum_low, precision=highest) + shift_one[:, :, None])
    active = low(jax.nn.gelu(mixed_one, approximate=False))
    mixed_two = low_back(jnp.einsum('bio,bim->bom', matrix_two, active, precision=highest) + shift_two[:, :, None])
    shrunk = mixed_two - shrink * jnp.tanh(mixed_two / shrink)
    synthesis = from_blocks(shrunk, ITEMS) * doubling
    filtered = jnp.einsum('dik,ck->dic', synthesis, transform, precision=highest).reshape(D, ITEMS * GRID * GRID)
    state = state + filtered + normed_one
    normed_two = low(normalize(state, gains[1], offsets[1]))
    before = low_back(jnp.dot(up_weight.T, normed_two, precision=highest) + up_bias[:, None])
    hidden = low(jax.nn.gelu(before, approximate=False))
    branch = low_back(jnp.dot(down_weight.T, hidden, precision=highest) + down_bias[:, None])
    return state + branch

def reference(field, noise, norm_gain, norm_bias, mix_weight, mix_bias, up_weight, up_bias, down_weight, down_bias, out_grad):
    transform, doubling = spectral_table(0, GRID)
    start = field.astype(jnp.float32) + noise.astype(jnp.float32)
    params = (norm_gain.astype(jnp.float32), norm_bias.astype(jnp.float32), mix_weight.astype(jnp.float32), mix_bias.astype(jnp.float32), up_weight.astype(jnp.float32), up_bias.astype(jnp.float32), down_weight.astype(jnp.float32), down_bias.astype(jnp.float32))

    def forward(state, weights):
        for layer_index in range(LAYERS):
            state = one_layer(state, weights[0][layer_index], weights[1][layer_index], weights[2][layer_index], weights[3][layer_index], weights[4][layer_index], weights[5][layer_index], weights[6][layer_index], weights[7][layer_index], transform, doubling)
        return state
    result, pullback = jax.vjp(forward, start, params)
    grad_start, grad_params = pullback(out_grad.astype(jnp.float32))
    return (result.astype(jnp.bfloat16), grad_start, grad_params[0], grad_params[1], grad_params[2], grad_params[3], grad_params[4], grad_params[5], grad_params[6], grad_params[7])
```

```python
import functools
import math

import jax
import jax.numpy as jnp
import numpy as np
from jax import lax
from jax.experimental import pallas as pl
from jax.experimental.pallas import tpu as pltpu
from jax.sharding import PartitionSpec as P

D = 512
FF = 2048
BS = 64
MODES = 32
GRID = 64
LAYERS = 2

NZ = 4
CH = D // NZ
CELLS = D
ROWS = 8
HALF = MODES // 2
MROWS = HALF * ROWS * 2
NMODE = HALF * MODES
SLICE = D // 8

eps = 1e-05
shrink = 0.1
f32 = jnp.float32
bf16 = jnp.bfloat16

NN = (((1,), (0,)), ((), ()))
NT = (((1,), (1,)), ((), ()))
TN = (((0,), (0,)), ((), ()))


def width_tables():
    kw = np.arange(MODES)[:, None] * np.arange(GRID)[None, :] % GRID
    angle = kw * (2.0 * math.pi / GRID)
    parts = np.stack([np.cos(angle), -np.sin(angle)], axis=1) / GRID
    eye = np.eye(ROWS)
    full = np.einsum("kpw,hg->khpgw", parts, eye).reshape(D, D)
    doubled = full.reshape(MODES, -1) * np.where(np.arange(MODES) == 0, 1.0, 2.0)[:, None]
    doubled = doubled.reshape(D, D)
    out = [full, doubled, full.T, doubled.T]
    return [np.ascontiguousarray(t).astype(bf16) for t in out]


def height_tables():
    along = np.arange(MODES)
    freq = np.where(along < MODES // 2, along, along - MODES + GRID)
    phase = np.arange(GRID)[:, None] * freq[None, :] % GRID
    angle = phase * (2.0 * math.pi / GRID)
    cosine, sine = np.cos(angle), np.sin(angle)
    from_real = np.stack([cosine, -sine], axis=1)
    from_imag = np.stack([sine, cosine], axis=1)
    table = np.stack([from_real, from_imag], axis=1)
    table = table.transpose(2, 3, 0, 1).reshape(2 * MODES, 2, GRID)
    both = np.stack(
        [
            np.concatenate([table[:, c], table[:, 1 - c]], axis=1)
            for c in range(2)
        ]
    )
    return both.astype(bf16), np.ascontiguousarray(both.transpose(0, 2, 1)).astype(bf16)


def sds(shape, dtype):
    return jax.ShapeDtypeStruct(shape, dtype)


def launch(body, name, ids, arrays, outs, scratch=(), anys=(), flops=0, vmem=40):
    in_specs = [pl.BlockSpec(memory_space=pltpu.SMEM)]
    for place in range(len(arrays)):
        space = pl.ANY if place in anys else pltpu.VMEM
        in_specs.append(pl.BlockSpec(memory_space=space))
    size = sum(math.prod(a.shape) * a.dtype.itemsize for a in list(arrays) + list(outs))
    return pl.pallas_call(
        body,
        name=name,
        out_shape=list(outs),
        in_specs=in_specs,
        out_specs=[pl.BlockSpec(memory_space=pltpu.VMEM) for _ in outs],
        scratch_shapes=list(scratch),
        compiler_params=pltpu.CompilerParams(vmem_limit_bytes=vmem * 2**20),
        cost_estimate=pl.CostEstimate(flops=flops, bytes_accessed=size, transcendentals=0),
    )(ids, *arrays)


def dot(a, b, dims=NN):
    return lax.dot_general(a, b, dims, preferred_element_type=f32)


def at(offset, size):
    return pl.ds(pl.multiple_of(offset, size), size)


def gelu_parts(v):
    cdf = 0.5 + 0.5 * lax.erf(v * (2.0**-0.5))
    slope = cdf + v * (jnp.exp(-0.5 * v * v) * ((2.0 * math.pi) ** -0.5))
    return v * cdf, slope


def column(row):
    size = row.shape[1]
    wide = jnp.broadcast_to(row, (size, size))
    on = lax.broadcasted_iota(jnp.int32, (size, size), 0) == lax.broadcasted_iota(
        jnp.int32, (size, size), 1
    )
    return jnp.sum(jnp.where(on, wide, 0.0), axis=1, keepdims=True)


def norm_rows(v, gain, shift):
    mean = jnp.mean(v, axis=1, keepdims=True)
    center = v - mean
    scale = lax.rsqrt(jnp.mean(center * center, axis=1, keepdims=True) + eps)
    unit = center * scale
    return unit * gain + shift, unit, scale


def norm_rows_back(dy, unit, scale, gain):
    dx = dy * gain
    mean = jnp.mean(dx, axis=1, keepdims=True)
    along = jnp.mean(dx * unit, axis=1, keepdims=True)
    back = scale * (dx - mean - unit * along)
    return back, jnp.sum(dy * unit, axis=0, keepdims=True), jnp.sum(dy, axis=0, keepdims=True)


def stats_body(ids, field, noise, out):
    v = field[...].astype(f32) + noise[...].astype(f32)
    total = jnp.sum(v, axis=0, keepdims=True)
    center = v - total * (1.0 / CH)
    out[0:1, :] = total
    out[1:2, :] = jnp.sum(center * center, axis=0, keepdims=True)


def first_body(ids, field, noise, gain, shift, s0, s1, s2, s3, table, keep, send, ms):
    core = ids[0]
    sums = [s0, s1, s2, s3]
    mean = (s0[0:1, :] + s1[0:1, :] + s2[0:1, :] + s3[0:1, :]) * (1.0 / D)
    second = jnp.zeros_like(mean)
    for s in sums:
        apart = s[0:1, :] * (1.0 / CH) - mean
        second = second + s[1:2, :] + CH * (apart * apart)
    scale = lax.rsqrt(second * (1.0 / D) + eps)
    ms[0:1, :] = mean
    ms[1:2, :] = scale
    v = field[...].astype(f32) + noise[...].astype(f32)
    normed = (v - mean) * scale * column(gain[...]) + column(shift[...])
    normed = normed.astype(bf16)
    mine = table[at(core * MROWS, MROWS), :]
    other = table[at((1 - core) * MROWS, MROWS), :]
    for s in range(NZ):
        part = normed[:, s * CELLS : (s + 1) * CELLS]
        keep[s] = dot(mine, part, NT).astype(bf16)
        send[s] = dot(other, part, NT).astype(bf16)


def second_body(
    ids, field, noise, gain, shift, ms, keep, recv, table, p0, p1, p2, p3, modes, cells
):
    core, z = ids[0], ids[1]
    for s in range(NZ):
        modes[at(core * MROWS, MROWS), s * CH : (s + 1) * CH] = keep[s]
        modes[at((1 - core) * MROWS, MROWS), s * CH : (s + 1) * CH] = recv[s]
    v = field[...].astype(f32) + noise[...].astype(f32)
    normed = (v - ms[0:1, :]) * ms[1:2, :] * column(gain[...]) + column(shift[...])
    both = v + normed
    filtered = dot(table[...], modes[...])
    for s in range(NZ):
        piece = filtered[:, s * CH : (s + 1) * CH] + both[:, s * CELLS : (s + 1) * CELLS].T
        cells[s] = piece.astype(bf16)
    for m, out in enumerate((p0, p1, p2, p3)):
        out[...] = cells[z ^ m]


def return_body(ids, g0, g1, g2, g3, table, keep, send, wide, modes):
    core, z = ids[0], ids[1]
    for m, g in enumerate((g0, g1, g2, g3)):
        wide[:, at((z ^ m) * CH, CH)] = g[...]
    modes[...] = dot(table[...], wide[...]).astype(bf16)
    for s in range(NZ):
        keep[s] = modes[at(core * MROWS, MROWS), s * CH : (s + 1) * CH]
        send[s] = modes[at((1 - core) * MROWS, MROWS), s * CH : (s + 1) * CH]


def last_body(
    ids, field, noise, ms, gain, g0, g1, g2, g3, keep, recv, table, base, sums, small, modes, wide
):
    core, z = ids[0], ids[1]
    for m, g in enumerate((g0, g1, g2, g3)):
        wide[:, at((z ^ m) * CH, CH)] = g[...]
    for s in range(NZ):
        modes[at(core * MROWS, MROWS), s * CH : (s + 1) * CH] = keep[s]
        modes[at((1 - core) * MROWS, MROWS), s * CH : (s + 1) * CH] = recv[s]
    grad = wide[...].astype(f32)
    dy_cells = dot(table[...], modes[...]) + grad
    col = column(gain[...])
    gain_sum = jnp.zeros((CH, 1), f32)
    shift_sum = jnp.zeros((CH, 1), f32)
    for s in range(NZ):
        here = slice(s * CELLS, (s + 1) * CELLS)
        dy = dy_cells[:, s * CH : (s + 1) * CH].T
        g = grad[:, s * CH : (s + 1) * CH].T
        v = field[:, here].astype(f32) + noise[:, here].astype(f32)
        unit = (v - ms[0:1, here]) * ms[1:2, here]
        dx = dy * col
        along = dx * unit
        sums[0:1, here] = jnp.sum(dx, axis=0, keepdims=True)
        sums[1:2, here] = jnp.sum(along, axis=0, keepdims=True)
        base[:, here] = g + ms[1:2, here] * dx
        gain_sum = gain_sum + jnp.sum(dy * unit, axis=1, keepdims=True)
        shift_sum = shift_sum + jnp.sum(dy, axis=1, keepdims=True)
    on = lax.broadcasted_iota(jnp.int32, (CH, CH), 0) == lax.broadcasted_iota(
        jnp.int32, (CH, CH), 1
    )
    small[0:1, :] = jnp.sum(jnp.where(on, gain_sum, 0.0), axis=0, keepdims=True)
    small[1:2, :] = jnp.sum(jnp.where(on, shift_sum, 0.0), axis=0, keepdims=True)


def close_body(ids, field, noise, ms, base, s0, s1, s2, s3, out):
    mean = (s0[0:1, :] + s1[0:1, :] + s2[0:1, :] + s3[0:1, :]) * (1.0 / D)
    along = (s0[1:2, :] + s1[1:2, :] + s2[1:2, :] + s3[1:2, :]) * (1.0 / D)
    v = field[...].astype(f32) + noise[...].astype(f32)
    unit = (v - ms[0:1, :]) * ms[1:2, :]
    out[...] = base[...] - ms[1:2, :] * (mean + unit * along)


def to_spectrum(table, keep, recv, out, order):
    for k in range(HALF):
        rows = slice(2 * ROWS * k, 2 * ROWS * (k + 1))
        block = jnp.concatenate(
            [group[s ^ order, rows, :] for group in (keep, recv) for s in range(NZ)], axis=0
        )
        modes = dot(table, block).astype(out.dtype)
        out[MODES * k : MODES * (k + 1), :CH] = modes[:MODES]
        out[MODES * k : MODES * (k + 1), CH:] = modes[MODES:]


def from_spectrum(table, spectrum, keep, send, order):
    for k in range(HALF):
        rows = slice(2 * ROWS * k, 2 * ROWS * (k + 1))
        here = slice(MODES * k, MODES * (k + 1))
        block = jnp.concatenate([spectrum[here, :CH], spectrum[here, CH:]], axis=0)
        cells = dot(table, block).astype(bf16)
        for s in range(NZ):
            keep[s ^ order, rows, :] = cells[2 * ROWS * s : 2 * ROWS * (s + 1)]
            send[s ^ order, rows, :] = cells[2 * ROWS * (NZ + s) : 2 * ROWS * (NZ + s + 1)]


def mix_body(
    ids, keep_in, recv, table, back_table, matrix, shift,
    keep, send, spectrum, active, slope, square, shrunk,
):
    core, order = ids[0], ids[3]
    to_spectrum(table[core], keep_in, recv, spectrum, order)
    one = dot(spectrum[...], matrix[0]) + shift[0:1, :]
    value, inner = gelu_parts(one)
    slope[...] = inner
    active[...] = value.astype(bf16)
    two = dot(active[...], matrix[1]) + shift[1:2, :]
    bend = jnp.tanh(two * (1.0 / shrink))
    square[...] = bend * bend
    shrunk[...] = (two - shrink * bend).astype(bf16)
    from_spectrum(back_table[core], shrunk, keep, send, order)


def mix_back_body(
    ids, keep_in, recv, table, back_table, matrix, spectrum, active, slope, square,
    keep, send, sums, modes, low_one, low_two,
):
    core, order = ids[0], ids[3]
    to_spectrum(table[core], keep_in, recv, modes, order)
    low_two[...] = (modes[...] * square[...]).astype(bf16)
    low_one[...] = (dot(low_two[...], matrix[1], NT) * slope[...]).astype(bf16)
    modes[...] = dot(low_one[...], matrix[0], NT)
    low = modes[...].astype(bf16)
    from_spectrum(back_table[core], low, keep, send, order)
    lane = lax.broadcasted_iota(jnp.int32, (BS, CH), 1)
    for j, (left, right) in enumerate(((spectrum, low_one), (active, low_two))):
        product = dot(left[...], right[...], TN)
        real = product[:CH, :CH] + product[CH:, CH:]
        imag = product[:CH, CH:] - product[CH:, :CH]
        top, middle = j * CH, j * CH + BS
        sums[top:middle, :] = jnp.where(lane < BS, real[:BS], pltpu.roll(imag[:BS], BS, 1))
        sums[middle : middle + BS, :] = jnp.where(
            lane < BS, pltpu.roll(real[BS:], BS, 1), imag[BS:]
        )
        total = jnp.sum(right[...].astype(f32), axis=0, keepdims=True)
        last = 2 * CH + 2 * j
        sums[last : last + 1, :] = total[:, :CH]
        sums[last + 1 : last + 2, :] = total[:, CH:]
    sums[2 * CH + 4 :, :] = jnp.zeros((4, CH), f32)


def weight_copies(layer, ids, up, down, pieces, store, sems):
    core_pos = ids[2]
    copies = [
        pltpu.make_async_copy(up.at[layer], store.at[0, 0], sems.at[0]),
        pltpu.make_async_copy(down.at[layer], store.at[0, 1], sems.at[1]),
    ]
    for e, piece in enumerate(pieces):
        row = (core_pos ^ e) * SLICE
        copies.append(
            pltpu.make_async_copy(
                piece, store.at[pl.ds(1, NZ - 1), :, at(row, SLICE), :], sems.at[2 + e]
            )
        )
    for copy in copies:
        copy.start()
    return copies


def gather_lanes(pieces, z, wide):
    for m, piece in enumerate(pieces):
        wide[:, at((z ^ m) * CH, CH)] = piece[...]


def gather_modes(pieces, ids, wide):
    core, z = ids[0], ids[1]
    for m, piece in enumerate(pieces):
        lanes = at((z ^ m) * CH, CH)
        wide[at(core * MROWS, MROWS), lanes] = piece[0]
        wide[at((1 - core) * MROWS, MROWS), lanes] = piece[1]


def scatter_lanes(wide, z, pieces):
    for m, piece in enumerate(pieces):
        piece[...] = wide[:, at((z ^ m) * CH, CH)].astype(piece.dtype)


def small_rows(pieces, first, z, rows, ups):
    for m, piece in enumerate(pieces):
        piece[first : first + 8, :] = rows[0:8, at((z ^ m) * CH, CH)]
        for q in range(4):
            piece[first + 8 + q : first + 9 + q, :] = ups[m : m + 1, q * CH : (q + 1) * CH]
        piece[first + 12 : first + 16, :] = jnp.zeros((4, CH), f32)


def cells_one_body(
    ids, p0, p1, p2, p3, vectors, up_shift, up, down, e0, e1, e2, e3, e4, e5, e6, e7, table,
    a0, a1, a2, a3, base, unit_one, scale_one, low_two, unit_two, scale_two, hidden, slope,
    store, sems, wide, total,
):
    z = ids[1]
    copies = weight_copies(0, ids, up, down, (e0, e1, e2, e3, e4, e5, e6, e7), store, sems)
    gather_lanes((p0, p1, p2, p3), z, wide)
    state = wide[...].astype(f32)
    normed, unit, scale = norm_rows(state, vectors[1:2, :], vectors[5:6, :])
    low_two[...] = normed.astype(bf16)
    unit_two[...] = unit.astype(bf16)
    scale_two[...] = jnp.broadcast_to(scale, (CELLS, CH))
    total[...] = state + vectors[8:9, :]
    for copy in copies:
        copy.wait()

    @pl.loop(0, NZ)
    def _(j):
        before = dot(low_two[...], store[j, 0]) + up_shift[pl.ds(j, 1), :]
        value, inner = gelu_parts(before)
        hidden[j] = value.astype(bf16)
        slope[j] = inner.astype(bf16)
        total[...] += dot(hidden[j], store[j, 1])

    state = total[...]
    normed, unit, scale = norm_rows(state, vectors[2:3, :], vectors[6:7, :])
    base[...] = state + normed
    unit_one[...] = unit.astype(bf16)
    scale_one[...] = jnp.broadcast_to(scale, (CELLS, CH))
    total[...] = dot(table[...], normed.astype(bf16))
    scatter_lanes(total, z, (a0, a1, a2, a3))


def cells_two_body(
    ids, b0, b1, b2, b3, base, r0, r1, r2, r3, vectors, up_shift, up, down,
    e0, e1, e2, e3, e4, e5, e6, e7, back_table, table,
    a0, a1, a2, a3, o0, o1, o2, o3, grad, low_two, low_grad, hidden, grad_before, n0, n1, n2, n3,
    store, sems, wide, total, other, sums, unit_two,
):
    z = ids[1]
    copies = weight_copies(1, ids, up, down, (e0, e1, e2, e3, e4, e5, e6, e7), store, sems)
    gather_modes((b0, b1, b2, b3), ids, wide)
    state = base[...] + dot(back_table[...], wide[...])
    normed, unit, scale = norm_rows(state, vectors[3:4, :], vectors[7:8, :])
    low_two[...] = normed.astype(bf16)
    unit_two[...] = unit
    total[...] = state + vectors[9:10, :]
    other[...] = jnp.zeros_like(other)
    for m, piece in enumerate((r0, r1, r2, r3)):
        low_grad[:, at((z ^ m) * CH, CH)] = piece[...].T
    for copy in copies:
        copy.wait()

    @pl.loop(0, NZ)
    def _(j):
        before = dot(low_two[...], store[j, 0]) + up_shift[pl.ds(j, 1), :]
        value, inner = gelu_parts(before)
        hidden[j] = value.astype(bf16)
        total[...] += dot(hidden[j], store[j, 1])
        late = dot(low_grad[...], store[j, 1], NT) * inner
        grad_before[j] = late.astype(bf16)
        sums[pl.ds(j, 1), :] = jnp.sum(grad_before[j].astype(f32), axis=0, keepdims=True)
        other[...] += dot(grad_before[j], store[j, 0], NT)

    scatter_lanes(total, z, (o0, o1, o2, o3))
    gradient = low_grad[...].astype(f32)
    back, gain_row, shift_row = norm_rows_back(other[...], unit_two[...], scale, vectors[3:4, :])
    grad[...] = gradient + back
    total[...] = dot(table[...], grad[...].astype(bf16))
    scatter_lanes(total, z, (a0, a1, a2, a3))
    other[0:1, :] = gain_row
    other[1:2, :] = shift_row
    other[2:3, :] = jnp.sum(gradient, axis=0, keepdims=True)
    small_rows((n0, n1, n2, n3), 0, z, other, sums)


def cells_three_body(
    ids, b0, b1, b2, b3, grad, unit_one, scale_one, unit_two, scale_two, slope, vectors,
    up, down, e0, e1, e2, e3, e4, e5, e6, e7, back_table, n0, n1, n2, n3,
    g0, g1, g2, g3, low_grad, grad_before, v0, v1, v2, v3,
    store, sems, wide, total, other, sums,
):
    z = ids[1]
    copies = weight_copies(0, ids, up, down, (e0, e1, e2, e3, e4, e5, e6, e7), store, sems)
    gather_modes((b0, b1, b2, b3), ids, wide)
    dy = grad[...] + dot(back_table[...], wide[...])
    back, gain_one, shift_one = norm_rows_back(
        dy, unit_one[...].astype(f32), scale_one[:, 0:1], vectors[2:3, :]
    )
    total[...] = grad[...] + back
    low_grad[...] = total[...].astype(bf16)
    other[...] = jnp.zeros_like(other)
    for copy in copies:
        copy.wait()

    @pl.loop(0, NZ)
    def _(j):
        late = dot(low_grad[...], store[j, 1], NT) * slope[j].astype(f32)
        grad_before[j] = late.astype(bf16)
        sums[pl.ds(j, 1), :] = jnp.sum(grad_before[j].astype(f32), axis=0, keepdims=True)
        other[...] += dot(grad_before[j], store[j, 0], NT)

    back, gain_two, shift_two = norm_rows_back(
        other[...], unit_two[...].astype(f32), scale_two[:, 0:1], vectors[1:2, :]
    )
    total[...] += back
    scatter_lanes(total, z, (g0, g1, g2, g3))
    other[0:1, :] = gain_two
    other[1:2, :] = shift_two
    other[2:3, :] = jnp.sum(low_grad[...].astype(f32), axis=0, keepdims=True)
    other[3:4, :] = gain_one
    other[4:5, :] = shift_one
    for v, n in zip((v0, v1, v2, v3), (n0, n1, n2, n3)):
        v[0:16, :] = n[...]
    small_rows((v0, v1, v2, v3), 16, z, other, sums)


def weights_body(
    ids, low_two, low_grad, hidden, grad_before,
    k0, k2, k4, k6, s0, s2, s4, s6, left, product,
):
    place = ids[2]
    left[0] = low_two[...].T
    left[1] = low_grad[...].T

    @pl.loop(0, NZ)
    def _(j):
        for side in range(2):
            right = grad_before if side == 0 else hidden
            product[...] = dot(left[side], right[j]).astype(bf16)
            for e, out in enumerate((k0, s0, k2, s2, k4, s4, k6, s6)):
                out[j, side] = product[at((place ^ e) * SLICE, SLICE), :]


def output_body(ids, o0, o1, o2, o3, out):
    z = ids[1]
    for m, piece in enumerate((o0, o1, o2, o3)):
        out[:, at((z ^ m) * CELLS, CELLS)] = piece[...].T


def weights_out_body(ids, *refs):
    place = ids[2]
    pieces, (up, down, whole) = refs[: 8 * LAYERS], refs[8 * LAYERS :]
    for layer in range(LAYERS):
        for e in range(8):
            row = at((place ^ e) * SLICE, SLICE)
            up[layer, row, :] = pieces[8 * layer + e][0].astype(f32)
            whole[row, :] = pieces[8 * layer + e][1]
        down[layer] = whole[...].T.astype(f32)


def swap(value, axis, mask):
    pairs = [(source, source ^ mask) for source in range(lax.axis_size(axis))]
    return lax.ppermute(value, axis, pairs)


def exchange(pieces):
    return [pieces[0]] + [swap(pieces[m], "narrow", m) for m in range(1, NZ)]


def wide_total(value):
    mask = 1
    while mask < lax.axis_size("wide"):
        value = value + swap(value, "wide", mask)
        mask *= 2
    return value


def gather_weights(up, down, place):
    row = place * SLICE
    mine = jnp.stack([lax.dynamic_slice_in_dim(w, row, SLICE, 0) for w in (up, down)])
    held = jnp.stack([swap(mine, "narrow", m) for m in range(1, NZ)])
    near = [held] + [swap(held, "wide", q) for q in (2, 4, 6)]
    pieces = []
    for value in near:
        pieces += [value, swap(value, "wide", 1)]
    return pieces


def reduce_weights(keep, send):
    arrived = [swap(value, "wide", 1) for value in send]
    sums = [a.astype(f32) + b.astype(f32) for a, b in zip(keep, arrived)]
    plane = [swap(sums[i].astype(bf16), "wide", 2 * i) for i in (1, 2, 3)]
    total = []
    for m in range(NZ):
        part = sums[0][m]
        for value in plane:
            part = part + value[m].astype(f32)
        total.append(part)
    result = total[0]
    for m in range(1, NZ):
        result = result + swap(total[m].astype(bf16), "narrow", m).astype(f32)
    mask = 8
    while mask < lax.axis_size("wide"):
        result = result + swap(result.astype(bf16), "wide", mask).astype(f32)
        mask *= 2
    mine = result.astype(bf16)
    near = [mine] + [swap(mine, "wide", q) for q in (2, 4, 6)]
    pieces = []
    for value in near:
        pieces += [value, swap(value, "wide", 1)]
    return pieces


def to_mode_layout(pieces, core):
    held = jnp.stack(exchange(pieces)).reshape(NZ, 2, MROWS, CH)
    keep = lax.dynamic_index_in_dim(held, core, 1, keepdims=False)
    send = lax.dynamic_index_in_dim(held, 1 - core, 1, keepdims=False)
    return keep, swap(send, "wide", 1)


def to_cell_layout(keep, send):
    arrived = swap(send, "wide", 1)
    return exchange([jnp.stack([keep[m], arrived[m]]) for m in range(NZ)])


def mixing_matrices(weight):
    on = np.kron(np.eye(2), np.ones((BS, BS))).astype(bool)
    wide = jnp.where(on, jnp.concatenate([weight, weight], axis=-1), 0)
    real, imag = wide[:, :, 0], wide[:, :, 1]
    top = jnp.concatenate([real, imag], axis=-1)
    bottom = jnp.concatenate([-imag, real], axis=-1)
    return jnp.concatenate([top, bottom], axis=-2)


def shards(
    field,
    noise,
    norm_gain,
    norm_bias,
    mix_weight,
    mix_bias,
    up_weight,
    up_bias,
    down_weight,
    down_bias,
    out_grad,
):
    wide, z = lax.axis_index("wide"), lax.axis_index("narrow")
    core, place = wide % 2, wide % 8
    ids = jnp.stack([core, z, place, z]).astype(jnp.int32)
    ids_first = jnp.stack([core, z, place, jnp.zeros_like(z)]).astype(jnp.int32)
    table, doubled, table_back, doubled_back = width_tables()
    height, height_back = height_tables()

    own = launch(stats_body, "stats", ids, [field, noise], [sds((2, NZ * CELLS), f32)])[0]
    first_sums = [own] + [swap(own, "narrow", m) for m in range(1, NZ)]

    packed = jnp.concatenate(
        [
            norm_gain.reshape(4, CH),
            norm_bias.reshape(4, CH),
            down_bias,
            up_bias.reshape(2 * NZ, CH),
            jnp.zeros((14, CH), bf16),
        ]
    )
    packs = jnp.stack(exchange([packed] * NZ)).astype(f32)
    vectors = packs[jnp.arange(NZ) ^ z, :10].transpose(1, 0, 2).reshape(10, D)
    up_shift = [packs[:, 10 + 4 * l : 14 + 4 * l].reshape(NZ, D) for l in range(LAYERS)]
    pieces = [gather_weights(up_weight[l], down_weight[l], place) for l in range(LAYERS)]
    matrices = mixing_matrices(mix_weight)
    shifts = mix_bias.astype(f32).reshape(LAYERS, 2, 2 * CH)
    first_gain = norm_gain[0, 0][None].astype(f32)
    first_shift = norm_bias[0, 0][None].astype(f32)

    half = sds((NZ, MROWS, CH), bf16)
    piece = sds((CELLS, CH), bf16)
    mode_low = sds((NMODE, 2 * CH), bf16)
    mode_f32 = sds((NMODE, 2 * CH), f32)
    cells_f32 = sds((CELLS, D), f32)
    cells_low = sds((CELLS, D), bf16)
    thin = sds((CELLS, CH), f32)
    chunks = sds((NZ, CELLS, D), bf16)
    vector = sds((16, CH), f32)
    weight_scratch = [
        pltpu.VMEM((NZ, 2, D, D), bf16),
        pltpu.SemaphoreType.DMA((10,)),
        pltpu.VMEM((D, D), bf16),
        pltpu.VMEM((CELLS, D), f32),
    ]

    def mix(layer, keep, recv, numbers):
        return launch(
            mix_body,
            "mix",
            numbers,
            [keep, recv, height, height_back, matrices[layer], shifts[layer]],
            [half, half, mode_low, mode_low, mode_f32, mode_f32],
            [pltpu.VMEM((NMODE, 2 * CH), bf16)],
            flops=2 * 10**8,
        )

    def mix_back(layer, keep, recv, saved, numbers):
        return launch(
            mix_back_body,
            "mix_back",
            numbers,
            [keep, recv, height, height_back, matrices[layer], *saved],
            [half, half, sds((2 * CH + 8, CH), f32)],
            [
                pltpu.VMEM((NMODE, 2 * CH), f32),
                pltpu.VMEM((NMODE, 2 * CH), bf16),
                pltpu.VMEM((NMODE, 2 * CH), bf16),
            ],
            flops=3 * 10**8,
        )

    keep, send, ms = launch(
        first_body,
        "first",
        ids,
        [field, noise, first_gain, first_shift, *first_sums, table],
        [half, half, sds((2, NZ * CELLS), f32)],
        flops=3 * 10**8,
    )
    keep, send, *saved_zero = mix(0, keep, swap(send, "wide", 1), ids_first)
    state = launch(
        second_body,
        "second",
        ids,
        [field, noise, first_gain, first_shift, ms, keep, swap(send, "wide", 1), doubled_back],
        [piece] * NZ,
        [pltpu.VMEM((D, D), bf16), pltpu.VMEM((NZ, CELLS, CH), bf16)],
        flops=3 * 10**8,
    )
    state = exchange(state)

    a0, a1, a2, a3, base, unit_one, scale_one, low_zero, unit_two, scale_two, hidden_zero, slope = (
        launch(
            cells_one_body,
            "cells_one",
            ids,
            [*state, vectors, up_shift[0], up_weight, down_weight, *pieces[0], table],
            [piece] * NZ
            + [cells_f32, cells_low, thin, cells_low, cells_low, thin, chunks, chunks],
            weight_scratch,
            anys=range(6, 16),
            flops=3 * 10**9,
        )
    )

    keep, recv = to_mode_layout([a0, a1, a2, a3], core)
    keep, send, *saved_one = mix(1, keep, recv, ids)
    modes = to_cell_layout(keep, send)

    late = [
        lax.dynamic_slice_in_dim(out_grad, (z ^ m) * CELLS, CELLS, 1) for m in range(NZ)
    ]
    late = exchange(late)

    *outs, grad, low_one, grad_one, hidden_one, before_one, n0, n1, n2, n3 = launch(
        cells_two_body,
        "cells_two",
        ids,
        [*modes, base, *late, vectors, up_shift[1], up_weight, down_weight, *pieces[1]]
        + [doubled_back, doubled],
        [piece] * 8 + [cells_f32, cells_low, cells_low, chunks, chunks] + [vector] * NZ,
        weight_scratch
        + [
            pltpu.VMEM((CELLS, D), f32),
            pltpu.VMEM((NZ, D), f32),
            pltpu.VMEM((CELLS, D), f32),
        ],
        anys=range(11, 21),
        flops=6 * 10**9,
    )

    def weight_sums(low, grad_low, hidden, before):
        eight = [sds((NZ, 2, SLICE, D), bf16)] * 8
        *out, = launch(
            weights_body,
            "weights",
            ids,
            [low, grad_low, hidden, before],
            eight,
            [pltpu.VMEM((2, D, CELLS), bf16), pltpu.VMEM((D, D), bf16)],
            flops=2 * 10**9,
        )
        return reduce_weights(out[:4], out[4:])

    keep, recv = to_mode_layout(outs[:NZ], core)
    keep, send, mix_sum_one = mix_back(1, keep, recv, saved_one, ids)
    modes = to_cell_layout(keep, send)
    weights_one = weight_sums(low_one, grad_one, hidden_one, before_one)
    mix_sum_one = wide_total(mix_sum_one)

    output = launch(
        output_body, "output", ids, exchange(outs[NZ:]), [sds((CH, NZ * CELLS), bf16)]
    )[0]

    g0, g1, g2, g3, grad_zero, before_zero, v0, v1, v2, v3 = launch(
        cells_three_body,
        "cells_three",
        ids,
        [*modes, grad, unit_one, scale_one, unit_two, scale_two, slope, vectors]
        + [up_weight, down_weight, *pieces[0], table_back, n0, n1, n2, n3],
        [piece] * NZ + [cells_low, chunks] + [sds((32, CH), f32)] * NZ,
        weight_scratch + [pltpu.VMEM((CELLS, D), f32), pltpu.VMEM((NZ, D), f32)],
        anys=range(11, 21),
        flops=4 * 10**9,
    )
    gradient = exchange([g0, g1, g2, g3])
    weights_zero = weight_sums(low_zero, grad_zero, hidden_zero, before_zero)
    vector_sum = wide_total(functools.reduce(jnp.add, exchange([v0, v1, v2, v3])))

    keep, send = launch(
        return_body,
        "return",
        ids,
        [*gradient, doubled],
        [half, half],
        [pltpu.VMEM((CELLS, D), bf16), pltpu.VMEM((D, D), bf16)],
        flops=3 * 10**8,
    )
    keep, send, mix_sum_zero = mix_back(0, keep, swap(send, "wide", 1), saved_zero, ids_first)
    mix_sum_zero = wide_total(mix_sum_zero)
    base, sums, first_small = launch(
        last_body,
        "last",
        ids,
        [field, noise, ms, first_gain, *gradient, keep, swap(send, "wide", 1), table_back],
        [sds((CH, NZ * CELLS), f32), sds((2, NZ * CELLS), f32), sds((8, CH), f32)],
        [pltpu.VMEM((D, D), bf16), pltpu.VMEM((CELLS, D), bf16)],
        flops=3 * 10**8,
    )
    first_small = wide_total(first_small)
    last_sums = [sums] + [swap(sums, "narrow", m) for m in range(1, NZ)]
    grad_field = launch(
        close_body,
        "close",
        ids,
        [field, noise, ms, base, *last_sums],
        [sds((CH, NZ * CELLS), f32)],
    )[0]

    grad_up, grad_down = launch(
        weights_out_body,
        "weights_out",
        ids,
        [*weights_zero, *weights_one],
        [sds((LAYERS, D, D), f32)] * 2,
        [pltpu.VMEM((D, D), bf16)],
    )

    one, zero = vector_sum[:16], vector_sum[16:]
    grad_gain = jnp.stack([first_small[0], zero[0], zero[3], one[0]]).reshape(2, 2, CH)
    grad_shift = jnp.stack([first_small[1], zero[1], zero[4], one[1]]).reshape(2, 2, CH)
    grad_down_bias = jnp.stack([zero[2], one[2]])
    grad_up_bias = jnp.stack([zero[8:12].reshape(D), one[8:12].reshape(D)])
    mixed = jnp.stack([mix_sum_zero, mix_sum_one])
    grad_mix = mixed[:, : 2 * CH].reshape(LAYERS, 2, CH, 2, BS).transpose(0, 1, 3, 2, 4)
    grad_mix_bias = mixed[:, 2 * CH : 2 * CH + 4].reshape(LAYERS, 2, 2, CH)
    return (
        output,
        grad_field,
        grad_gain,
        grad_shift,
        grad_mix,
        grad_mix_bias,
        grad_up,
        grad_up_bias,
        grad_down,
        grad_down_bias,
    )


def solution(mesh):
    placed = (
        P("narrow", "wide"),
        P("narrow", "wide"),
        P(None, None, "narrow"),
        P(None, None, "narrow"),
        P(None, None, None, "narrow", None),
        P(None, None, None, "narrow"),
        P(None, None, "narrow"),
        P(None, "narrow"),
        P(None, "narrow", None),
        P(None, "narrow"),
        P("narrow", "wide"),
    )
    return jax.shard_map(
        shards,
        mesh=mesh,
        in_specs=placed,
        out_specs=(
            P("narrow", "wide"),
            P("narrow", "wide"),
            P(None, None, "narrow"),
            P(None, None, "narrow"),
            P(None, None, None, "narrow", None),
            P(None, None, None, "narrow"),
            P(None, None, "narrow"),
            P(None, "narrow"),
            P(None, "narrow", None),
            P(None, "narrow"),
        ),
        check_vma=False,
    )
```

```python
import math

import jax
import jax.numpy as jnp
import numpy as np
from jax import lax
from jax.experimental import pallas as pl
from jax.experimental.pallas import tpu as pltpu
from jax.sharding import PartitionSpec as P

D = 512
FF = 2048
BS = 64
MODES = 32
GRID = 64
LAYERS = 2

NZ = 4
CH = D // NZ
CELLS = D
ROWS = 8
LINE = NZ * CELLS
SPAN = 2 * ROWS
NMODE = MODES * MODES
HALF = NMODE // 2
SLICE = D // 8
QUARTER = D // 4
HID = D // 2
VROWS = 32
PARAMS = 32

eps = 1e-05
shrink = 0.1
f32 = jnp.float32
bf16 = jnp.bfloat16

NN = (((1,), (0,)), ((), ()))
NT = (((1,), (1,)), ((), ()))
TN = (((0,), (0,)), ((), ()))


MICROS = {
    "stats": 3, "first": 3, "second": 4, "mix": 4, "mix_back": 4.5, "return": 3, "last": 4,
    "close": 3, "cells_one": 9, "cells_two": 11, "cells_three": 8, "weights_one": 7,
    "weights_zero": 7, "plane_sum": 3, "plane_sum_zero": 3, "output": 3, "weights_out_one": 3,
    "weights_out_zero": 3, "fan": 3,
}


def width_tables():
    kw = np.arange(MODES)[:, None] * np.arange(GRID)[None, :] % GRID
    angle = kw * (2.0 * math.pi / GRID)
    parts = np.stack([np.cos(angle), -np.sin(angle)], axis=1) / GRID
    full = np.einsum("kpw,hg->khpgw", parts, np.eye(ROWS)).reshape(D, D)
    doubled = full.reshape(MODES, -1) * np.where(np.arange(MODES) == 0, 1.0, 2.0)[:, None]
    doubled = doubled.reshape(D, D)
    return [np.ascontiguousarray(t).astype(bf16) for t in (full, doubled, full.T, doubled.T)]


def height_tables():
    along = np.arange(MODES)
    freq = np.where(along < MODES // 2, along, along - MODES + GRID)
    phase = np.arange(GRID)[:, None] * freq[None, :] % GRID
    angle = phase * (2.0 * math.pi / GRID)
    cosine, sine = np.cos(angle), np.sin(angle)
    from_real = np.stack([cosine, -sine], axis=1)
    from_imag = np.stack([sine, cosine], axis=1)
    table = np.stack([from_real, from_imag], axis=1)
    table = table.transpose(2, 3, 0, 1).reshape(2 * MODES, 2, NZ, SPAN)
    ahead, back = [], []
    for core in range(2):
        for z in range(NZ):
            turned = table[:, [core, 1 - core]][:, :, [z ^ m for m in range(NZ)]]
            ahead.append(turned.reshape(2 * MODES, 2 * GRID))
            back.append(turned[:, 0].reshape(2 * MODES, GRID).T)
    return np.stack(ahead).astype(bf16), np.ascontiguousarray(np.stack(back)).astype(bf16)


def sds(shape, dtype):
    return pltpu.VMEM(shape, dtype)


def far(shape, dtype):
    return pltpu.HBM(shape, dtype)


def auto(shape, dtype):
    return jax.ShapeDtypeStruct(shape, dtype)


class Copies:
    def __init__(self, sems):
        self.sems, self.used, self.left = sems, 0, []

    def start(self, source, target):
        copy = pltpu.make_async_copy(source, target, self.sems.at[self.used])
        self.used += 1
        copy.start()
        return copy

    def get(self, *pairs):
        return [self.start(source, target) for source, target in pairs]

    def put(self, source, target):
        self.left.append(self.start(source, target))

    def finish(self):
        for copy in self.left:
            copy.wait()


def wait(copies):
    for copy in copies:
        copy.wait()


class Arrived:
    def __init__(self, value):
        self.value = value


def launch(body, name, ids, near, distant, outs, scratch, vmem, aliases=None):
    hbm, local = pl.BlockSpec(memory_space=pltpu.HBM), pl.BlockSpec(memory_space=pltpu.VMEM)
    count = 64

    def whole(ids_ref, *refs):
        copies = Copies(refs[-1])
        body(ids_ref, copies, *refs[:-1])
        copies.finish()

    settled = []
    for value in distant:
        if isinstance(value, Arrived):
            settled.append(value.value)
        else:
            settled.append(pltpu.with_memory_space_constraint(value, pltpu.HBM))
    return pl.pallas_call(
        whole,
        name=name,
        out_shape=list(outs),
        in_specs=[pl.BlockSpec(memory_space=pltpu.SMEM)]
        + [local] * len(near)
        + [pl.BlockSpec(memory_space=pl.ANY) if isinstance(v, Arrived) else hbm for v in distant],
        out_specs=[
            hbm if getattr(out, "memory_space", None) == pltpu.HBM else local for out in outs
        ],
        scratch_shapes=list(scratch) + [pltpu.SemaphoreType.DMA((count,))],
        input_output_aliases=aliases or {},
        compiler_params=pltpu.CompilerParams(vmem_limit_bytes=vmem * 2**20),
        cost_estimate=pl.CostEstimate(
            flops=int(MICROS[name] * 1.1e9), bytes_accessed=2**16, transcendentals=0
        ),
    )(ids, *near, *settled)


def vm(shape, dtype):
    return pltpu.VMEM(shape, dtype)


def dot(a, b, dims=NN):
    return lax.dot_general(a, b, dims, preferred_element_type=f32)


def at(offset, size):
    return pl.ds(pl.multiple_of(offset, size), size)


def gelu_parts(v):
    cdf = 0.5 + 0.5 * lax.erf(v * (2.0**-0.5))
    slope = cdf + v * (jnp.exp(-0.5 * v * v) * ((2.0 * math.pi) ** -0.5))
    return v * cdf, slope


def diagonal(size):
    first = lax.broadcasted_iota(jnp.int32, (size, size), 0)
    return first == lax.broadcasted_iota(jnp.int32, (size, size), 1)


def column(row):
    wide = jnp.broadcast_to(row.astype(f32), (CH, CH))
    return jnp.sum(jnp.where(diagonal(CH), wide, 0.0), axis=1, keepdims=True)


def norm_rows(v, gain, shift):
    mean = jnp.mean(v, axis=1, keepdims=True)
    center = v - mean
    scale = lax.rsqrt(jnp.mean(center * center, axis=1, keepdims=True) + eps)
    unit = center * scale
    return unit * gain + shift, unit, scale


def norm_rows_back(dy, unit, scale, gain):
    dx = dy * gain
    mean = jnp.mean(dx, axis=1, keepdims=True)
    along = jnp.mean(dx * unit, axis=1, keepdims=True)
    back = scale * (dx - mean - unit * along)
    return back, jnp.sum(dy * unit, axis=0, keepdims=True), jnp.sum(dy, axis=0, keepdims=True)


def stats_body(
    ids, io, field, noise, norm_gain, norm_bias, down_bias, up_bias, up, down,
    sums, slices, a, b, gains, shifts, downs, ups, params, rows_vm,
):
    rows = at(ids[2] * SLICE, SLICE)
    first = io.get(
        (up.at[0, rows], rows_vm.at[0:SLICE]), (down.at[0, rows], rows_vm.at[SLICE : 2 * SLICE])
    )
    small = io.get((norm_gain, gains), (norm_bias, shifts), (down_bias, downs), (up_bias, ups))
    loads = io.get((field, a), (noise, b))
    wait(first)
    for n in range(NZ):
        io.put(rows_vm, slices.at[n, 0 : 2 * SLICE])
    wait(small)
    lines = []
    for source in (gains, shifts):
        lines += [source[l, j : j + 1, :] for l in range(LAYERS) for j in range(2)]
    lines += [downs[l : l + 1, :] for l in range(LAYERS)]
    for l in range(LAYERS):
        lines += [ups[l : l + 1, q * CH : (q + 1) * CH] for q in range(NZ)]
    lines = [line.astype(f32) for line in lines]
    lines.append(jnp.zeros((PARAMS - len(lines), CH), f32))
    params[...] = jnp.zeros((PARAMS, D), bf16)
    params[:, 0:CH] = jnp.concatenate(lines, axis=0).astype(bf16)
    for n in range(NZ):
        io.put(params, slices.at[n, 2 * SLICE : 2 * SLICE + PARAMS])
    wait(loads)
    v = a[...].astype(f32) + b[...].astype(f32)
    total = jnp.sum(v, axis=0, keepdims=True)
    center = v - total * (1.0 / CH)
    sums[0:1, :] = total
    sums[1:2, :] = jnp.sum(center * center, axis=0, keepdims=True)


def first_body(
    ids, io, s0, s1, s2, s3, field, noise, norm_gain, norm_bias, table_in, up, down, turned,
    out, ms_out, l0, l1, l2, l3, slices, a, b, gains, shifts, table, ms, lines, held,
):
    loads = io.get((field, a), (noise, b), (norm_gain, gains), (norm_bias, shifts))
    late = io.get((table_in, table))
    z, rows = ids[1], at(ids[2] * SLICE, SLICE)
    other = [
        io.start(turned.at[:, at((z ^ m) * CELLS, CELLS)], lines.at[m]) for m in range(NZ)
    ]
    other += io.get((up.at[1, rows], held.at[0:SLICE]), (down.at[1, rows], held.at[SLICE:]))
    sums = (s0, s1, s2, s3)
    mean = (s0[0:1, :] + s1[0:1, :] + s2[0:1, :] + s3[0:1, :]) * (1.0 / D)
    second = jnp.zeros_like(mean)
    for s in sums:
        apart = s[0:1, :] * (1.0 / CH) - mean
        second = second + s[1:2, :] + CH * (apart * apart)
    scale = lax.rsqrt(second * (1.0 / D) + eps)
    ms[0:1, :] = mean
    ms[1:2, :] = scale
    io.put(ms, ms_out)
    wait(loads)
    v = a[...].astype(f32) + b[...].astype(f32)
    gain, shift = column(gains[0, 0:1, :]), column(shifts[0, 0:1, :])
    normed = ((v - mean) * scale * gain + shift).astype(bf16)
    wait(other)
    l0[...] = lines[0]
    for m, l in ((1, l1), (2, l2), (3, l3)):
        io.put(lines.at[m], l)
    for n in range(NZ):
        io.put(held, slices.at[n])
    wait(late)
    for s in range(NZ):
        part = normed[:, s * CELLS : (s + 1) * CELLS]
        out[s] = dot(table[...], part, NT).astype(bf16)


def second_body(
    ids, io, modes, ms_in, field, noise, norm_gain, norm_bias, table_in,
    p0, p1, p2, p3, a, b, gains, shifts, ms, table, held,
):
    z = ids[1]
    loads = io.get((field, a), (noise, b), (norm_gain, gains), (norm_bias, shifts), (ms_in, ms))
    more = io.get((table_in, table))
    wait(loads)
    v = a[...].astype(f32) + b[...].astype(f32)
    gain, shift = column(gains[0, 0:1, :]), column(shifts[0, 0:1, :])
    both = v + (v - ms[0:1, :]) * ms[1:2, :] * gain + shift
    wait(more)
    for s in range(NZ):
        held[s] = (
            dot(table[...], modes[s]) + both[:, s * CELLS : (s + 1) * CELLS].T
        ).astype(bf16)
    for m, out in enumerate((p0, p1, p2, p3)):
        out[...] = held[z ^ m]


def return_body(
    ids, io, g0, g1, g2, g3, table_in, out, cells, small_out, table, small
):
    z = ids[1]
    loads = io.get((table_in, table))
    rows = jnp.zeros((VROWS, CH), f32)
    for m, g in enumerate((g0, g1, g2, g3)):
        cells[z ^ m] = g[0:CELLS, :]
        high, low = g[CELLS : CELLS + VROWS, :], g[CELLS + VROWS : CELLS + 2 * VROWS, :]
        rows = rows + (high.astype(f32) + low.astype(f32))
    small[...] = rows
    io.put(small, small_out)
    wait(loads)
    for s in range(NZ):
        out[s] = dot(table[...], cells[s]).astype(bf16)


def last_body(
    ids, io, modes, cells, ms_in, small, mix_one, mix_zero, field, noise, norm_gain, table_in,
    base, sums, tail, a, b, gains, ms, table,
):
    loads = io.get((table_in, table), (ms_in, ms))
    loads += io.get((field, a), (noise, b), (norm_gain, gains))
    size = 2 * CH + 8
    copies = io.get(
        (small, tail.at[0:VROWS]),
        (mix_one, tail.at[VROWS : VROWS + size]),
        (mix_zero, tail.at[VROWS + size : VROWS + 2 * size]),
    )
    wait(loads)
    col = column(gains[0, 0:1, :])
    gain_sum = jnp.zeros((CH, 1), f32)
    shift_sum = jnp.zeros((CH, 1), f32)
    for s in range(NZ):
        here = slice(s * CELLS, (s + 1) * CELLS)
        up = cells[s].astype(f32)
        dy = (dot(table[...], modes[s]) + up).T
        up = up.T
        v = a[:, here].astype(f32) + b[:, here].astype(f32)
        unit = (v - ms[0:1, here]) * ms[1:2, here]
        dx = dy * col
        sums[0:1, here] = jnp.sum(dx, axis=0, keepdims=True)
        sums[1:2, here] = jnp.sum(dx * unit, axis=0, keepdims=True)
        base[:, here] = up + ms[1:2, here] * dx
        gain_sum = gain_sum + jnp.sum(dy * unit, axis=1, keepdims=True)
        shift_sum = shift_sum + jnp.sum(dy, axis=1, keepdims=True)
    wait(copies)
    on = diagonal(CH)
    first = VROWS + 2 * size
    tail[first : first + 8, :] = jnp.zeros((8, CH), f32)
    tail[first : first + 1, :] = jnp.sum(jnp.where(on, gain_sum, 0.0), axis=0, keepdims=True)
    tail[first + 1 : first + 2, :] = jnp.sum(
        jnp.where(on, shift_sum, 0.0), axis=0, keepdims=True
    )


def close_body(ids, io, base, s0, s1, ms_in, field, noise, out, a, b, ms, result):
    loads = io.get((field, a), (noise, b), (ms_in, ms))
    mean = (s0[0:1, :] + s1[0:1, :]) * (1.0 / D)
    along = (s0[1:2, :] + s1[1:2, :]) * (1.0 / D)
    wait(loads)
    for s in range(NZ):
        here = slice(s * CELLS, (s + 1) * CELLS)
        v = a[:, here].astype(f32) + b[:, here].astype(f32)
        unit = (v - ms[0:1, here]) * ms[1:2, here]
        result[:, here] = base[:, here] - ms[1:2, here] * (mean[:, here] + unit * along[:, here])
        io.put(result.at[:, here], out.at[:, here])


def groups(arrays):
    return [arrays[0].at[s] for s in range(NZ)] if len(arrays) == 1 else list(arrays)


def mixing_matrix(real, imag):
    first = lax.broadcasted_iota(jnp.int32, (CH, CH), 0) // BS
    on = first == lax.broadcasted_iota(jnp.int32, (CH, CH), 1) // BS

    def spread(part):
        part = part.astype(f32).T
        return jnp.where(on, jnp.concatenate([part, part], axis=1), 0.0)

    real, imag = spread(real), spread(imag)
    top = jnp.concatenate([real, imag], axis=1)
    bottom = jnp.concatenate([-imag, real], axis=1)
    return jnp.concatenate([top, bottom], axis=0).astype(bf16)


def to_spectrum(table, own, other, out):
    sources = groups([own]) + groups([other])
    for k in range(MODES):
        rows = slice(SPAN * k, SPAN * (k + 1))
        block = jnp.concatenate([source[rows, :] for source in sources], axis=0)
        modes = dot(table, block).astype(out.dtype)
        out[MODES * k : MODES * (k + 1), :CH] = modes[:MODES]
        out[MODES * k : MODES * (k + 1), CH:] = modes[MODES:]


def from_spectrum(table, spectrum, outs):
    targets = groups(outs)
    for k in range(MODES):
        rows = slice(SPAN * k, SPAN * (k + 1))
        here = slice(MODES * k, MODES * (k + 1))
        block = jnp.concatenate([spectrum[here, :CH], spectrum[here, CH:]], axis=0)
        cells = dot(table, block).astype(bf16)
        for m, target in enumerate(targets):
            target[rows, :] = cells[SPAN * m : SPAN * (m + 1)]


def load_tables(io, ids, cells, tables, rooms):
    which = ids[0] * NZ + ids[1] if cells else ids[0] * NZ
    ahead, back, *weights = tables
    return io.get((ahead.at[which], rooms[0]), (back.at[which], rooms[1])) + io.get(
        *zip(weights, rooms[2:])
    )


def mix_body(layer, cells, ids, io, own, other, *refs):
    refs, take = list(refs), lambda n: [refs.pop(0) for _ in range(n)]
    tables, outs, saved = take(4), take(NZ if cells else 1), take(4)
    spectrum, active, slope, square, *rooms = refs
    table, back, weight, bias = rooms
    wait(load_tables(io, ids, cells, tables, rooms))
    to_spectrum(table[...], own, other, spectrum)
    io.put(spectrum, saved[0])

    def product(j, values):
        matrix = mixing_matrix(weight[layer, j, 0], weight[layer, j, 1])
        shift = jnp.concatenate([bias[layer, j, 0:1, :], bias[layer, j, 1:2, :]], axis=1)
        return dot(values, matrix) + shift.astype(f32)

    value, inner = gelu_parts(product(0, spectrum[...]))
    active[...] = value.astype(bf16)
    slope[...] = inner.astype(slope.dtype)
    io.put(active, saved[1])
    io.put(slope, saved[2])
    two = product(1, active[...])
    bend = jnp.tanh(two * (1.0 / shrink))
    square[...] = (bend * bend).astype(square.dtype)
    io.put(square, saved[3])
    from_spectrum(back[...], (two - shrink * bend).astype(bf16), outs)


def mix_back_body(layer, cells, ids, io, own, other, *refs):
    refs, take = list(refs), lambda n: [refs.pop(0) for _ in range(n)]
    saved, tables, outs, (sums_out,) = take(4), take(3), take(NZ if cells else 1), take(1)
    spectrum, active, slope, square, low_one, low_two, sums, *rooms = refs
    table, back, weight = rooms
    share = at(ids[0] * HALF, HALF)
    loads = load_tables(io, ids, cells, tables, rooms)
    late = io.get((saved[3], square), (saved[2], slope))
    later = io.get((saved[0].at[share], spectrum), (saved[1].at[share], active))
    wait(loads)
    to_spectrum(table[...], own, other, low_two)
    wait(late)

    def product(j, values):
        return dot(values, mixing_matrix(weight[layer, j, 0], weight[layer, j, 1]), NT)

    low_two[...] = (low_two[...].astype(f32) * square[...].astype(f32)).astype(bf16)
    low_one[...] = (product(1, low_two[...]) * slope[...].astype(f32)).astype(bf16)
    from_spectrum(back[...], product(0, low_one[...]).astype(bf16), outs)
    wait(later)
    lane = lax.broadcasted_iota(jnp.int32, (BS, CH), 1)
    sums[2 * CH :, :] = jnp.zeros((8, CH), f32)
    for j, (left, right) in enumerate(((spectrum, low_one), (active, low_two))):
        outer = dot(left[...], right[share, :], TN)
        real = outer[:CH, :CH] + outer[CH:, CH:]
        imag = outer[:CH, CH:] - outer[CH:, :CH]
        parts = jnp.concatenate(
            [
                jnp.where(lane < BS, real[:BS], pltpu.roll(imag[:BS], BS, 1)),
                jnp.where(lane < BS, pltpu.roll(real[BS:], BS, 1), imag[BS:]),
            ],
            axis=0,
        )
        sums[j * CH : (j + 1) * CH, :] = parts.T
        total = jnp.sum(right[share, :].astype(f32), axis=0, keepdims=True)
        first = 2 * CH + 2 * j
        sums[first : first + 1, :] = total[:, :CH]
        sums[first + 1 : first + 2, :] = total[:, CH:]
    io.put(sums, sums_out)


def load_weights(io, layer, ids, up, down, near, distant, store):
    place = ids[2]
    copies = io.get((up.at[layer], store.at[0, 0]), (down.at[layer], store.at[0, 1]))
    for core, array in enumerate((near, distant)):
        for side in range(2):
            for index, e in enumerate((0, 2, 4, 6) if side == 0 else (0, 4, 2, 6)):
                rows = at((place ^ e ^ core) * SLICE, SLICE)
                part = array.at[side, index]
                copies.append(io.start(part, store.at[1:NZ, side, rows]))
    return copies


def load_weights_one(io, ids, up, down, near, distant, store):
    copies = io.get((up.at[1], store.at[0, 0]), (down.at[1], store.at[0, 1]))
    for array, core in ((near, ids[0]), (distant, 1 - ids[0])):
        for chip in range(4):
            rows = at((2 * chip + core) * SLICE, SLICE)
            for side in range(2):
                part = array.at[chip, :, side * SLICE : (side + 1) * SLICE]
                copies.append(io.start(part, store.at[1:NZ, side, rows]))
    return copies


def fan_body(ids, io, arrived, out, held):
    wait([io.start(arrived.at[ids[1] ^ m], held.at[m - 1]) for m in range(1, NZ)])
    for chip in range(4):
        io.put(held, out.at[chip])


def gather_lanes(z, pieces, wide):
    for m, piece in enumerate(pieces):
        wide[:, at((z ^ m) * CH, CH)] = piece[...]


def scatter_lanes(z, wide, pieces):
    for m, piece in enumerate(pieces):
        piece[0:CELLS, :] = wide[:, at((z ^ m) * CH, CH)].astype(piece.dtype)


def store_send(io, core, chunk, place, keep, send):
    io.put(chunk.at[:, at(core * HID, HID)], keep)
    io.put(chunk.at[:, at((1 - core) * HID, HID)], send.at[place * CELLS : (place + 1) * CELLS])


def store_cells(io, values, place, send):
    for half in range(2):
        rows = slice((place + half) * CELLS, (place + half + 1) * CELLS)
        io.put(values.at[:, half * HID : (half + 1) * HID], send.at[rows])


def cells_one_body(
    ids, io, p0, p1, p2, p3, l0, l1, l2, l3, arrived, up, down, near, distant, table_in,
    a0, a1, a2, a3, vectors_out, up_shift_out, base_out, unit_one_out, scale_one_out,
    unit_two_out, scale_two_out, slope_out, low_out, keep, send, turned_out,
    store, wide, params, table, low, total, hidden, vectors, up_shift, base, unit_one, unit_two,
    scales, slope, turned,
):
    core, z = ids[0], ids[1]
    loads = [
        io.start(arrived.at[z ^ m, 2 * SLICE : 2 * SLICE + PARAMS, 0:CH], params.at[m])
        for m in range(NZ)
    ]
    weights = load_weights(io, 0, ids, up, down, near, distant, store)
    late = io.get((table_in, table))
    gather_lanes(z, (p0, p1, p2, p3), wide)
    wait(loads)
    for m in range(NZ):
        rows = params[m].astype(f32)
        vectors[0:10, at((z ^ m) * CH, CH)] = rows[0:10]
        for l in range(LAYERS):
            top = 10 + NZ * l
            shift = jnp.concatenate([rows[top + q : top + q + 1] for q in range(NZ)], axis=1)
            up_shift[l, m : m + 1, :] = shift
    io.put(vectors, vectors_out)
    io.put(up_shift, up_shift_out)
    state = wide[...].astype(f32)
    normed, unit, scale = norm_rows(state, vectors[1:2, :], vectors[5:6, :])
    low[...] = normed.astype(bf16)
    unit_two[...] = unit.astype(bf16)
    scales[0] = jnp.broadcast_to(scale, (CELLS, CH))
    total[...] = state + vectors[8:9, :]
    io.put(unit_two, unit_two_out)
    io.put(scales.at[0], scale_two_out)
    io.put(low, low_out)
    store_cells(io, low, NZ, send)
    for m, piece in enumerate((l0, l1, l2, l3)):
        turned[:, at((z ^ m) * CH, CH)] = piece[...].T
    io.put(turned, turned_out)
    wait(weights)
    for j in range(NZ):
        before = dot(low[...], store[j, 0]) + up_shift[0, j : j + 1, :]
        value, inner = gelu_parts(before)
        hidden[j] = value.astype(bf16)
        slope[j] = inner.astype(bf16)
        io.put(slope.at[j], slope_out.at[j])
        store_send(io, core, hidden.at[j], j, keep.at[j], send)
        total[...] += dot(hidden[j], store[j, 1])
    state = total[...]
    normed, unit, scale = norm_rows(state, vectors[2:3, :], vectors[6:7, :])
    base[...] = state + normed
    unit_one[...] = unit.astype(bf16)
    scales[1] = jnp.broadcast_to(scale, (CELLS, CH))
    io.put(base, base_out)
    io.put(unit_one, unit_one_out)
    io.put(scales.at[1], scale_one_out)
    wait(late)
    total[...] = dot(table[...], normed.astype(bf16))
    scatter_lanes(z, total, (a0, a1, a2, a3))


def fill_small(rows, ups, z, small):
    for m in range(NZ):
        small[m, 0:8, :] = rows[0:8, at((z ^ m) * CH, CH)]
        line = ups[m : m + 1, :]
        for q in range(NZ):
            small[m, 8 + q : 9 + q, :] = line[:, q * CH : (q + 1) * CH]
        small[m, 12:16, :] = jnp.zeros((4, CH), f32)


def cells_two_body(
    ids, io, arrived, base_in, vectors_in, up_shift_in,
    turned_in, up, down, near, distant, back_in, table_in,
    a0, a1, a2, a3, o0, o1, o2, o3, small_out, grad_out, low_out, hidden_keep,
    before_keep, send,
    store, wide, back_table, table, low, low_grad, unit_two, total, other, hidden,
    before_grad, ups, base, vectors, up_shift, small, grad, result,
):
    core, z = ids[0], ids[1]
    loads = io.get((back_in, back_table), (base_in, base), (vectors_in, vectors))
    loads += io.get((up_shift_in, up_shift))
    loads += io.get((turned_in, low_grad))
    weights = load_weights_one(io, ids, up, down, near, distant, store)
    last = io.get((table_in, table))
    gather_lanes(z, [arrived.at[m] for m in range(NZ)], wide)
    wait(loads)
    state = base[...] + dot(back_table[...], wide[...])
    normed, unit, scale = norm_rows(state, vectors[3:4, :], vectors[7:8, :])
    low[...] = normed.astype(bf16)
    io.put(low, low_out)
    store_cells(io, low, 2 * NZ, send)
    unit_two[...] = unit
    total[...] = state + vectors[9:10, :]
    other[...] = jnp.zeros_like(other)
    store_cells(io, low_grad, 2 * NZ + 2, send)
    wait(weights)
    for j in range(NZ):
        before = dot(low[...], store[j, 0]) + up_shift[1, j : j + 1, :]
        value, inner = gelu_parts(before)
        hidden[j] = value.astype(bf16)
        store_send(io, core, hidden.at[j], j, hidden_keep.at[j], send)
        total[...] += dot(hidden[j], store[j, 1])
        turn = dot(low_grad[...], store[j, 1], NT) * inner
        before_grad[j] = turn.astype(bf16)
        store_send(io, core, before_grad.at[j], NZ + j, before_keep.at[j], send)
        ups[j : j + 1, :] = jnp.sum(before_grad[j].astype(f32), axis=0, keepdims=True)
        other[...] += dot(before_grad[j], store[j, 0], NT)
    gradient = low_grad[...].astype(f32)
    change, gain_row, shift_row = norm_rows_back(other[...], unit_two[...], scale, vectors[3:4, :])
    grad[...] = gradient + change
    io.put(grad, grad_out)
    result[...] = total[...].astype(bf16)
    for m, out in enumerate((o0, o1, o2, o3)):
        io.put(result.at[:, at((z ^ m) * CH, CH)], out)
    wait(last)
    total[...] = dot(table[...], grad[...].astype(bf16))
    scatter_lanes(z, total, (a0, a1, a2, a3))
    other[0:8, :] = jnp.zeros((8, D), f32)
    other[0:1, :] = gain_row
    other[1:2, :] = shift_row
    other[2:3, :] = jnp.sum(gradient, axis=0, keepdims=True)
    fill_small(other, ups, z, small)
    io.put(small, small_out)


def cells_three_body(
    ids, io, b0, b1, b2, b3, grad_in, unit_one_in, scale_one_in, unit_two_in, scale_two_in,
    vectors_in, small_in, slope_in, up, down, near, distant, back_in,
    g0, g1, g2, g3, low_grad_out, keep, send,
    store, wide, back_table, low_grad, total, other, before_grad, ups, small, grad, unit_one,
    unit_two, scales, vectors, small_one, slope,
):
    core, z = ids[0], ids[1]
    loads = io.get((back_in, back_table), (grad_in, grad), (vectors_in, vectors))
    loads += io.get((unit_one_in, unit_one), (scale_one_in, scales.at[0]))
    weights = load_weights(io, 0, ids, up, down, near, distant, store)
    weights += io.get((slope_in, slope))
    later = io.get((unit_two_in, unit_two), (scale_two_in, scales.at[1]), (small_in, small_one))
    gather_lanes(z, (b0, b1, b2, b3), wide)
    wait(loads)
    dy = grad[...] + dot(back_table[...], wide[...])
    change, gain_one, shift_one = norm_rows_back(
        dy, unit_one[...].astype(f32), scales[0, :, 0:1], vectors[2:3, :]
    )
    total[...] = grad[...] + change
    low_grad[...] = total[...].astype(bf16)
    io.put(low_grad, low_grad_out)
    store_cells(io, low_grad, NZ, send)
    other[...] = jnp.zeros_like(other)
    wait(weights)
    for j in range(NZ):
        turn = dot(low_grad[...], store[j, 1], NT) * slope[j].astype(f32)
        before_grad[j] = turn.astype(bf16)
        store_send(io, core, before_grad.at[j], j, keep.at[j], send)
        ups[j : j + 1, :] = jnp.sum(before_grad[j].astype(f32), axis=0, keepdims=True)
        other[...] += dot(before_grad[j], store[j, 0], NT)
    wait(later)
    change, gain_two, shift_two = norm_rows_back(
        other[...], unit_two[...].astype(f32), scales[1, :, 0:1], vectors[1:2, :]
    )
    total[...] += change
    pieces = (g0, g1, g2, g3)
    scatter_lanes(z, total, pieces)
    other[0:8, :] = jnp.zeros((8, D), f32)
    other[0:1, :] = gain_two
    other[1:2, :] = shift_two
    other[2:3, :] = jnp.sum(low_grad[...].astype(f32), axis=0, keepdims=True)
    other[3:4, :] = gain_one
    other[4:5, :] = shift_one
    fill_small(other, ups, z, small)
    for m, piece in enumerate(pieces):
        rows = jnp.concatenate([small_one[m], small[m]], axis=0)
        high = rows.astype(bf16)
        piece[CELLS : CELLS + VROWS, :] = high
        piece[CELLS + VROWS : CELLS + 2 * VROWS, :] = (rows - high.astype(f32)).astype(bf16)


def weights_body(
    places, ids, io, low_own, grad_own, hidden_own, before_own, *refs
):
    lows, left, right, product = refs[-4:]
    count = 1 + max(array for array, _ in places.values())
    sent, parts = refs[:count], refs[count:-4]

    def other(name, chunk):
        array, first = places[name]
        return sent[array].at[(first + chunk) * CELLS : (first + chunk + 1) * CELLS]

    loads = io.get((low_own, lows.at[0, 0]), (grad_own, lows.at[1, 0]))
    for side, name in enumerate(("low", "grad")):
        for half in range(2):
            target = lows.at[side, 1, :, half * HID : (half + 1) * HID]
            loads.append(io.start(other(name, half), target))
    later = []
    for j in range(NZ):
        step = []
        for side, (value, name) in enumerate(((before_own, "before"), (hidden_own, "hidden"))):
            step.append(io.start(value.at[j], right.at[j, side, 0:CELLS]))
            step.append(io.start(other(name, j), right.at[j, side, CELLS : 2 * CELLS]))
        later.append(step)
    wait(loads)
    for side in range(2):
        for half in range(2):
            left[side, :, half * CELLS : (half + 1) * CELLS] = lows[side, half].T
    for j in range(NZ):
        wait(later[j])
        for side in range(2):
            product[j, side] = dot(left[side], right[j, side]).astype(bf16)
        for q in range(4):
            if len(parts) == 1:
                rows, part = slice(q * QUARTER, (q + 1) * QUARTER), parts[0].at[q]
            else:
                rows, part = at(((ids[2] // 2) ^ q) * QUARTER, QUARTER), parts[q]
            io.put(product.at[j, :, rows], part.at[j])


def plane_sum_body(ids, io, k1, k2, k3, k0, *refs):
    outs, own = refs[:-1], refs[-1]
    wait(io.get((k0, own)))
    for m in range(NZ):
        part = own[m].astype(f32) + k1[m].astype(f32)
        part = part + (k2[m].astype(f32) + k3[m].astype(f32))
        outs[m][...] = part.astype(outs[m].dtype)


def all_sum_body(ids, io, parts, out, held):
    loads = [io.start(parts.at[:, m], held.at[:, m]) for m in range(NZ)]
    for m in range(NZ):
        loads[m].wait()
        part = held[0, m].astype(f32) + held[1, m].astype(f32)
        part = part + (held[2, m].astype(f32) + held[3, m].astype(f32))
        out[ids[1] ^ m] = part.astype(bf16)


def output_body(ids, io, o0, o1, o2, o3, out, held, wide):
    z = ids[1]
    loads = [io.start(o, held.at[m]) for m, o in enumerate((o0, o1, o2, o3))]
    for m in range(NZ):
        loads[m].wait()
        wide[m] = held[m].T
        io.put(wide.at[m], out.at[:, at((z ^ m) * CELLS, CELLS)])


def weights_out_body(layer, ids, io, *refs):
    core, chip = ids[0], ids[2] // 2
    pieces = refs[:8]
    up, down, both, result = refs[-4:]
    for e, piece in enumerate(pieces):
        rows, lanes = at((chip ^ (e // 2)) * QUARTER, QUARTER), at((core ^ (e % 2)) * HID, HID)
        both[:, rows, lanes] = piece[...]
    result[0] = both[0].astype(f32)
    io.put(result.at[0], up.at[layer])
    result[1] = both[1].T.astype(f32)
    io.put(result.at[1], down.at[layer])


def swap(value, axis, mask):
    pairs = [(source, source ^ mask) for source in range(lax.axis_size(axis))]
    return lax.ppermute(value, axis, pairs)


def after(values, *done):
    values = list(values)
    return list(lax.optimization_barrier((*values, *done))[: len(values)])


def exchange(pieces):
    return [pieces[0]] + [swap(pieces[m], "narrow", m) for m in range(1, NZ)]


def spread(value):
    return lax.all_to_all(value, "narrow", 0, 0)


def chips():
    return [
        [8 * g + 2 * chip + core for chip in range(4)]
        for g in range(lax.axis_size("wide") // 8)
        for core in range(2)
    ]


def wide_total(value, done):
    mask = 1
    while mask < lax.axis_size("wide"):
        if mask == 2:
            value = after([value], done)[0]
        value = value + swap(value, "wide", mask)
        mask *= 2
    return value


def shards(
    field,
    noise,
    norm_gain,
    norm_bias,
    mix_weight,
    mix_bias,
    up_weight,
    up_bias,
    down_weight,
    down_bias,
    out_grad,
):
    wide, z = lax.axis_index("wide"), lax.axis_index("narrow")
    core, place = wide % 2, wide % 8
    ids = jnp.stack([core, z, place]).astype(jnp.int32)
    table, doubled, table_back, doubled_back = width_tables()
    height, height_back = height_tables()

    weight_turned = jnp.swapaxes(mix_weight, 3, 4)

    line_low, pair = vm((CH, LINE), bf16), vm((2, LINE), f32)
    params_two = vm((LAYERS, 2, CH), bf16)
    square_low, square_f32 = vm((D, D), bf16), vm((D, D), f32)
    chunks = vm((NZ, CELLS, D), bf16)
    store = vm((NZ, 2, D, D), bf16)
    up_rows, vector_rows = vm((NZ, D), f32), vm((10, D), f32)
    shift_rows = vm((LAYERS, NZ, D), f32)
    small_vm, two_scales = vm((NZ, VROWS // 2, CH), f32), vm((2, CELLS, CH), f32)
    piece_vm, group_vm = vm((CELLS, CH), bf16), vm((NZ, D, CH), bf16)
    modes_vm, share_vm = vm((NMODE, 2 * CH), bf16), vm((HALF, 2 * CH), bf16)
    mix_sums = (2 * CH + 8, CH)
    table_vms = [vm((2 * MODES, 2 * GRID), bf16), vm((GRID, 2 * MODES), bf16)]
    table_vms.append(vm((LAYERS, 2, 2, BS, CH), bf16))

    own_piece, piece, far_piece = [kind((CELLS, CH), bf16) for kind in (auto, sds, far)]
    group = auto((NZ, D, CH), bf16)
    far_modes = far((NMODE, 2 * CH), bf16)
    far_low, far_f32, far_thin = far((CELLS, D), bf16), far((CELLS, D), f32), far((CELLS, CH), f32)
    halves, whole = far((NZ, CELLS, HID), bf16), far((NZ, CELLS, D), bf16)
    send = far(((NZ + 2) * CELLS, HID), bf16)
    parts = far((NZ, 2, QUARTER, HID), bf16)
    line_sums = auto((2, LINE), f32)
    far_small = far((NZ, VROWS // 2, CH), f32)

    def mix(layer, cells, own, other):
        outs = launch(
            lambda *refs: mix_body(layer, cells, *refs),
            "mix",
            ids,
            [own, other],
            [height, height_back, weight_turned, mix_bias],
            ([own_piece] + [piece] * 3 if cells else [group]) + [far_modes] * 4,
            [modes_vm] * 4 + table_vms + [vm((LAYERS, 2, 2, CH), bf16)],
            16,
        )
        return outs[:-4], outs[-4:]

    def mix_back(layer, cells, own, other, saved):
        outs = launch(
            lambda *refs: mix_back_body(layer, cells, *refs),
            "mix_back",
            ids,
            [own, other],
            [*saved, height, height_back, weight_turned],
            ([own_piece] + [piece] * 3 if cells else [group]) + [far(mix_sums, f32)],
            [share_vm, share_vm, modes_vm, modes_vm, modes_vm, modes_vm, vm(mix_sums, f32)]
            + table_vms,
            16,
        )
        return outs[:-1], outs[-1]

    def first_step(arrived):
        others = [lax.dynamic_index_in_dim(arrived, z ^ m, 0, False) for m in range(1, NZ)]
        ups = jnp.stack([r[:SLICE] for r in others])
        downs = jnp.stack([r[SLICE : 2 * SLICE] for r in others])
        return ups, downs, swap(ups, "wide", 2), swap(downs, "wide", 4)

    def second_step(ups, downs, ups_near, downs_near):
        ups, downs = jnp.stack([ups, ups_near]), jnp.stack([downs, downs_near])
        return ups, downs, swap(ups, "wide", 4), swap(downs, "wide", 2)

    def third_step(ups, downs, ups_far, downs_far):
        held = jnp.stack(
            [jnp.concatenate([ups, ups_far]), jnp.concatenate([downs, downs_far])]
        )
        return held, swap(held, "wide", 1)

    def fan(arrived):
        sent = launch(
            fan_body, "fan", ids, [], [Arrived(arrived)], [far((4, 3, 2 * SLICE, D), bf16)],
            [vm((3, 2 * SLICE, D), bf16)], 12,
        )[0]
        return sent

    own, mine = launch(
        stats_body,
        "stats",
        ids,
        [],
        [field, noise, norm_gain, norm_bias, down_bias, up_bias, up_weight, down_weight],
        [line_sums, far((NZ, 2 * SLICE + PARAMS, D), bf16)],
        [line_low, line_low, params_two, params_two, vm((LAYERS, CH), bf16)]
        + [vm((LAYERS, D), bf16), vm((PARAMS, D), bf16), vm((2 * SLICE, D), bf16)],
        12,
    )
    first_sums = [own] + [swap(own, "narrow", m) for m in range(1, NZ)]
    zero = spread(after([mine], *first_sums[1:])[0])

    modes, ms, *late, mine_one = launch(
        first_body,
        "first",
        ids,
        first_sums,
        [field, noise, norm_gain, norm_bias, table, up_weight, down_weight, out_grad],
        [group, far((2, LINE), f32)]
        + [auto((CH, CELLS), bf16)]
        + [far((CH, CELLS), bf16)] * 3
        + [far((NZ, 2 * SLICE, D), bf16)],
        [line_low, line_low, params_two, params_two, square_low, pair]
        + [vm((NZ, CH, CELLS), bf16), vm((2 * SLICE, D), bf16)],
        16,
    )
    (modes,), saved_zero = mix(0, False, modes, swap(modes, "wide", 1))
    spread_zero = second_step(*first_step(after([zero], modes)[0]))
    late = exchange([late[0], *after(late[1:], modes)])
    p0, p1, p2, p3 = launch(
        second_body,
        "second",
        ids,
        [modes],
        [ms, field, noise, norm_gain, norm_bias, doubled_back],
        [own_piece] + [piece] * 3,
        [line_low, line_low, params_two, params_two, pair, square_low, group_vm],
        16,
    )
    p1, p2, p3 = after([p1, p2, p3], *late[1:])
    state = exchange([p0, p1, p2, p3])
    ups_zero, downs_zero = after(spread_zero[2:], *state[1:])
    weights_zero = third_step(*spread_zero[:2], ups_zero, downs_zero)

    one = spread(after([mine_one], *state[1:])[0])

    (
        a0, a1, a2, a3, vectors, up_shift, base, unit_one, scale_one, unit_two, scale_two, slope,
        low_zero, hidden_zero, send_zero, grad_one,
    ) = launch(
        cells_one_body,
        "cells_one",
        ids,
        [*state, *late],
        [Arrived(zero), up_weight, down_weight, *map(Arrived, weights_zero), table],
        [own_piece]
        + [piece] * 3
        + [far((10, D), f32), far((LAYERS, NZ, D), f32)]
        + [far_f32, far_low, far_thin, far_low, far_thin, whole]
        + [far_low, halves, send, far_low],
        [store, square_low, vm((NZ, PARAMS, CH), bf16), square_low, square_low, square_f32]
        + [chunks, vector_rows, shift_rows, square_f32, square_low, square_low, two_scales]
        + [chunks, square_low],
        28,
    )

    sent_one = fan(after([one], a0)[0])
    own = jnp.stack(after(exchange([a0, a1, a2, a3]), sent_one))
    near_one = lax.all_to_all(sent_one, "wide", 0, 0, axis_index_groups=chips())
    modes, saved_one = mix(1, True, own, swap(own, "wide", 1))
    ready = modes[0]
    modes = jnp.stack(exchange(modes))
    near_one = after([near_one], modes)[0]
    weights_one = [near_one, swap(near_one, "wide", 1)]
    first_other = swap(after([send_zero], ready)[0], "wide", 1)
    base = after([base], first_other)[0]

    (
        a0, a1, a2, a3, o0, o1, o2, o3, small, grad, low_one, hidden_one, before_one,
        send_one,
    ) = launch(
        cells_two_body,
        "cells_two",
        ids,
        [modes],
        [base, vectors, up_shift, grad_one, up_weight, down_weight]
        + [*map(Arrived, weights_one), doubled_back, doubled],
        [own_piece]
        + [piece] * 3
        + [far_piece] * 4
        + [far_small, far_f32, far_low, halves, halves]
        + [far(((2 * NZ + 4) * CELLS, HID), bf16)],
        [store, square_low, square_low, square_low, square_low, square_low]
        + [square_f32] * 3
        + [chunks, chunks, up_rows, square_f32, vector_rows, shift_rows, small_vm, square_f32]
        + [square_low],
        34,
    )

    def plane_sum(parts, outs):
        return launch(
            plane_sum_body, "plane_sum", ids, parts[1:], parts[:1], outs,
            [vm((NZ, 2, QUARTER, HID), bf16)], 12,
        )

    def finish_weights(result, *done):
        mask = 8
        while mask < lax.axis_size("wide"):
            result = result + swap(result.astype(bf16), "wide", mask).astype(f32)
            mask *= 2
        result = result.astype(bf16)
        pieces = []
        for value in [result] + [swap(result, "wide", q) for q in (2, 4, 6)]:
            pieces += [value, swap(after([value], *done)[0], "wide", 1)]
        return pieces

    def weight_parts(name, places, operands, outs):
        return launch(
            lambda *refs: weights_body(places, *refs),
            name,
            ids,
            [],
            operands,
            outs,
            [vm((2, 2, CELLS, D), bf16), vm((2, D, 2 * CELLS), bf16)]
            + [vm((NZ, 2, 2 * CELLS, HID), bf16), vm((NZ, 2, D, HID), bf16)],
            20,
        )

    own = exchange([a0, a1, a2, a3])
    parts_one = weight_parts(
        "weights_one",
        {"hidden": (0, 0), "before": (0, NZ), "low": (0, 2 * NZ), "grad": (0, 2 * NZ + 2)},
        [low_one, grad_one, hidden_one, before_one, Arrived(swap(send_one, "wide", 1))],
        [parts] * 4,
    )
    own = jnp.stack(after(own, parts_one[0]))
    modes, mix_one = mix_back(1, True, own, swap(own, "wide", 1), saved_one)
    own_part, *other_parts = [parts_one[0], *after(parts_one[1:], modes[0])]
    modes = exchange(modes)
    other_parts[2] = after([other_parts[2]], *modes[1:])[0]
    other_parts = [swap(other_parts[q - 1], "wide", 2 * q) for q in (1, 2, 3)]

    g0, g1, g2, g3, grad_zero, before_zero, last_send = launch(
        cells_three_body,
        "cells_three",
        ids,
        modes,
        [grad, unit_one, scale_one, unit_two, scale_two, vectors, small, slope]
        + [up_weight, down_weight, *map(Arrived, weights_zero), table_back],
        [auto((CELLS + 2 * VROWS, CH), bf16)]
        + [sds((CELLS + 2 * VROWS, CH), bf16)] * 3
        + [far_low, halves, send],
        [store, square_low, square_low, square_low, square_f32, square_f32, chunks, up_rows]
        + [small_vm, square_f32, square_low, square_low, two_scales, vector_rows, small_vm]
        + [chunks],
        28,
    )
    last_send = after([last_send], *other_parts[:2])[0]
    last_other = swap(last_send, "wide", 1)
    gradient = exchange([g0, g1, g2, g3])
    (parts_zero,) = weight_parts(
        "weights_zero",
        {"hidden": (0, 0), "low": (0, NZ), "before": (1, 0), "grad": (1, NZ)},
        [low_zero, grad_zero, hidden_zero, before_zero, *map(Arrived, (first_other, last_other))],
        [far((4, NZ, 2, QUARTER, HID), bf16)],
    )
    gradient = [after([gradient[0]], parts_zero)[0]] + gradient[1:]
    parts_zero = lax.all_to_all(parts_zero, "wide", 0, 0, axis_index_groups=chips())
    total_one = plane_sum(
        [own_part, *other_parts],
        [auto((2, QUARTER, HID), f32)] + [sds((2, QUARTER, HID), bf16)] * 3,
    )
    total_one = exchange(total_one)

    modes, cells, small = launch(
        return_body,
        "return",
        ids,
        gradient,
        [doubled],
        [group, group, far((VROWS, CH), f32)],
        [square_low, vm((VROWS, CH), f32)],
        12,
    )
    result_one = total_one[0]
    for value in total_one[1:]:
        result_one = result_one + value.astype(f32)
    total_zero = launch(
        all_sum_body,
        "plane_sum_zero",
        ids,
        [],
        [Arrived(parts_zero)],
        [auto((NZ, 2, QUARTER, HID), bf16)],
        [vm((4, NZ, 2, QUARTER, HID), bf16)],
        12,
    )[0]
    (modes,), mix_zero = mix_back(0, False, modes, swap(modes, "wide", 1), saved_zero)
    sums_zero = spread(total_zero)
    size = VROWS + 2 * (2 * CH + 8) + 8
    base, sums, tail = launch(
        last_body,
        "last",
        ids,
        [modes, cells],
        [ms, small, mix_one, mix_zero, field, noise, norm_gain, table_back],
        [auto((CH, LINE), f32), line_sums, auto((size, CH), f32)],
        [line_low, line_low, params_two, pair, square_low],
        20,
    )
    result_zero = jnp.sum(sums_zero.astype(f32), axis=0)
    outs = exchange([o0, *after([o1, o2, o3], sums)])
    output = launch(
        output_body,
        "output",
        ids,
        [],
        [outs[0], *map(Arrived, outs[1:])],
        [far((CH, LINE), bf16)],
        [vm((NZ, CELLS, CH), bf16), vm((NZ, CH, CELLS), bf16)],
        12,
    )[0]
    sums = sums + swap(sums, "narrow", 1)
    grad_field = launch(
        close_body,
        "close",
        ids,
        [base, sums, swap(after([sums], total_zero)[0], "narrow", 2)],
        [ms, field, noise],
        [far((CH, LINE), f32)],
        [line_low, line_low, pair, vm((CH, LINE), f32)],
        16,
    )[0]
    tail = wide_total(tail, total_zero)
    one, zero = tail[:16], tail[16:32]
    mixed = tail[32 : size - 8].reshape(2, 2 * CH + 8, CH)[::-1]
    first = tail[size - 8 :]
    grad_gain = jnp.stack([first[0], zero[0], zero[3], one[0]]).reshape(2, 2, CH)
    grad_shift = jnp.stack([first[1], zero[1], zero[4], one[1]]).reshape(2, 2, CH)
    grad_down_bias = jnp.stack([zero[2], one[2]])
    grad_up_bias = jnp.stack([zero[8:12].reshape(D), one[8:12].reshape(D)])
    grad_mix = mixed[:, : 2 * CH].reshape(LAYERS, 2, 2, BS, CH).swapaxes(3, 4)
    grad_mix_bias = mixed[:, 2 * CH : 2 * CH + 4].reshape(LAYERS, 2, 2, CH)
    small = [grad_gain, grad_shift, grad_mix, grad_mix_bias, grad_up_bias, grad_down_bias]
    pieces_one = finish_weights(after([result_one], total_zero)[0])
    grads = launch(
        lambda *refs: weights_out_body(1, *refs),
        "weights_out_one",
        ids,
        pieces_one,
        [],
        [far((LAYERS, D, D), f32)] * 2,
        [vm((2, D, D), bf16), vm((2, D, D), f32)],
        12,
    )
    pieces_zero = finish_weights(result_zero, grad_field, output, grads[0], *small)
    grad_up, grad_down = launch(
        lambda *refs: weights_out_body(0, *refs),
        "weights_out_zero",
        ids,
        pieces_zero,
        grads,
        [far((LAYERS, D, D), f32)] * 2,
        [vm((2, D, D), bf16), vm((2, D, D), f32)],
        12,
        {9: 0, 10: 1},
    )
    return (
        output,
        grad_field,
        grad_gain,
        grad_shift,
        grad_mix,
        grad_mix_bias,
        grad_up,
        grad_up_bias,
        grad_down,
        grad_down_bias,
    )


def solution(mesh):
    placed = (
        P("narrow", "wide"),
        P("narrow", "wide"),
        P(None, None, "narrow"),
        P(None, None, "narrow"),
        P(None, None, None, "narrow", None),
        P(None, None, None, "narrow"),
        P(None, None, "narrow"),
        P(None, "narrow"),
        P(None, "narrow", None),
        P(None, "narrow"),
        P("narrow", "wide"),
    )
    return jax.shard_map(
        shards,
        mesh=mesh,
        in_specs=placed,
        out_specs=(
            P("narrow", "wide"),
            P("narrow", "wide"),
            P(None, None, "narrow"),
            P(None, None, "narrow"),
            P(None, None, None, "narrow", None),
            P(None, None, None, "narrow"),
            P(None, None, "narrow"),
            P(None, "narrow"),
            P(None, "narrow", None),
            P(None, "narrow"),
        ),
        check_vma=False,
    )
```

```python
import math

import jax
import jax.numpy as jnp
import numpy as np
from jax import lax
from jax.experimental import pallas as pl
from jax.experimental.pallas import tpu as pltpu
from jax.sharding import PartitionSpec as P

D = 512
FF = 2048
BS = 64
MODES = 32
GRID = 64
LAYERS = 2

NZ = 4
CH = D // NZ
CELLS = D
ROWS = 8
LINE = NZ * CELLS
SPAN = 2 * ROWS
NMODE = MODES * MODES
HALF = NMODE // 2
SLICE = D // 8
QUARTER = D // 4
HID = D // 2
VROWS = 32
PARAMS = 32

ORDER = (0, 3, 2, 1)

eps = 1e-05
shrink = 0.1
f32 = jnp.float32
bf16 = jnp.bfloat16

NN = (((1,), (0,)), ((), ()))
NT = (((1,), (1,)), ((), ()))
TN = (((0,), (0,)), ((), ()))


MICROS = {
    "stats": 3, "first": 3, "second": 4, "mix": 4, "mix_back": 4.5, "return": 3, "last": 4,
    "close": 3, "cells_one": 9, "cells_two": 11, "cells_three": 8, "weights_one": 7,
    "weights_zero": 7, "plane_sum": 3, "plane_sum_zero": 3, "output": 3, "weights_out_one": 3,
    "weights_out_zero": 3, "fan": 0.3, "small": 2,
}


def width_tables():
    kw = np.arange(MODES)[:, None] * np.arange(GRID)[None, :] % GRID
    angle = kw * (2.0 * math.pi / GRID)
    parts = np.stack([np.cos(angle), -np.sin(angle)], axis=1) / GRID
    full = np.einsum("kpw,hg->khpgw", parts, np.eye(ROWS)).reshape(D, D)
    doubled = full.reshape(MODES, -1) * np.where(np.arange(MODES) == 0, 1.0, 2.0)[:, None]
    doubled = doubled.reshape(D, D)
    return [np.ascontiguousarray(t).astype(bf16) for t in (full, doubled, full.T, doubled.T)]


def height_tables():
    along = np.arange(MODES)
    freq = np.where(along < MODES // 2, along, along - MODES + GRID)
    phase = np.arange(GRID)[:, None] * freq[None, :] % GRID
    angle = phase * (2.0 * math.pi / GRID)
    cosine, sine = np.cos(angle), np.sin(angle)
    from_real = np.stack([cosine, -sine], axis=1)
    from_imag = np.stack([sine, cosine], axis=1)
    table = np.stack([from_real, from_imag], axis=1)
    table = table.transpose(2, 3, 0, 1).reshape(2 * MODES, 2, NZ, SPAN)
    ahead, back = [], []
    for core in range(2):
        for groups_here in [[z ^ m for m in ORDER] for z in range(NZ)] + [list(range(NZ))]:
            turned = table[:, [core, 1 - core]][:, :, groups_here]
            ahead.append(turned.reshape(2 * MODES, 2 * GRID))
            back.append(turned[:, 0].reshape(2 * MODES, GRID).T)
    return np.stack(ahead).astype(bf16), np.ascontiguousarray(np.stack(back)).astype(bf16)


def sds(shape, dtype):
    return pltpu.VMEM(shape, dtype)


def far(shape, dtype):
    return pltpu.HBM(shape, dtype)


def auto(shape, dtype):
    return jax.ShapeDtypeStruct(shape, dtype)


class Copies:
    def __init__(self, sems):
        self.sems, self.used, self.left = sems, 0, []

    def start(self, source, target):
        copy = pltpu.make_async_copy(source, target, self.sems.at[self.used])
        self.used += 1
        copy.start()
        return copy

    def get(self, *pairs):
        return [self.start(source, target) for source, target in pairs]

    def put(self, source, target):
        self.left.append(self.start(source, target))

    def finish(self):
        for copy in self.left:
            copy.wait()


def wait(copies):
    for copy in copies:
        copy.wait()


class Arrived:
    def __init__(self, value):
        self.value = value


def launch(body, name, ids, near, distant, outs, scratch, vmem, aliases=None):
    hbm, local = pl.BlockSpec(memory_space=pltpu.HBM), pl.BlockSpec(memory_space=pltpu.VMEM)
    count = 64

    def whole(ids_ref, *refs):
        copies = Copies(refs[-1])
        body(ids_ref, copies, *refs[:-1])
        copies.finish()

    settled = []
    for value in distant:
        if isinstance(value, Arrived):
            settled.append(value.value)
        else:
            settled.append(pltpu.with_memory_space_constraint(value, pltpu.HBM))
    return pl.pallas_call(
        whole,
        name=name,
        out_shape=list(outs),
        in_specs=[pl.BlockSpec(memory_space=pltpu.SMEM)]
        + [local] * len(near)
        + [pl.BlockSpec(memory_space=pl.ANY) if isinstance(v, Arrived) else hbm for v in distant],
        out_specs=[
            hbm if getattr(out, "memory_space", None) == pltpu.HBM else local for out in outs
        ],
        scratch_shapes=list(scratch) + [pltpu.SemaphoreType.DMA((count,))],
        input_output_aliases=aliases or {},
        compiler_params=pltpu.CompilerParams(vmem_limit_bytes=vmem * 2**20),
        cost_estimate=pl.CostEstimate(
            flops=int(MICROS[name] * 1.1e9), bytes_accessed=2**16, transcendentals=0
        ),
    )(ids, *near, *settled)


def vm(shape, dtype):
    return pltpu.VMEM(shape, dtype)


def dot(a, b, dims=NN):
    return lax.dot_general(a, b, dims, preferred_element_type=f32)


def at(offset, size):
    return pl.ds(pl.multiple_of(offset, size), size)


def gelu_parts(v):
    cdf = 0.5 + 0.5 * lax.erf(v * (2.0**-0.5))
    slope = cdf + v * (jnp.exp(-0.5 * v * v) * ((2.0 * math.pi) ** -0.5))
    return v * cdf, slope


def diagonal(size):
    first = lax.broadcasted_iota(jnp.int32, (size, size), 0)
    return first == lax.broadcasted_iota(jnp.int32, (size, size), 1)


def column(row):
    wide = jnp.broadcast_to(row.astype(f32), (CH, CH))
    return jnp.sum(jnp.where(diagonal(CH), wide, 0.0), axis=1, keepdims=True)


def norm_rows(v, gain, shift):
    mean = jnp.mean(v, axis=1, keepdims=True)
    center = v - mean
    scale = lax.rsqrt(jnp.mean(center * center, axis=1, keepdims=True) + eps)
    unit = center * scale
    return unit * gain + shift, unit, scale


def norm_rows_back(dy, unit, scale, gain):
    dx = dy * gain
    mean = jnp.mean(dx, axis=1, keepdims=True)
    along = jnp.mean(dx * unit, axis=1, keepdims=True)
    back = scale * (dx - mean - unit * along)
    return back, jnp.sum(dy * unit, axis=0, keepdims=True), jnp.sum(dy, axis=0, keepdims=True)


def stats_body(
    ids, io, field, noise, norm_gain, norm_bias, down_bias, up_bias, up, down,
    sums, slices, a, b, gains, shifts, downs, ups, params, rows_vm,
):
    rows = at(ids[2] * SLICE, SLICE)
    first = io.get(
        (up.at[0, rows], rows_vm.at[0:SLICE]), (down.at[0, rows], rows_vm.at[SLICE : 2 * SLICE])
    )
    small = io.get((norm_gain, gains), (norm_bias, shifts), (down_bias, downs), (up_bias, ups))
    loads = io.get((field, a), (noise, b))
    wait(first)
    for n in range(NZ):
        io.put(rows_vm, slices.at[n, 0 : 2 * SLICE])
    wait(small)
    lines = []
    for source in (gains, shifts):
        lines += [source[l, j : j + 1, :] for l in range(LAYERS) for j in range(2)]
    lines += [downs[l : l + 1, :] for l in range(LAYERS)]
    for l in range(LAYERS):
        lines += [ups[l : l + 1, q * CH : (q + 1) * CH] for q in range(NZ)]
    lines = [line.astype(f32) for line in lines]
    lines.append(jnp.zeros((PARAMS - len(lines), CH), f32))
    params[...] = jnp.zeros((PARAMS, D), bf16)
    params[:, 0:CH] = jnp.concatenate(lines, axis=0).astype(bf16)
    for n in range(NZ):
        io.put(params, slices.at[n, 2 * SLICE : 2 * SLICE + PARAMS])
    wait(loads)
    v = a[...].astype(f32) + b[...].astype(f32)
    total = jnp.sum(v, axis=0, keepdims=True)
    center = v - total * (1.0 / CH)
    sums[0:1, :] = total
    sums[1:2, :] = jnp.sum(center * center, axis=0, keepdims=True)


def first_body(
    ids, io, s0, s1, s2, s3, field, noise, norm_gain, norm_bias, table_in, up, down, turned,
    out, ms_out, l0, l1, l2, l3, slices, a, b, gains, shifts, table, ms, lines, held,
):
    loads = io.get((field, a), (noise, b), (norm_gain, gains), (norm_bias, shifts))
    late = io.get((table_in, table))
    z, rows = ids[1], at(ids[2] * SLICE, SLICE)
    other = [
        io.start(turned.at[:, at((z ^ m) * CELLS, CELLS)], lines.at[m]) for m in range(NZ)
    ]
    other += io.get((up.at[1, rows], held.at[0:SLICE]), (down.at[1, rows], held.at[SLICE:]))
    sums = (s0, s1, s2, s3)
    mean = (s0[0:1, :] + s1[0:1, :] + s2[0:1, :] + s3[0:1, :]) * (1.0 / D)
    second = jnp.zeros_like(mean)
    for s in sums:
        apart = s[0:1, :] * (1.0 / CH) - mean
        second = second + s[1:2, :] + CH * (apart * apart)
    scale = lax.rsqrt(second * (1.0 / D) + eps)
    ms[0:1, :] = mean
    ms[1:2, :] = scale
    io.put(ms, ms_out)
    wait(loads)
    v = a[...].astype(f32) + b[...].astype(f32)
    gain, shift = column(gains[0, 0:1, :]), column(shifts[0, 0:1, :])
    normed = ((v - mean) * scale * gain + shift).astype(bf16)
    wait(other)
    for m, l in enumerate((l0, l1, l2, l3)):
        io.put(lines.at[m], l)
    for n in range(NZ):
        io.put(held, slices.at[n])
    wait(late)
    for s in range(NZ):
        part = normed[:, s * CELLS : (s + 1) * CELLS]
        out[s] = dot(table[...], part, NT).astype(bf16)


def second_body(
    ids, io, modes, ms_in, field, noise, norm_gain, norm_bias, table_in,
    p3, p2, p1, p0, a, b, gains, shifts, ms, table, held, own,
):
    z = ids[1]
    loads = io.get((field, a), (noise, b), (norm_gain, gains), (norm_bias, shifts), (ms_in, ms))
    more = io.get((table_in, table))
    wait(loads)
    v = a[...].astype(f32) + b[...].astype(f32)
    gain, shift = column(gains[0, 0:1, :]), column(shifts[0, 0:1, :])
    both = v + (v - ms[0:1, :]) * ms[1:2, :] * gain + shift
    wait(more)
    for s in range(NZ):
        held[s] = (
            dot(table[...], modes[s]) + both[:, s * CELLS : (s + 1) * CELLS].T
        ).astype(bf16)
    own[...] = held[z]
    io.put(own, p0)
    for m, out in ((1, p1), (2, p2), (3, p3)):
        out[...] = held[z ^ m]


def return_body(
    ids, io, g0, g3, g2, g1, table_in, out, small_out, cells_out, table, small, cells
):
    z = ids[1]
    loads = io.get((table_in, table))
    rows = jnp.zeros((VROWS, CH), f32)
    for m, g in enumerate((g0, g1, g2, g3)):
        cells[z ^ m] = g[0:CELLS, :]
        high, low = g[CELLS : CELLS + VROWS, :], g[CELLS + VROWS : CELLS + 2 * VROWS, :]
        rows = rows + (high.astype(f32) + low.astype(f32))
    io.put(cells, cells_out)
    small[...] = rows
    io.put(small, small_out)
    wait(loads)
    for s in range(NZ):
        out[s] = dot(table[...], cells[s]).astype(bf16)


def last_body(
    ids, io, modes, cells_in, ms_in, small, mix_one, mix_zero, field, noise, norm_gain, table_in,
    base, sums, tail, a, b, gains, ms, table, cells,
):
    loads = io.get((table_in, table), (ms_in, ms), (cells_in, cells))
    loads += io.get((field, a), (noise, b), (norm_gain, gains))
    size = 2 * CH + 8
    copies = io.get(
        (small, tail.at[0:VROWS]),
        (mix_one, tail.at[VROWS : VROWS + size]),
        (mix_zero, tail.at[VROWS + size : VROWS + 2 * size]),
    )
    wait(loads)
    col = column(gains[0, 0:1, :])
    gain_sum = jnp.zeros((CH, 1), f32)
    shift_sum = jnp.zeros((CH, 1), f32)
    for s in range(NZ):
        here = slice(s * CELLS, (s + 1) * CELLS)
        up = cells[s].astype(f32)
        dy = (dot(table[...], modes[s]) + up).T
        up = up.T
        v = a[:, here].astype(f32) + b[:, here].astype(f32)
        unit = (v - ms[0:1, here]) * ms[1:2, here]
        dx = dy * col
        sums[0:1, here] = jnp.sum(dx, axis=0, keepdims=True)
        sums[1:2, here] = jnp.sum(dx * unit, axis=0, keepdims=True)
        base[:, here] = up + ms[1:2, here] * dx
        gain_sum = gain_sum + jnp.sum(dy * unit, axis=1, keepdims=True)
        shift_sum = shift_sum + jnp.sum(dy, axis=1, keepdims=True)
    wait(copies)
    on = diagonal(CH)
    first = VROWS + 2 * size
    tail[first : first + 8, :] = jnp.zeros((8, CH), f32)
    tail[first : first + 1, :] = jnp.sum(jnp.where(on, gain_sum, 0.0), axis=0, keepdims=True)
    tail[first + 1 : first + 2, :] = jnp.sum(
        jnp.where(on, shift_sum, 0.0), axis=0, keepdims=True
    )


def close_body(ids, io, base, s0, s1, ms_in, field, noise, out, a, b, ms, result):
    loads = io.get((field, a), (noise, b), (ms_in, ms))
    mean = (s0[0:1, :] + s1[0:1, :]) * (1.0 / D)
    along = (s0[1:2, :] + s1[1:2, :]) * (1.0 / D)
    wait(loads)
    for s in range(NZ):
        here = slice(s * CELLS, (s + 1) * CELLS)
        v = a[:, here].astype(f32) + b[:, here].astype(f32)
        unit = (v - ms[0:1, here]) * ms[1:2, here]
        result[:, here] = base[:, here] - ms[1:2, here] * (mean[:, here] + unit * along[:, here])
        io.put(result.at[:, here], out.at[:, here])


def groups(arrays):
    return [arrays[0].at[s] for s in range(NZ)] if len(arrays) == 1 else list(arrays)


def mixing_matrix(real, imag):
    first = lax.broadcasted_iota(jnp.int32, (CH, CH), 0) // BS
    on = first == lax.broadcasted_iota(jnp.int32, (CH, CH), 1) // BS

    def spread(part):
        part = part.astype(f32).T
        return jnp.where(on, jnp.concatenate([part, part], axis=1), 0.0)

    real, imag = spread(real), spread(imag)
    top = jnp.concatenate([real, imag], axis=1)
    bottom = jnp.concatenate([-imag, real], axis=1)
    return jnp.concatenate([top, bottom], axis=0).astype(bf16)


def to_spectrum(table, own, other, out):
    sources = groups([own]) + groups([other])
    for k in range(0, MODES, 2):
        sides = [
            jnp.concatenate([source[SPAN * n : SPAN * (n + 1), :] for source in sources], axis=0)
            for n in (k, k + 1)
        ]
        modes = dot(table, jnp.concatenate(sides, axis=1)).astype(out.dtype)
        for n in range(2):
            here = slice(MODES * (k + n), MODES * (k + n + 1))
            out[here, :CH] = modes[:MODES, n * CH : (n + 1) * CH]
            out[here, CH:] = modes[MODES:, n * CH : (n + 1) * CH]


def from_spectrum(table, spectrum, outs):
    targets = groups(outs)
    for k in range(0, MODES, 2):
        sides = []
        for n in (k, k + 1):
            here = slice(MODES * n, MODES * (n + 1))
            sides.append(jnp.concatenate([spectrum[here, :CH], spectrum[here, CH:]], axis=0))
        cells = dot(table, jnp.concatenate(sides, axis=1)).astype(bf16)
        for n in range(2):
            rows = slice(SPAN * (k + n), SPAN * (k + n + 1))
            for m, target in enumerate(targets):
                target[rows, :] = cells[SPAN * m : SPAN * (m + 1), n * CH : (n + 1) * CH]


def variant(ids, cells):
    return ids[0] * (NZ + 1) + (ids[1] if cells else NZ)


def mix_body(layer, cells, ids, io, own, other, table, back, weight, bias, *refs):
    refs, take = list(refs), lambda n: [refs.pop(0) for _ in range(n)]
    outs, saved = take(NZ if cells else 1), take(4)
    spectrum, active, slope, square = refs
    which = variant(ids, cells)
    to_spectrum(table[which], own, other, spectrum)
    io.put(spectrum, saved[0])

    def product(j, values):
        matrix = mixing_matrix(weight[layer, j, 0], weight[layer, j, 1])
        shift = jnp.concatenate([bias[layer, j, 0:1, :], bias[layer, j, 1:2, :]], axis=1)
        return dot(values, matrix) + shift.astype(f32)

    value, inner = gelu_parts(product(0, spectrum[...]))
    active[...] = value.astype(bf16)
    slope[...] = inner.astype(slope.dtype)
    io.put(active, saved[1])
    io.put(slope, saved[2])
    two = product(1, active[...])
    bend = jnp.tanh(two * (1.0 / shrink))
    square[...] = (bend * bend).astype(square.dtype)
    io.put(square, saved[3])
    from_spectrum(back[which], (two - shrink * bend).astype(bf16), outs)


def mix_back_body(layer, cells, ids, io, own, other, table, back, weight, *refs):
    refs, take = list(refs), lambda n: [refs.pop(0) for _ in range(n)]
    saved, outs, (sums_out,) = take(4), take(NZ if cells else 1), take(1)
    spectrum, active, slope, square, low_one, low_two, sums = refs
    which = variant(ids, cells)
    share = at(ids[0] * HALF, HALF)
    late = io.get((saved[3], square), (saved[2], slope))
    later = io.get((saved[0].at[share], spectrum), (saved[1].at[share], active))
    to_spectrum(table[which], own, other, low_two)
    wait(late)

    def product(j, values):
        return dot(values, mixing_matrix(weight[layer, j, 0], weight[layer, j, 1]), NT)

    low_two[...] = (low_two[...].astype(f32) * square[...].astype(f32)).astype(bf16)
    low_one[...] = (product(1, low_two[...]) * slope[...].astype(f32)).astype(bf16)
    from_spectrum(back[which], product(0, low_one[...]).astype(bf16), outs)
    wait(later)
    lane = lax.broadcasted_iota(jnp.int32, (BS, CH), 1)
    sums[2 * CH :, :] = jnp.zeros((8, CH), f32)
    for j, (left, right) in enumerate(((spectrum, low_one), (active, low_two))):
        outer = dot(left[...], right[share, :], TN)
        real = outer[:CH, :CH] + outer[CH:, CH:]
        imag = outer[:CH, CH:] - outer[CH:, :CH]
        parts = jnp.concatenate(
            [
                jnp.where(lane < BS, real[:BS], pltpu.roll(imag[:BS], BS, 1)),
                jnp.where(lane < BS, pltpu.roll(real[BS:], BS, 1), imag[BS:]),
            ],
            axis=0,
        )
        sums[j * CH : (j + 1) * CH, :] = parts.T
        total = jnp.sum(right[share, :].astype(f32), axis=0, keepdims=True)
        first = 2 * CH + 2 * j
        sums[first : first + 1, :] = total[:, :CH]
        sums[first + 1 : first + 2, :] = total[:, CH:]
    io.put(sums, sums_out)


def load_weights(io, layer, ids, up, down, near, distant, store):
    place = ids[2]
    copies = io.get((up.at[layer], store.at[0, 0]), (down.at[layer], store.at[0, 1]))
    for core, array in enumerate((near, distant)):
        for side in range(2):
            for index, e in enumerate((0, 2, 4, 6) if side == 0 else (0, 4, 2, 6)):
                rows = at((place ^ e ^ core) * SLICE, SLICE)
                part = array.at[side, index]
                copies.append(io.start(part, store.at[1:NZ, side, rows]))
    return copies


def load_weights_one(io, ids, up, down, near, distant, store):
    copies = io.get((up.at[1], store.at[0, 0]), (down.at[1], store.at[0, 1]))
    for array, core in ((near, ids[0]), (distant, 1 - ids[0])):
        for chip in range(4):
            rows = at((2 * chip + core) * SLICE, SLICE)
            for side in range(2):
                part = array.at[chip, :, side * SLICE : (side + 1) * SLICE]
                copies.append(io.start(part, store.at[1:NZ, side, rows]))
    return copies


def fan_body(ids, io, arrived, out, held):
    wait([io.start(arrived.at[ids[1] ^ m], held.at[m - 1]) for m in range(1, NZ)])
    for chip in range(4):
        io.put(held, out.at[chip])


def gather_lanes(z, pieces, wide):
    for m, piece in enumerate(pieces):
        wide[:, at((z ^ m) * CH, CH)] = piece[...]


def scatter_lanes(z, wide, pieces):
    for m, piece in enumerate(pieces):
        piece[0:CELLS, :] = wide[:, at((z ^ m) * CH, CH)].astype(piece.dtype)


def store_send(io, core, chunk, place, keep, send):
    io.put(chunk.at[:, at(core * HID, HID)], keep)
    io.put(chunk.at[:, at((1 - core) * HID, HID)], send.at[place * CELLS : (place + 1) * CELLS])


def store_cells(io, values, place, send):
    for half in range(2):
        rows = slice((place + half) * CELLS, (place + half + 1) * CELLS)
        io.put(values.at[:, half * HID : (half + 1) * HID], send.at[rows])


def cells_one_body(
    ids, io, p0, p3, p2, p1, l0, l1, l2, l3, arrived, up, down, near, distant, table_in,
    a0, a3, a2, a1, vectors_out, up_shift_out, base_out, unit_one_out, scale_one_out,
    unit_two_out, scale_two_out, slope_out, low_out, keep, send, turned_out,
    store, wide, params, table, low, total, hidden, vectors, up_shift, base, unit_one, unit_two,
    scales, slope, turned, late,
):
    core, z = ids[0], ids[1]
    loads = [
        io.start(arrived.at[z ^ m, 2 * SLICE : 2 * SLICE + PARAMS, 0:CH], params.at[m])
        for m in range(NZ)
    ]
    loads += [
        io.start(p, wide.at[:, at((z ^ m) * CH, CH)]) for m, p in enumerate((p0, p1, p2, p3))
    ]
    pieces = [io.start(l, late.at[m]) for m, l in enumerate((l0, l1, l2, l3))]
    weights = load_weights(io, 0, ids, up, down, near, distant, store)
    last = io.get((table_in, table))
    wait(loads)
    for m in range(NZ):
        rows = params[m].astype(f32)
        vectors[0:10, at((z ^ m) * CH, CH)] = rows[0:10]
        for l in range(LAYERS):
            top = 10 + NZ * l
            shift = jnp.concatenate([rows[top + q : top + q + 1] for q in range(NZ)], axis=1)
            up_shift[l, m : m + 1, :] = shift
    io.put(vectors, vectors_out)
    io.put(up_shift, up_shift_out)
    state = wide[...].astype(f32)
    normed, unit, scale = norm_rows(state, vectors[1:2, :], vectors[5:6, :])
    low[...] = normed.astype(bf16)
    unit_two[...] = unit.astype(bf16)
    scales[0] = jnp.broadcast_to(scale, (CELLS, CH))
    total[...] = state + vectors[8:9, :]
    io.put(unit_two, unit_two_out)
    io.put(scales.at[0], scale_two_out)
    io.put(low, low_out)
    store_cells(io, low, NZ, send)
    wait(pieces)
    for m in range(NZ):
        turned[:, at((z ^ m) * CH, CH)] = late[m].T
    io.put(turned, turned_out)
    wait(weights[:2])
    for j in range(NZ):
        if j == 1:
            wait(weights[2:])
        before = dot(low[...], store[j, 0]) + up_shift[0, j : j + 1, :]
        value, inner = gelu_parts(before)
        hidden[j] = value.astype(bf16)
        slope[j] = inner.astype(bf16)
        io.put(slope.at[j], slope_out.at[j])
        store_send(io, core, hidden.at[j], j, keep.at[j], send)
        total[...] += dot(hidden[j], store[j, 1])
    state = total[...]
    normed, unit, scale = norm_rows(state, vectors[2:3, :], vectors[6:7, :])
    base[...] = state + normed
    unit_one[...] = unit.astype(bf16)
    scales[1] = jnp.broadcast_to(scale, (CELLS, CH))
    io.put(base, base_out)
    io.put(unit_one, unit_one_out)
    io.put(scales.at[1], scale_one_out)
    wait(last)
    total[...] = dot(table[...], normed.astype(bf16))
    scatter_lanes(z, total, (a0, a1, a2, a3))


def fill_small(rows, ups, z, small):
    for m in range(NZ):
        small[m, 0:8, :] = rows[0:8, at((z ^ m) * CH, CH)]
        line = ups[m : m + 1, :]
        for q in range(NZ):
            small[m, 8 + q : 9 + q, :] = line[:, q * CH : (q + 1) * CH]
        small[m, 12:16, :] = jnp.zeros((4, CH), f32)


def cells_two_body(
    ids, io, arrived, base_in, vectors_in, up_shift_in,
    turned_in, up, down, near, distant, back_in, table_in,
    a0, a3, a2, a1, o0, o1, o2, o3, small_out, grad_out, low_out, hidden_keep,
    before_keep, send,
    store, wide, back_table, table, low, low_grad, unit_two, total, other, hidden,
    before_grad, ups, base, vectors, up_shift, small, grad, result,
):
    core, z = ids[0], ids[1]
    loads = io.get((back_in, back_table), (base_in, base), (vectors_in, vectors))
    loads += io.get((up_shift_in, up_shift))
    loads += io.get((turned_in, low_grad))
    weights = load_weights_one(io, ids, up, down, near, distant, store)
    last = io.get((table_in, table))
    gather_lanes(z, [arrived.at[place] for place in ORDER], wide)
    wait(loads)
    state = base[...] + dot(back_table[...], wide[...])
    normed, unit, scale = norm_rows(state, vectors[3:4, :], vectors[7:8, :])
    low[...] = normed.astype(bf16)
    io.put(low, low_out)
    store_cells(io, low, 2 * NZ, send)
    unit_two[...] = unit
    total[...] = state + vectors[9:10, :]
    other[...] = jnp.zeros_like(other)
    store_cells(io, low_grad, 2 * NZ + 2, send)
    wait(weights[:2])
    for j in range(NZ):
        if j == 1:
            wait(weights[2:])
        before = dot(low[...], store[j, 0]) + up_shift[1, j : j + 1, :]
        value, inner = gelu_parts(before)
        hidden[j] = value.astype(bf16)
        store_send(io, core, hidden.at[j], j, hidden_keep.at[j], send)
        total[...] += dot(hidden[j], store[j, 1])
        turn = dot(low_grad[...], store[j, 1], NT) * inner
        before_grad[j] = turn.astype(bf16)
        store_send(io, core, before_grad.at[j], NZ + j, before_keep.at[j], send)
        ups[j : j + 1, :] = jnp.sum(before_grad[j].astype(f32), axis=0, keepdims=True)
        other[...] += dot(before_grad[j], store[j, 0], NT)
    gradient = low_grad[...].astype(f32)
    change, gain_row, shift_row = norm_rows_back(other[...], unit_two[...], scale, vectors[3:4, :])
    grad[...] = gradient + change
    io.put(grad, grad_out)
    result[...] = total[...].astype(bf16)
    for m, out in enumerate((o0, o1, o2, o3)):
        io.put(result.at[:, at((z ^ m) * CH, CH)], out)
    wait(last)
    total[...] = dot(table[...], grad[...].astype(bf16))
    scatter_lanes(z, total, (a0, a1, a2, a3))
    other[0:8, :] = jnp.zeros((8, D), f32)
    other[0:1, :] = gain_row
    other[1:2, :] = shift_row
    other[2:3, :] = jnp.sum(gradient, axis=0, keepdims=True)
    fill_small(other, ups, z, small)
    io.put(small, small_out)


def cells_three_body(
    ids, io, b0, b3, b2, b1, grad_in, unit_one_in, scale_one_in, unit_two_in, scale_two_in,
    vectors_in, small_in, slope_in, up, down, near, distant, back_in,
    g0, g3, g2, g1, low_grad_out, keep, send,
    store, wide, back_table, low_grad, total, other, before_grad, ups, small, grad, unit_one,
    unit_two, scales, vectors, small_one, slope,
):
    core, z = ids[0], ids[1]
    loads = io.get((back_in, back_table), (grad_in, grad), (vectors_in, vectors))
    loads += io.get((unit_one_in, unit_one), (scale_one_in, scales.at[0]))
    slopes = [io.start(slope_in.at[0], slope.at[0])]
    weights = load_weights(io, 0, ids, up, down, near, distant, store)
    slopes += [io.start(slope_in.at[j], slope.at[j]) for j in range(1, NZ)]
    later = io.get((unit_two_in, unit_two), (scale_two_in, scales.at[1]), (small_in, small_one))
    gather_lanes(z, (b0, b1, b2, b3), wide)
    wait(loads)
    dy = grad[...] + dot(back_table[...], wide[...])
    change, gain_one, shift_one = norm_rows_back(
        dy, unit_one[...].astype(f32), scales[0, :, 0:1], vectors[2:3, :]
    )
    total[...] = grad[...] + change
    low_grad[...] = total[...].astype(bf16)
    io.put(low_grad, low_grad_out)
    store_cells(io, low_grad, NZ, send)
    other[...] = jnp.zeros_like(other)
    wait(weights[:2])
    for j in range(NZ):
        slopes[j].wait()
        if j == 1:
            wait(weights[2:])
        turn = dot(low_grad[...], store[j, 1], NT) * slope[j].astype(f32)
        before_grad[j] = turn.astype(bf16)
        store_send(io, core, before_grad.at[j], j, keep.at[j], send)
        ups[j : j + 1, :] = jnp.sum(before_grad[j].astype(f32), axis=0, keepdims=True)
        other[...] += dot(before_grad[j], store[j, 0], NT)
    wait(later)
    change, gain_two, shift_two = norm_rows_back(
        other[...], unit_two[...].astype(f32), scales[1, :, 0:1], vectors[1:2, :]
    )
    total[...] += change
    pieces = (g0, g1, g2, g3)
    scatter_lanes(z, total, pieces)
    other[0:8, :] = jnp.zeros((8, D), f32)
    other[0:1, :] = gain_two
    other[1:2, :] = shift_two
    other[2:3, :] = jnp.sum(low_grad[...].astype(f32), axis=0, keepdims=True)
    other[3:4, :] = gain_one
    other[4:5, :] = shift_one
    fill_small(other, ups, z, small)
    for m, piece in enumerate(pieces):
        rows = jnp.concatenate([small_one[m], small[m]], axis=0)
        high = rows.astype(bf16)
        piece[CELLS : CELLS + VROWS, :] = high
        piece[CELLS + VROWS : CELLS + 2 * VROWS, :] = (rows - high.astype(f32)).astype(bf16)


def weights_body(
    places, ids, io, low_own, grad_own, hidden_own, before_own, *refs
):
    lows, left, right, product = refs[-4:]
    count = 1 + max(array for array, _ in places.values())
    sent, parts = refs[:count], refs[count:-4]

    def other(name, chunk):
        array, first = places[name]
        return sent[array].at[(first + chunk) * CELLS : (first + chunk + 1) * CELLS]

    loads = io.get((low_own, lows.at[0, 0]), (grad_own, lows.at[1, 0]))
    for side, name in enumerate(("low", "grad")):
        for half in range(2):
            target = lows.at[side, 1, :, half * HID : (half + 1) * HID]
            loads.append(io.start(other(name, half), target))
    later = []
    for j in range(NZ):
        step = []
        for side, (value, name) in enumerate(((before_own, "before"), (hidden_own, "hidden"))):
            step.append(io.start(value.at[j], right.at[j, side, 0:CELLS]))
            step.append(io.start(other(name, j), right.at[j, side, CELLS : 2 * CELLS]))
        later.append(step)
    wait(loads)
    for side in range(2):
        for half in range(2):
            left[side, :, half * CELLS : (half + 1) * CELLS] = lows[side, half].T
    for j in range(NZ):
        wait(later[j])
        for side in range(2):
            product[j, side] = dot(left[side], right[j, side]).astype(bf16)
        for q in range(4):
            if len(parts) == 1:
                rows, part = slice(q * QUARTER, (q + 1) * QUARTER), parts[0].at[q]
            else:
                rows, part = at(((ids[2] // 2) ^ q) * QUARTER, QUARTER), parts[q]
            io.put(product.at[j, :, rows], part.at[j])


def plane_sum_body(ids, io, k1, k2, k3, k0, t0, t1, t2, t3, own):
    wait(io.get((k0, own)))
    for m, out in enumerate((t0, t1, t2, t3)):
        part = own[m].astype(f32) + k1[m].astype(f32)
        part = part + (k2[m].astype(f32) + k3[m].astype(f32))
        out[...] = part.astype(out.dtype)


def all_sum_body(ids, io, parts, out, held):
    loads = [io.start(parts.at[:, m], held.at[:, m]) for m in range(NZ)]
    for m in range(NZ):
        loads[m].wait()
        part = held[0, m].astype(f32) + held[1, m].astype(f32)
        part = part + (held[2, m].astype(f32) + held[3, m].astype(f32))
        out[ids[1] ^ m] = part.astype(bf16)


def output_body(ids, io, o0, o1, o2, o3, out, held, wide):
    z = ids[1]
    loads = [io.start(o, held.at[m]) for m, o in enumerate((o0, o1, o2, o3))]
    for m in range(NZ):
        loads[m].wait()
        wide[m] = held[m].T
        io.put(wide.at[m], out.at[:, at((z ^ m) * CELLS, CELLS)])


def weights_out_body(layer, ids, io, *refs):
    core, chip = ids[0], ids[2] // 2
    pieces = refs[:8]
    up, down, both, result = refs[-4:]
    for e, piece in enumerate(pieces):
        rows, lanes = at((chip ^ (e // 2)) * QUARTER, QUARTER), at((core ^ (e % 2)) * HID, HID)
        both[:, rows, lanes] = piece[...]
    result[0] = both[0].astype(f32)
    io.put(result.at[0], up.at[layer])
    result[1] = both[1].T.astype(f32)
    io.put(result.at[1], down.at[layer])


def small_body(
    ids, io, left, right, gain_out, shift_out, mix_out, mix_bias_out, up_out, down_out,
    total, gain, shift, mix_bias, up, down,
):
    total[...] = left[...] + right[...]
    size = 2 * CH + 8
    first, zero, one = VROWS + 2 * size, VROWS // 2, 0
    blocks = (VROWS + size, VROWS)
    for l in range(LAYERS):
        for j in range(2):
            for part in range(2):
                here = blocks[l] + (2 * j + part) * BS
                io.put(total.at[here : here + BS], mix_out.at[l, j, part])
                here = blocks[l] + 2 * CH + 2 * j + part
                mix_bias[l, j, part : part + 1, :] = total[here : here + 1, :]
    for place, out, rows in (
        ((0, 0), gain, first), ((0, 1), gain, zero), ((1, 0), gain, zero + 3), ((1, 1), gain, one),
        ((0, 0), shift, first + 1), ((0, 1), shift, zero + 1), ((1, 0), shift, zero + 4),
        ((1, 1), shift, one + 1),
    ):
        l, j = place
        out[l, j : j + 1, :] = total[rows : rows + 1, :]
    for l, here in enumerate((zero, one)):
        down[l : l + 1, :] = total[here + 2 : here + 3, :]
        for q in range(NZ):
            up[l : l + 1, q * CH : (q + 1) * CH] = total[here + 8 + q : here + 9 + q, :]
    for source, out in (
        (gain, gain_out), (shift, shift_out), (mix_bias, mix_bias_out), (up, up_out),
        (down, down_out),
    ):
        io.put(source, out)


def swap(value, axis, mask):
    pairs = [(source, source ^ mask) for source in range(lax.axis_size(axis))]
    return lax.ppermute(value, axis, pairs)


def after(values, *done):
    values = list(values)
    return list(lax.optimization_barrier((*values, *done))[: len(values)])


def exchange(pieces):
    return [pieces[0]] + [swap(pieces[m], "narrow", m) for m in range(1, NZ)]


def in_order(pieces):
    return [pieces[m] for m in ORDER]


def spread(value):
    return lax.all_to_all(value, "narrow", 0, 0)


def chips():
    return [
        [8 * g + 2 * chip + core for chip in range(4)]
        for g in range(lax.axis_size("wide") // 8)
        for core in range(2)
    ]


def wide_total(value, mask, end):
    while mask < end:
        value = value + swap(value, "wide", mask)
        mask *= 2
    return value


def shards(
    field,
    noise,
    norm_gain,
    norm_bias,
    mix_weight,
    mix_bias,
    up_weight,
    up_bias,
    down_weight,
    down_bias,
    out_grad,
):
    wide, z = lax.axis_index("wide"), lax.axis_index("narrow")
    core, place = wide % 2, wide % 8
    ids = jnp.stack([core, z, place]).astype(jnp.int32)
    table, doubled, table_back, doubled_back = width_tables()
    height, height_back = height_tables()

    weight_turned = jnp.swapaxes(mix_weight, 3, 4)

    line_low, pair = vm((CH, LINE), bf16), vm((2, LINE), f32)
    params_two = vm((LAYERS, 2, CH), bf16)
    square_low, square_f32 = vm((D, D), bf16), vm((D, D), f32)
    chunks = vm((NZ, CELLS, D), bf16)
    store = vm((NZ, 2, D, D), bf16)
    up_rows, vector_rows = vm((NZ, D), f32), vm((10, D), f32)
    shift_rows = vm((LAYERS, NZ, D), f32)
    small_vm, two_scales = vm((NZ, VROWS // 2, CH), f32), vm((2, CELLS, CH), f32)
    piece_vm, group_vm = vm((CELLS, CH), bf16), vm((NZ, D, CH), bf16)
    modes_vm, share_vm = vm((NMODE, 2 * CH), bf16), vm((HALF, 2 * CH), bf16)
    mix_sums = (2 * CH + 8, CH)


    own_piece, piece, far_piece = [kind((CELLS, CH), bf16) for kind in (auto, sds, far)]
    group = auto((NZ, D, CH), bf16)
    far_modes = far((NMODE, 2 * CH), bf16)
    far_low, far_f32, far_thin = far((CELLS, D), bf16), far((CELLS, D), f32), far((CELLS, CH), f32)
    halves, whole = far((NZ, CELLS, HID), bf16), far((NZ, CELLS, D), bf16)
    send = far(((NZ + 2) * CELLS, HID), bf16)
    parts = far((NZ, 2, QUARTER, HID), bf16)
    line_sums = auto((2, LINE), f32)
    far_small = far((NZ, VROWS // 2, CH), f32)

    def mix(layer, cells, own, other):
        outs = launch(
            lambda *refs: mix_body(layer, cells, *refs),
            "mix",
            ids,
            [own, other, height, height_back, weight_turned, mix_bias],
            [],
            ([own_piece] + [piece] * 3 if cells else [group]) + [far_modes] * 4,
            [modes_vm] * 4,
            16,
        )
        pieces = list(outs[:-4])
        return pieces[:1] + pieces[:0:-1], outs[-4:]

    def mix_back(layer, cells, own, other, saved):
        outs = launch(
            lambda *refs: mix_back_body(layer, cells, *refs),
            "mix_back",
            ids,
            [own, other, height, height_back, weight_turned],
            saved,
            ([own_piece] + [piece] * 3 if cells else [group]) + [far(mix_sums, f32)],
            [share_vm, share_vm, modes_vm, modes_vm, modes_vm, modes_vm, vm(mix_sums, f32)],
            16,
        )
        pieces = list(outs[:-1])
        return pieces[:1] + pieces[:0:-1], outs[-1]

    def first_step(arrived):
        others = [lax.dynamic_index_in_dim(arrived, z ^ m, 0, False) for m in range(1, NZ)]
        ups = jnp.stack([r[:SLICE] for r in others])
        downs = jnp.stack([r[SLICE : 2 * SLICE] for r in others])
        return ups, downs, swap(ups, "wide", 2), swap(downs, "wide", 4)

    def second_step(ups, downs, ups_near, downs_near):
        ups, downs = jnp.stack([ups, ups_near]), jnp.stack([downs, downs_near])
        return ups, downs, swap(ups, "wide", 4), swap(downs, "wide", 2)

    def third_step(ups, downs, ups_far, downs_far):
        held = jnp.stack(
            [jnp.concatenate([ups, ups_far]), jnp.concatenate([downs, downs_far])]
        )
        return held, swap(held, "wide", 1)

    def fan(arrived):
        sent = launch(
            fan_body, "fan", ids, [], [Arrived(arrived)], [far((4, 3, 2 * SLICE, D), bf16)],
            [vm((3, 2 * SLICE, D), bf16)], 12,
        )[0]
        return sent

    own, mine = launch(
        stats_body,
        "stats",
        ids,
        [],
        [field, noise, norm_gain, norm_bias, down_bias, up_bias, up_weight, down_weight],
        [line_sums, far((NZ, 2 * SLICE + PARAMS, D), bf16)],
        [line_low, line_low, params_two, params_two, vm((LAYERS, CH), bf16)]
        + [vm((LAYERS, D), bf16), vm((PARAMS, D), bf16), vm((2 * SLICE, D), bf16)],
        12,
    )
    first_sums = [own] + [swap(own, "narrow", m) for m in range(1, NZ)]
    zero = spread(after([mine], *first_sums[1:])[0])

    modes, ms, *late, mine_one = launch(
        first_body,
        "first",
        ids,
        first_sums,
        [field, noise, norm_gain, norm_bias, table, up_weight, down_weight, out_grad],
        [group, far((2, LINE), f32)]
        + [far((CH, CELLS), bf16)] * NZ
        + [far((NZ, 2 * SLICE, D), bf16)],
        [line_low, line_low, params_two, params_two, square_low, pair]
        + [vm((NZ, CH, CELLS), bf16), vm((2 * SLICE, D), bf16)],
        16,
    )
    (modes,), saved_zero = mix(0, False, modes, swap(modes, "wide", 1))
    spread_zero = second_step(*first_step(after([zero], modes)[0]))
    late = exchange([late[0], *after(late[1:], modes)])
    p3, p2, p1, p0 = launch(
        second_body,
        "second",
        ids,
        [modes],
        [ms, field, noise, norm_gain, norm_bias, doubled_back],
        [piece] * 3 + [far_piece],
        [line_low, line_low, params_two, params_two, pair, square_low, group_vm, piece_vm],
        16,
    )
    p1, p2, p3 = after([p1, p2, p3], *late[1:])
    state = exchange([p0, p1, p2, p3])
    ups_zero, downs_zero = after(spread_zero[2:], *state[1:])
    weights_zero = third_step(*spread_zero[:2], ups_zero, downs_zero)

    one = spread(after([mine_one], *state[1:])[0])

    (
        a0, a3, a2, a1, vectors, up_shift, base, unit_one, scale_one, unit_two, scale_two, slope,
        low_zero, hidden_zero, send_zero, grad_one,
    ) = launch(
        cells_one_body,
        "cells_one",
        ids,
        [],
        [state[0], *map(Arrived, state[:0:-1]), late[0], *map(Arrived, late[1:]), Arrived(zero), up_weight, down_weight, *map(Arrived, weights_zero), table],
        [own_piece]
        + [piece] * 3
        + [far((10, D), f32), far((LAYERS, NZ, D), f32)]
        + [far_f32, far_low, far_thin, far_low, far_thin, whole]
        + [far_low, halves, send, far_low],
        [store, square_low, vm((NZ, PARAMS, CH), bf16), square_low, square_low, square_f32]
        + [chunks, vector_rows, shift_rows, square_f32, square_low, square_low, two_scales]
        + [chunks, square_low, vm((NZ, CH, CELLS), bf16)],
        28,
    )

    sent_one = fan(after([one], a0)[0])
    own = jnp.stack(after(in_order(exchange([a0, a1, a2, a3])), sent_one))
    near_one = lax.all_to_all(sent_one, "wide", 0, 0, axis_index_groups=chips())
    modes, saved_one = mix(1, True, own, swap(own, "wide", 1))
    ready = modes[0]
    modes = jnp.stack(after(in_order(exchange(modes)), near_one))
    near_one = after([near_one], modes)[0]
    weights_one = [near_one, swap(near_one, "wide", 1)]
    first_other = swap(after([send_zero], ready)[0], "wide", 1)
    base = after([base], first_other)[0]

    (
        a0, a3, a2, a1, o0, o1, o2, o3, small, grad, low_one, hidden_one, before_one,
        send_one,
    ) = launch(
        cells_two_body,
        "cells_two",
        ids,
        [modes],
        [base, vectors, up_shift, grad_one, up_weight, down_weight]
        + [*map(Arrived, weights_one), doubled_back, doubled],
        [own_piece]
        + [piece] * 3
        + [far_piece] * 4
        + [far_small, far_f32, far_low, halves, halves]
        + [far(((2 * NZ + 4) * CELLS, HID), bf16)],
        [store, square_low, square_low, square_low, square_low, square_low]
        + [square_f32] * 3
        + [chunks, chunks, up_rows, square_f32, vector_rows, shift_rows, small_vm, square_f32]
        + [square_low],
        34,
    )

    def finish_weights(result, *done):
        mask = 8
        while mask < lax.axis_size("wide"):
            result = result + swap(result.astype(bf16), "wide", mask).astype(f32)
            mask *= 2
        result = result.astype(bf16)
        pieces = []
        for value in [result] + [swap(result, "wide", q) for q in (2, 4, 6)]:
            pieces += [value, swap(after([value], *done)[0], "wide", 1)]
        return pieces

    def weight_parts(name, places, operands, outs):
        return launch(
            lambda *refs: weights_body(places, *refs),
            name,
            ids,
            [],
            operands,
            outs,
            [vm((2, 2, CELLS, D), bf16), vm((2, D, 2 * CELLS), bf16)]
            + [vm((NZ, 2, 2 * CELLS, HID), bf16), vm((NZ, 2, D, HID), bf16)],
            20,
        )

    own = exchange([a0, a1, a2, a3])
    parts_one = weight_parts(
        "weights_one",
        {"hidden": (0, 0), "before": (0, NZ), "low": (0, 2 * NZ), "grad": (0, 2 * NZ + 2)},
        [low_one, grad_one, hidden_one, before_one, Arrived(swap(send_one, "wide", 1))],
        [parts] * 4,
    )
    own = jnp.stack(after(in_order(own), parts_one[0]))
    modes, mix_one = mix_back(1, True, own, swap(own, "wide", 1), saved_one)
    own_part, *other_parts = [parts_one[0], *after(parts_one[1:], modes[0])]
    modes = exchange(modes)
    other_parts[2] = after([other_parts[2]], *modes[1:])[0]
    other_parts = [swap(other_parts[q - 1], "wide", 2 * q) for q in (1, 2, 3)]

    g0, g3, g2, g1, grad_zero, before_zero, last_send = launch(
        cells_three_body,
        "cells_three",
        ids,
        in_order(modes),
        [grad, unit_one, scale_one, unit_two, scale_two, vectors, small, slope]
        + [up_weight, down_weight, *map(Arrived, weights_zero), table_back],
        [auto((CELLS + 2 * VROWS, CH), bf16)]
        + [sds((CELLS + 2 * VROWS, CH), bf16)] * 3
        + [far_low, halves, send],
        [store, square_low, square_low, square_low, square_f32, square_f32, chunks, up_rows]
        + [small_vm, square_f32, square_low, square_low, two_scales, vector_rows, small_vm]
        + [chunks],
        28,
    )
    last_send = after([last_send], *other_parts[:2])[0]
    last_other = swap(last_send, "wide", 1)
    gradient = exchange([g0, g1, g2, g3])
    (parts_zero,) = weight_parts(
        "weights_zero",
        {"hidden": (0, 0), "low": (0, NZ), "before": (1, 0), "grad": (1, NZ)},
        [low_zero, grad_zero, hidden_zero, before_zero, *map(Arrived, (first_other, last_other))],
        [far((4, NZ, 2, QUARTER, HID), bf16)],
    )
    gradient = [after([gradient[0]], parts_zero)[0]] + gradient[1:]
    parts_zero = after([parts_zero], other_parts[2])[0]
    parts_zero = lax.all_to_all(parts_zero, "wide", 0, 0, axis_index_groups=chips())
    modes, small, cells = launch(
        return_body,
        "return",
        ids,
        in_order(gradient),
        [doubled],
        [group, far((VROWS, CH), f32), far((NZ, D, CH), bf16)],
        [square_low, vm((VROWS, CH), f32), group_vm],
        12,
    )
    outs = exchange([o0, *after([o1, o2, o3], modes)])
    (modes,), mix_zero = mix_back(0, False, modes, swap(modes, "wide", 1), saved_zero)
    total_one = launch(
        plane_sum_body,
        "plane_sum",
        ids,
        other_parts,
        after([own_part], modes),
        [auto((2, QUARTER, HID), f32)] + [sds((2, QUARTER, HID), bf16)] * 3,
        [vm((NZ, 2, QUARTER, HID), bf16)],
        12,
    )
    total_one = exchange(total_one)
    size = VROWS + 2 * (2 * CH + 8) + 8
    modes = after([modes], *outs[1:])[0]
    base, sums, tail = launch(
        last_body,
        "last",
        ids,
        [modes],
        [cells, ms, small, mix_one, mix_zero, field, noise, norm_gain, table_back],
        [auto((CH, LINE), f32), line_sums, auto((size, CH), f32)],
        [line_low, line_low, params_two, pair, square_low, group_vm],
        20,
    )
    output = launch(
        output_body,
        "output",
        ids,
        [],
        [outs[0], *map(Arrived, outs[1:])],
        [far((CH, LINE), bf16)],
        [vm((NZ, CELLS, CH), bf16), vm((NZ, CH, CELLS), bf16)],
        12,
    )[0]
    total_zero = launch(
        all_sum_body,
        "plane_sum_zero",
        ids,
        [],
        [Arrived(after([parts_zero], output)[0])],
        [auto((NZ, 2, QUARTER, HID), bf16)],
        [vm((4, NZ, 2, QUARTER, HID), bf16)],
        12,
    )[0]
    sums = sums + swap(sums, "narrow", 1)
    grad_field = launch(
        close_body,
        "close",
        ids,
        [base, sums, swap(sums, "narrow", 2)],
        [ms, field, noise],
        [far((CH, LINE), f32)],
        [line_low, line_low, pair, vm((CH, LINE), f32)],
        16,
    )[0]
    tail = wide_total(tail, 1, 4)
    sums_zero = spread(after([total_zero], grad_field, tail, *total_one[1:])[0])
    result_one = total_one[0]
    for value in total_one[1:]:
        result_one = result_one + value.astype(f32)
    last_mask = lax.axis_size("wide") // 2
    tail = wide_total(tail, 4, last_mask)
    result_zero = jnp.sum(sums_zero.astype(f32), axis=0)
    small_shapes = [
        (LAYERS, 2, CH), (LAYERS, 2, CH), (LAYERS, 2, 2, BS, CH), (LAYERS, 2, 2, CH), (LAYERS, D),
        (LAYERS, CH),
    ]
    small = launch(
        small_body,
        "small",
        ids,
        [tail, swap(tail, "wide", last_mask)],
        [],
        [far(shape, f32) for shape in small_shapes],
        [vm((size, CH), f32)] + [vm(small_shapes[place], f32) for place in (0, 1, 3, 4, 5)],
        12,
    )
    grad_gain, grad_shift, grad_mix, grad_mix_bias, grad_up_bias, grad_down_bias = small
    grad_mix = grad_mix.swapaxes(3, 4)
    pieces_one = finish_weights(after([result_one], total_zero)[0])
    grads = launch(
        lambda *refs: weights_out_body(1, *refs),
        "weights_out_one",
        ids,
        pieces_one,
        [],
        [far((LAYERS, D, D), f32)] * 2,
        [vm((2, D, D), bf16), vm((2, D, D), f32)],
        12,
    )
    pieces_zero = finish_weights(result_zero, grad_field, output, grads[0], small[0])
    grad_up, grad_down = launch(
        lambda *refs: weights_out_body(0, *refs),
        "weights_out_zero",
        ids,
        pieces_zero,
        grads,
        [far((LAYERS, D, D), f32)] * 2,
        [vm((2, D, D), bf16), vm((2, D, D), f32)],
        12,
        {9: 0, 10: 1},
    )
    return (
        output,
        grad_field,
        grad_gain,
        grad_shift,
        grad_mix,
        grad_mix_bias,
        grad_up,
        grad_up_bias,
        grad_down,
        grad_down_bias,
    )


def solution(mesh):
    placed = (
        P("narrow", "wide"),
        P("narrow", "wide"),
        P(None, None, "narrow"),
        P(None, None, "narrow"),
        P(None, None, None, "narrow", None),
        P(None, None, None, "narrow"),
        P(None, None, "narrow"),
        P(None, "narrow"),
        P(None, "narrow", None),
        P(None, "narrow"),
        P("narrow", "wide"),
    )
    return jax.shard_map(
        shards,
        mesh=mesh,
        in_specs=placed,
        out_specs=(
            P("narrow", "wide"),
            P("narrow", "wide"),
            P(None, None, "narrow"),
            P(None, None, "narrow"),
            P(None, None, None, "narrow", None),
            P(None, None, None, "narrow"),
            P(None, None, "narrow"),
            P(None, "narrow"),
            P(None, "narrow", None),
            P(None, "narrow"),
        ),
        check_vma=False,
    )
```

```python
import math

import jax
import jax.numpy as jnp
import numpy as np
from jax import lax
from jax.experimental import pallas as pl
from jax.experimental.pallas import tpu as pltpu
from jax.sharding import PartitionSpec as P

D = 512
FF = 2048
BS = 64
MODES = 32
GRID = 64
LAYERS = 2

NZ = 4
CH = D // NZ
CELLS = D
ROWS = 8
LINE = NZ * CELLS
SPAN = 2 * ROWS
NMODE = MODES * MODES
HALF = NMODE // 2
SLICE = D // 8
QUARTER = D // 4
HID = D // 2
VROWS = 32
PARAMS = 32

ORDER = (0, 3, 2, 1)

eps = 1e-05
shrink = 0.1
f32 = jnp.float32
bf16 = jnp.bfloat16

NN = (((1,), (0,)), ((), ()))
NT = (((1,), (1,)), ((), ()))
TN = (((0,), (0,)), ((), ()))


MICROS = {
    "stats": 3, "first": 3, "second": 4, "mix": 4, "mix_back": 4.5, "return": 3, "last": 4,
    "close": 3, "cells_one": 9, "cells_two": 11, "cells_three": 8, "weights_one": 7,
    "weights_zero": 7, "plane_sum": 3, "plane_sum_zero": 3, "output": 3, "weights_out_one": 3,
    "weights_out_zero": 3, "fan": 0.3, "small": 2,
}


def width_tables():
    kw = np.arange(MODES)[:, None] * np.arange(GRID)[None, :] % GRID
    angle = kw * (2.0 * math.pi / GRID)
    parts = np.stack([np.cos(angle), -np.sin(angle)], axis=1) / GRID
    full = np.einsum("kpw,hg->khpgw", parts, np.eye(ROWS)).reshape(D, D)
    doubled = full.reshape(MODES, -1) * np.where(np.arange(MODES) == 0, 1.0, 2.0)[:, None]
    doubled = doubled.reshape(D, D)
    return [np.ascontiguousarray(t).astype(bf16) for t in (full, doubled, full.T, doubled.T)]


def height_tables():
    along = np.arange(MODES)
    freq = np.where(along < MODES // 2, along, along - MODES + GRID)
    phase = np.arange(GRID)[:, None] * freq[None, :] % GRID
    angle = phase * (2.0 * math.pi / GRID)
    cosine, sine = np.cos(angle), np.sin(angle)
    from_real = np.stack([cosine, -sine], axis=1)
    from_imag = np.stack([sine, cosine], axis=1)
    table = np.stack([from_real, from_imag], axis=1)
    table = table.transpose(2, 3, 0, 1).reshape(2 * MODES, 2, NZ, SPAN)
    ahead, back = [], []
    for core in range(2):
        for groups_here in [[z ^ m for m in ORDER] for z in range(NZ)] + [list(range(NZ))]:
            turned = table[:, [core, 1 - core]][:, :, groups_here]
            ahead.append(turned.reshape(2 * MODES, 2 * GRID))
            back.append(turned[:, 0].reshape(2 * MODES, GRID).T)
    return np.stack(ahead).astype(bf16), np.ascontiguousarray(np.stack(back)).astype(bf16)


def sds(shape, dtype):
    return pltpu.VMEM(shape, dtype)


def far(shape, dtype):
    return pltpu.HBM(shape, dtype)


def auto(shape, dtype):
    return jax.ShapeDtypeStruct(shape, dtype)


class Copies:
    def __init__(self, sems):
        self.sems, self.used, self.left = sems, 0, []

    def start(self, source, target):
        copy = pltpu.make_async_copy(source, target, self.sems.at[self.used])
        self.used += 1
        copy.start()
        return copy

    def get(self, *pairs):
        return [self.start(source, target) for source, target in pairs]

    def put(self, source, target):
        self.left.append(self.start(source, target))

    def finish(self):
        for copy in self.left:
            copy.wait()


def wait(copies):
    for copy in copies:
        copy.wait()


class Arrived:
    def __init__(self, value):
        self.value = value


def launch(body, name, ids, near, distant, outs, scratch, vmem, aliases=None):
    hbm, local = pl.BlockSpec(memory_space=pltpu.HBM), pl.BlockSpec(memory_space=pltpu.VMEM)
    count = 64

    def whole(ids_ref, *refs):
        copies = Copies(refs[-1])
        body(ids_ref, copies, *refs[:-1])
        copies.finish()

    settled = []
    for value in distant:
        if isinstance(value, Arrived):
            settled.append(value.value)
        else:
            settled.append(pltpu.with_memory_space_constraint(value, pltpu.HBM))
    return pl.pallas_call(
        whole,
        name=name,
        out_shape=list(outs),
        in_specs=[pl.BlockSpec(memory_space=pltpu.SMEM)]
        + [local] * len(near)
        + [pl.BlockSpec(memory_space=pl.ANY) if isinstance(v, Arrived) else hbm for v in distant],
        out_specs=[
            hbm if getattr(out, "memory_space", None) == pltpu.HBM else local for out in outs
        ],
        scratch_shapes=list(scratch) + [pltpu.SemaphoreType.DMA((count,))],
        input_output_aliases=aliases or {},
        compiler_params=pltpu.CompilerParams(vmem_limit_bytes=vmem * 2**20),
        cost_estimate=pl.CostEstimate(
            flops=int(MICROS[name] * 1.1e9), bytes_accessed=2**16, transcendentals=0
        ),
    )(ids, *near, *settled)


def vm(shape, dtype):
    return pltpu.VMEM(shape, dtype)


def dot(a, b, dims=NN):
    return lax.dot_general(a, b, dims, preferred_element_type=f32)


def at(offset, size):
    return pl.ds(pl.multiple_of(offset, size), size)


def gelu_parts(v):
    cdf = 0.5 + 0.5 * lax.erf(v * (2.0**-0.5))
    slope = cdf + v * (jnp.exp(-0.5 * v * v) * ((2.0 * math.pi) ** -0.5))
    return v * cdf, slope


def diagonal(size):
    first = lax.broadcasted_iota(jnp.int32, (size, size), 0)
    return first == lax.broadcasted_iota(jnp.int32, (size, size), 1)


def column(row):
    wide = jnp.broadcast_to(row.astype(f32), (CH, CH))
    return jnp.sum(jnp.where(diagonal(CH), wide, 0.0), axis=1, keepdims=True)


def norm_rows(v, gain, shift):
    mean = jnp.mean(v, axis=1, keepdims=True)
    center = v - mean
    scale = lax.rsqrt(jnp.mean(center * center, axis=1, keepdims=True) + eps)
    unit = center * scale
    return unit * gain + shift, unit, scale


def norm_rows_back(dy, unit, scale, gain):
    dx = dy * gain
    mean = jnp.mean(dx, axis=1, keepdims=True)
    along = jnp.mean(dx * unit, axis=1, keepdims=True)
    back = scale * (dx - mean - unit * along)
    return back, jnp.sum(dy * unit, axis=0, keepdims=True), jnp.sum(dy, axis=0, keepdims=True)


def stats_body(
    ids, io, field, noise, norm_gain, norm_bias, down_bias, up_bias, up, down,
    sums, slices, a, b, gains, shifts, downs, ups, params, rows_vm,
):
    rows = at(ids[2] * SLICE, SLICE)
    first = io.get(
        (up.at[0, rows], rows_vm.at[0:SLICE]), (down.at[0, rows], rows_vm.at[SLICE : 2 * SLICE])
    )
    small = io.get((norm_gain, gains), (norm_bias, shifts), (down_bias, downs), (up_bias, ups))
    loads = io.get((field, a), (noise, b))
    wait(first)
    for n in range(NZ):
        io.put(rows_vm, slices.at[n, 0 : 2 * SLICE])
    wait(small)
    lines = []
    for source in (gains, shifts):
        lines += [source[l, j : j + 1, :] for l in range(LAYERS) for j in range(2)]
    lines += [downs[l : l + 1, :] for l in range(LAYERS)]
    for l in range(LAYERS):
        lines += [ups[l : l + 1, q * CH : (q + 1) * CH] for q in range(NZ)]
    lines = [line.astype(f32) for line in lines]
    lines.append(jnp.zeros((PARAMS - len(lines), CH), f32))
    params[...] = jnp.zeros((PARAMS, D), bf16)
    params[:, 0:CH] = jnp.concatenate(lines, axis=0).astype(bf16)
    for n in range(NZ):
        io.put(params, slices.at[n, 2 * SLICE : 2 * SLICE + PARAMS])
    wait(loads)
    v = a[...].astype(f32) + b[...].astype(f32)
    total = jnp.sum(v, axis=0, keepdims=True)
    center = v - total * (1.0 / CH)
    sums[0:1, :] = total
    sums[1:2, :] = jnp.sum(center * center, axis=0, keepdims=True)


def first_body(
    ids, io, s0, s1, s2, s3, field, noise, norm_gain, norm_bias, table_in, up, down, turned,
    out, ms_out, l0, l1, l2, l3, slices, a, b, gains, shifts, table, ms, lines, held,
):
    loads = io.get((field, a), (noise, b), (norm_gain, gains), (norm_bias, shifts))
    late = io.get((table_in, table))
    z, rows = ids[1], at(ids[2] * SLICE, SLICE)
    other = [
        io.start(turned.at[:, at((z ^ m) * CELLS, CELLS)], lines.at[m]) for m in range(NZ)
    ]
    other += io.get((up.at[1, rows], held.at[0:SLICE]), (down.at[1, rows], held.at[SLICE:]))
    sums = (s0, s1, s2, s3)
    mean = (s0[0:1, :] + s1[0:1, :] + s2[0:1, :] + s3[0:1, :]) * (1.0 / D)
    second = jnp.zeros_like(mean)
    for s in sums:
        apart = s[0:1, :] * (1.0 / CH) - mean
        second = second + s[1:2, :] + CH * (apart * apart)
    scale = lax.rsqrt(second * (1.0 / D) + eps)
    ms[0:1, :] = mean
    ms[1:2, :] = scale
    io.put(ms, ms_out)
    wait(loads)
    v = a[...].astype(f32) + b[...].astype(f32)
    gain, shift = column(gains[0, 0:1, :]), column(shifts[0, 0:1, :])
    normed = ((v - mean) * scale * gain + shift).astype(bf16)
    wait(other)
    for m, l in enumerate((l0, l1, l2, l3)):
        io.put(lines.at[m], l)
    for n in range(NZ):
        io.put(held, slices.at[n])
    wait(late)
    for s in range(NZ):
        part = normed[:, s * CELLS : (s + 1) * CELLS]
        out[s] = dot(table[...], part, NT).astype(bf16)


def second_body(
    ids, io, modes, ms_in, field, noise, norm_gain, norm_bias, table_in,
    p3, p2, p1, p0, a, b, gains, shifts, ms, table, held, own,
):
    z = ids[1]
    loads = io.get((field, a), (noise, b), (norm_gain, gains), (norm_bias, shifts), (ms_in, ms))
    more = io.get((table_in, table))
    wait(loads)
    v = a[...].astype(f32) + b[...].astype(f32)
    gain, shift = column(gains[0, 0:1, :]), column(shifts[0, 0:1, :])
    center = v - ms[0:1, :]
    both = center + center * ms[1:2, :] * gain + shift
    wait(more)
    for s in range(NZ):
        held[s] = (
            dot(table[...], modes[s]) + both[:, s * CELLS : (s + 1) * CELLS].T
        ).astype(bf16)
    own[...] = held[z]
    io.put(own, p0)
    for m, out in ((1, p1), (2, p2), (3, p3)):
        out[...] = held[z ^ m]


def return_body(
    ids, io, g0, g3, g2, g1, table_in, out, small_out, cells_out, table, small, cells
):
    z = ids[1]
    loads = io.get((table_in, table))
    rows = jnp.zeros((VROWS, CH), f32)
    for m, g in enumerate((g0, g1, g2, g3)):
        cells[z ^ m] = g[0:CELLS, :]
        high, low = g[CELLS : CELLS + VROWS, :], g[CELLS + VROWS : CELLS + 2 * VROWS, :]
        rows = rows + (high.astype(f32) + low.astype(f32))
    io.put(cells, cells_out)
    small[...] = rows
    io.put(small, small_out)
    wait(loads)
    for s in range(NZ):
        out[s] = dot(table[...], cells[s]).astype(bf16)


def last_body(
    ids, io, modes, cells_in, ms_in, small, mix_one, mix_zero, field, noise, norm_gain, table_in,
    base, sums, tail, a, b, gains, ms, table, cells,
):
    loads = io.get((table_in, table), (ms_in, ms), (cells_in, cells))
    loads += io.get((field, a), (noise, b), (norm_gain, gains))
    size = 2 * CH + 8
    copies = io.get(
        (small, tail.at[0:VROWS]),
        (mix_one, tail.at[VROWS : VROWS + size]),
        (mix_zero, tail.at[VROWS + size : VROWS + 2 * size]),
    )
    wait(loads)
    col = column(gains[0, 0:1, :])
    gain_sum = jnp.zeros((CH, 1), f32)
    shift_sum = jnp.zeros((CH, 1), f32)
    for s in range(NZ):
        here = slice(s * CELLS, (s + 1) * CELLS)
        up = cells[s].astype(f32)
        dy = (dot(table[...], modes[s]) + up).T
        up = up.T
        v = a[:, here].astype(f32) + b[:, here].astype(f32)
        unit = (v - ms[0:1, here]) * ms[1:2, here]
        dx = dy * col
        sums[0:1, here] = jnp.sum(dx, axis=0, keepdims=True)
        sums[1:2, here] = jnp.sum(dx * unit, axis=0, keepdims=True)
        base[:, here] = up + ms[1:2, here] * dx
        gain_sum = gain_sum + jnp.sum(dy * unit, axis=1, keepdims=True)
        shift_sum = shift_sum + jnp.sum(dy, axis=1, keepdims=True)
    wait(copies)
    on = diagonal(CH)
    first = VROWS + 2 * size
    tail[first : first + 8, :] = jnp.zeros((8, CH), f32)
    tail[first : first + 1, :] = jnp.sum(jnp.where(on, gain_sum, 0.0), axis=0, keepdims=True)
    tail[first + 1 : first + 2, :] = jnp.sum(
        jnp.where(on, shift_sum, 0.0), axis=0, keepdims=True
    )


def close_body(ids, io, base, s0, s1, ms_in, field, noise, out, a, b, ms, result):
    loads = io.get((field, a), (noise, b), (ms_in, ms))
    mean = (s0[0:1, :] + s1[0:1, :]) * (1.0 / D)
    along = (s0[1:2, :] + s1[1:2, :]) * (1.0 / D)
    wait(loads)
    for s in range(NZ):
        here = slice(s * CELLS, (s + 1) * CELLS)
        v = a[:, here].astype(f32) + b[:, here].astype(f32)
        unit = (v - ms[0:1, here]) * ms[1:2, here]
        result[:, here] = base[:, here] - ms[1:2, here] * (mean[:, here] + unit * along[:, here])
        io.put(result.at[:, here], out.at[:, here])


def groups(arrays):
    return [arrays[0].at[s] for s in range(NZ)] if len(arrays) == 1 else list(arrays)


def mixing_matrix(real, imag):
    first = lax.broadcasted_iota(jnp.int32, (CH, CH), 0) // BS
    on = first == lax.broadcasted_iota(jnp.int32, (CH, CH), 1) // BS

    def spread(part):
        part = part.astype(f32).T
        return jnp.where(on, jnp.concatenate([part, part], axis=1), 0.0)

    real, imag = spread(real), spread(imag)
    top = jnp.concatenate([real, imag], axis=1)
    bottom = jnp.concatenate([-imag, real], axis=1)
    return jnp.concatenate([top, bottom], axis=0).astype(bf16)


def to_spectrum(table, own, other, out):
    sources = groups([own]) + groups([other])
    for k in range(0, MODES, 2):
        sides = [
            jnp.concatenate([source[SPAN * n : SPAN * (n + 1), :] for source in sources], axis=0)
            for n in (k, k + 1)
        ]
        modes = dot(table, jnp.concatenate(sides, axis=1)).astype(out.dtype)
        for n in range(2):
            here = slice(MODES * (k + n), MODES * (k + n + 1))
            out[here, :CH] = modes[:MODES, n * CH : (n + 1) * CH]
            out[here, CH:] = modes[MODES:, n * CH : (n + 1) * CH]


def from_spectrum(table, spectrum, outs):
    targets = groups(outs)
    for k in range(0, MODES, 2):
        sides = []
        for n in (k, k + 1):
            here = slice(MODES * n, MODES * (n + 1))
            sides.append(jnp.concatenate([spectrum[here, :CH], spectrum[here, CH:]], axis=0))
        cells = dot(table, jnp.concatenate(sides, axis=1)).astype(bf16)
        for n in range(2):
            rows = slice(SPAN * (k + n), SPAN * (k + n + 1))
            for m, target in enumerate(targets):
                target[rows, :] = cells[SPAN * m : SPAN * (m + 1), n * CH : (n + 1) * CH]


def variant(ids, cells):
    return ids[0] * (NZ + 1) + (ids[1] if cells else NZ)


def mix_body(layer, cells, ids, io, own, other, table, back, weight, bias, *refs):
    refs, take = list(refs), lambda n: [refs.pop(0) for _ in range(n)]
    outs, saved = take(NZ if cells else 1), take(4)
    spectrum, active, slope, square = refs
    which = variant(ids, cells)
    to_spectrum(table[which], own, other, spectrum)
    io.put(spectrum, saved[0])

    def product(j, values):
        matrix = mixing_matrix(weight[layer, j, 0], weight[layer, j, 1])
        shift = jnp.concatenate([bias[layer, j, 0:1, :], bias[layer, j, 1:2, :]], axis=1)
        return dot(values, matrix) + shift.astype(f32)

    value, inner = gelu_parts(product(0, spectrum[...]))
    active[...] = value.astype(bf16)
    slope[...] = inner.astype(slope.dtype)
    io.put(active, saved[1])
    io.put(slope, saved[2])
    two = product(1, active[...])
    bend = jnp.tanh(two * (1.0 / shrink))
    square[...] = (bend * bend).astype(square.dtype)
    io.put(square, saved[3])
    from_spectrum(back[which], (two - shrink * bend).astype(bf16), outs)


def mix_back_body(layer, cells, ids, io, own, other, *refs):
    refs, take = list(refs), lambda n: [refs.pop(0) for _ in range(n)]
    if cells:
        table, back, weight = take(3)
        saved, which = take(4), variant(ids, cells)
    else:
        saved, (table_in, back_in, weight_in) = take(4), take(3)
    outs, (sums_out,) = take(NZ if cells else 1), take(1)
    spectrum, active, slope, square, low_one, low_two, sums, *rooms = refs
    if not cells:
        (table, back, weight), which = rooms, 0
        here = variant(ids, cells)
        wait(
            io.get(
                (table_in.at[here], table.at[0]), (back_in.at[here], back.at[0]), (weight_in, weight)
            )
        )
    share = at(ids[0] * HALF, HALF)
    late = io.get((saved[3], square), (saved[2], slope))
    later = io.get((saved[0].at[share], spectrum), (saved[1].at[share], active))
    to_spectrum(table[which], own, other, low_two)
    wait(late)

    def product(j, values):
        return dot(values, mixing_matrix(weight[layer, j, 0], weight[layer, j, 1]), NT)

    low_two[...] = (low_two[...].astype(f32) * square[...].astype(f32)).astype(bf16)
    low_one[...] = (product(1, low_two[...]) * slope[...].astype(f32)).astype(bf16)
    from_spectrum(back[which], product(0, low_one[...]).astype(bf16), outs)
    wait(later)
    lane = lax.broadcasted_iota(jnp.int32, (BS, CH), 1)
    sums[2 * CH :, :] = jnp.zeros((8, CH), f32)
    for j, (left, right) in enumerate(((spectrum, low_one), (active, low_two))):
        outer = dot(left[...], right[share, :], TN)
        real = outer[:CH, :CH] + outer[CH:, CH:]
        imag = outer[:CH, CH:] - outer[CH:, :CH]
        parts = jnp.concatenate(
            [
                jnp.where(lane < BS, real[:BS], pltpu.roll(imag[:BS], BS, 1)),
                jnp.where(lane < BS, pltpu.roll(real[BS:], BS, 1), imag[BS:]),
            ],
            axis=0,
        )
        sums[j * CH : (j + 1) * CH, :] = parts.T
        total = jnp.sum(right[share, :].astype(f32), axis=0, keepdims=True)
        first = 2 * CH + 2 * j
        sums[first : first + 1, :] = total[:, :CH]
        sums[first + 1 : first + 2, :] = total[:, CH:]
    io.put(sums, sums_out)


def load_weights(io, layer, ids, up, down, near, distant, store):
    place = ids[2]
    copies = io.get((up.at[layer], store.at[0, 0]), (down.at[layer], store.at[0, 1]))
    for core, array in enumerate((near, distant)):
        for side in range(2):
            for index, e in enumerate((0, 2, 4, 6) if side == 0 else (0, 4, 2, 6)):
                rows = at((place ^ e ^ core) * SLICE, SLICE)
                part = array.at[side, index]
                copies.append(io.start(part, store.at[1:NZ, side, rows]))
    return copies


def load_weights_one(io, ids, up, down, near, distant, store):
    copies = io.get((up.at[1], store.at[0, 0]), (down.at[1], store.at[0, 1]))
    for array, core in ((near, ids[0]), (distant, 1 - ids[0])):
        for chip in range(4):
            rows = at((2 * chip + core) * SLICE, SLICE)
            for side in range(2):
                part = array.at[chip, :, side * SLICE : (side + 1) * SLICE]
                copies.append(io.start(part, store.at[1:NZ, side, rows]))
    return copies


def fan_body(ids, io, arrived, out, held):
    wait([io.start(arrived.at[ids[1] ^ m], held.at[m - 1]) for m in range(1, NZ)])
    for chip in range(4):
        io.put(held, out.at[chip])


def gather_lanes(z, pieces, wide):
    for m, piece in enumerate(pieces):
        wide[:, at((z ^ m) * CH, CH)] = piece[...]


def scatter_lanes(z, wide, pieces):
    for m, piece in enumerate(pieces):
        piece[0:CELLS, :] = wide[:, at((z ^ m) * CH, CH)].astype(piece.dtype)


def store_send(io, core, chunk, place, keep, send):
    io.put(chunk.at[:, at(core * HID, HID)], keep)
    io.put(chunk.at[:, at((1 - core) * HID, HID)], send.at[place * CELLS : (place + 1) * CELLS])


def store_cells(io, values, place, send):
    for half in range(2):
        rows = slice((place + half) * CELLS, (place + half + 1) * CELLS)
        io.put(values.at[:, half * HID : (half + 1) * HID], send.at[rows])


def cells_one_body(
    ids, io, p0, p3, p2, p1, l0, l3, l2, l1, arrived, up, down, near, distant, table_in,
    a0, a3, a2, a1, vectors_out, up_shift_out, base_out, unit_one_out, scale_one_out,
    unit_two_out, scale_two_out, slope_out, low_out, keep, send, turned_out,
    store, wide, params, table, low, total, hidden, vectors, up_shift, base, unit_one, unit_two,
    scales, slope, turned, late,
):
    core, z = ids[0], ids[1]
    loads = [
        io.start(arrived.at[z ^ m, 2 * SLICE : 2 * SLICE + PARAMS, 0:CH], params.at[m])
        for m in range(NZ)
    ]
    loads += [
        io.start(p, wide.at[:, at((z ^ m) * CH, CH)]) for m, p in enumerate((p0, p1, p2, p3))
    ]
    pieces = [io.start(l, late.at[m]) for m, l in enumerate((l0, l1, l2, l3))]
    weights = load_weights(io, 0, ids, up, down, near, distant, store)
    last = io.get((table_in, table))
    wait(loads)
    for m in range(NZ):
        rows = params[m].astype(f32)
        vectors[0:10, at((z ^ m) * CH, CH)] = rows[0:10]
        for l in range(LAYERS):
            top = 10 + NZ * l
            shift = jnp.concatenate([rows[top + q : top + q + 1] for q in range(NZ)], axis=1)
            up_shift[l, m : m + 1, :] = shift
    io.put(vectors, vectors_out)
    io.put(up_shift, up_shift_out)
    state = wide[...].astype(f32)
    normed, unit, scale = norm_rows(state, vectors[1:2, :], vectors[5:6, :])
    low[...] = normed.astype(bf16)
    unit_two[...] = unit.astype(bf16)
    scales[0] = jnp.broadcast_to(scale, (CELLS, CH))
    total[...] = state + vectors[8:9, :]
    io.put(unit_two, unit_two_out)
    io.put(scales.at[0], scale_two_out)
    io.put(low, low_out)
    store_cells(io, low, NZ, send)
    wait(pieces)
    for m in range(NZ):
        turned[:, at((z ^ m) * CH, CH)] = late[m].T
    io.put(turned, turned_out)
    wait(weights[:2])
    for j in range(NZ):
        if j == 1:
            wait(weights[2:])
        before = dot(low[...], store[j, 0]) + up_shift[0, j : j + 1, :]
        value, inner = gelu_parts(before)
        hidden[j] = value.astype(bf16)
        slope[j] = inner.astype(bf16)
        io.put(slope.at[j], slope_out.at[j])
        store_send(io, core, hidden.at[j], j, keep.at[j], send)
        total[...] += dot(hidden[j], store[j, 1])
    state = total[...]
    normed, unit, scale = norm_rows(state, vectors[2:3, :], vectors[6:7, :])
    base[...] = state + normed
    unit_one[...] = unit.astype(bf16)
    scales[1] = jnp.broadcast_to(scale, (CELLS, CH))
    io.put(base, base_out)
    io.put(unit_one, unit_one_out)
    io.put(scales.at[1], scale_one_out)
    wait(last)
    total[...] = dot(table[...], normed.astype(bf16))
    scatter_lanes(z, total, (a0, a1, a2, a3))


def fill_small(rows, ups, z, small):
    for m in range(NZ):
        small[m, 0:8, :] = rows[0:8, at((z ^ m) * CH, CH)]
        line = ups[m : m + 1, :]
        for q in range(NZ):
            small[m, 8 + q : 9 + q, :] = line[:, q * CH : (q + 1) * CH]
        small[m, 12:16, :] = jnp.zeros((4, CH), f32)


def cells_two_body(
    ids, io, arrived, base_in, vectors_in, up_shift_in,
    turned_in, up, down, near, distant, back_in, table_in,
    a0, a3, a2, a1, o0, o1, o2, o3, small_out, grad_out, low_out, hidden_keep,
    before_keep, send,
    store, wide, back_table, table, low, low_grad, unit_two, total, other, hidden,
    before_grad, ups, base, vectors, up_shift, small, grad, result,
):
    core, z = ids[0], ids[1]
    loads = io.get((back_in, back_table), (base_in, base), (vectors_in, vectors))
    loads += io.get((up_shift_in, up_shift))
    loads += io.get((turned_in, low_grad))
    weights = load_weights_one(io, ids, up, down, near, distant, store)
    last = io.get((table_in, table))
    gather_lanes(z, [arrived.at[place] for place in ORDER], wide)
    wait(loads)
    state = base[...] + dot(back_table[...], wide[...])
    normed, unit, scale = norm_rows(state, vectors[3:4, :], vectors[7:8, :])
    low[...] = normed.astype(bf16)
    io.put(low, low_out)
    store_cells(io, low, 2 * NZ, send)
    unit_two[...] = unit
    total[...] = state + vectors[9:10, :]
    other[...] = jnp.zeros_like(other)
    store_cells(io, low_grad, 2 * NZ + 2, send)
    wait(weights[:2])
    for j in range(NZ):
        if j == 1:
            wait(weights[2:])
        before = dot(low[...], store[j, 0]) + up_shift[1, j : j + 1, :]
        value, inner = gelu_parts(before)
        hidden[j] = value.astype(bf16)
        store_send(io, core, hidden.at[j], j, hidden_keep.at[j], send)
        total[...] += dot(hidden[j], store[j, 1])
        turn = dot(low_grad[...], store[j, 1], NT) * inner
        before_grad[j] = turn.astype(bf16)
        store_send(io, core, before_grad.at[j], NZ + j, before_keep.at[j], send)
        ups[j : j + 1, :] = jnp.sum(before_grad[j].astype(f32), axis=0, keepdims=True)
        other[...] += dot(before_grad[j], store[j, 0], NT)
    gradient = low_grad[...].astype(f32)
    change, gain_row, shift_row = norm_rows_back(other[...], unit_two[...], scale, vectors[3:4, :])
    grad[...] = gradient + change
    io.put(grad, grad_out)
    result[...] = total[...].astype(bf16)
    for m, out in enumerate((o0, o1, o2, o3)):
        io.put(result.at[:, at((z ^ m) * CH, CH)], out)
    wait(last)
    total[...] = dot(table[...], grad[...].astype(bf16))
    scatter_lanes(z, total, (a0, a1, a2, a3))
    other[0:8, :] = jnp.zeros((8, D), f32)
    other[0:1, :] = gain_row
    other[1:2, :] = shift_row
    other[2:3, :] = jnp.sum(gradient, axis=0, keepdims=True)
    fill_small(other, ups, z, small)
    io.put(small, small_out)


def cells_three_body(
    ids, io, b0, b3, b2, b1, grad_in, unit_one_in, scale_one_in, unit_two_in, scale_two_in,
    vectors_in, small_in, slope_in, up, down, near, distant, back_in,
    g0, g3, g2, g1, low_grad_out, keep, send,
    store, wide, back_table, low_grad, total, other, before_grad, ups, small, grad, unit_one,
    unit_two, scales, vectors, small_one, slope,
):
    core, z = ids[0], ids[1]
    loads = io.get((back_in, back_table), (grad_in, grad), (vectors_in, vectors))
    loads += io.get((unit_one_in, unit_one), (scale_one_in, scales.at[0]))
    slopes = [io.start(slope_in.at[0], slope.at[0])]
    weights = load_weights(io, 0, ids, up, down, near, distant, store)
    slopes += [io.start(slope_in.at[j], slope.at[j]) for j in range(1, NZ)]
    later = io.get((unit_two_in, unit_two), (scale_two_in, scales.at[1]), (small_in, small_one))
    gather_lanes(z, (b0, b1, b2, b3), wide)
    wait(loads)
    dy = grad[...] + dot(back_table[...], wide[...])
    change, gain_one, shift_one = norm_rows_back(
        dy, unit_one[...].astype(f32), scales[0, :, 0:1], vectors[2:3, :]
    )
    total[...] = grad[...] + change
    low_grad[...] = total[...].astype(bf16)
    io.put(low_grad, low_grad_out)
    store_cells(io, low_grad, NZ, send)
    other[...] = jnp.zeros_like(other)
    wait(weights[:2])
    for j in range(NZ):
        slopes[j].wait()
        if j == 1:
            wait(weights[2:])
        turn = dot(low_grad[...], store[j, 1], NT) * slope[j].astype(f32)
        before_grad[j] = turn.astype(bf16)
        store_send(io, core, before_grad.at[j], j, keep.at[j], send)
        ups[j : j + 1, :] = jnp.sum(before_grad[j].astype(f32), axis=0, keepdims=True)
        other[...] += dot(before_grad[j], store[j, 0], NT)
    wait(later)
    change, gain_two, shift_two = norm_rows_back(
        other[...], unit_two[...].astype(f32), scales[1, :, 0:1], vectors[1:2, :]
    )
    total[...] += change
    pieces = (g0, g1, g2, g3)
    scatter_lanes(z, total, pieces)
    other[0:8, :] = jnp.zeros((8, D), f32)
    other[0:1, :] = gain_two
    other[1:2, :] = shift_two
    other[2:3, :] = jnp.sum(low_grad[...].astype(f32), axis=0, keepdims=True)
    other[3:4, :] = gain_one
    other[4:5, :] = shift_one
    fill_small(other, ups, z, small)
    for m, piece in enumerate(pieces):
        rows = jnp.concatenate([small_one[m], small[m]], axis=0)
        high = rows.astype(bf16)
        piece[CELLS : CELLS + VROWS, :] = high
        piece[CELLS + VROWS : CELLS + 2 * VROWS, :] = (rows - high.astype(f32)).astype(bf16)


def weights_body(
    places, ids, io, low_own, grad_own, hidden_own, before_own, *refs
):
    lows, left, right, product = refs[-4:]
    count = 1 + max(array for array, _ in places.values())
    sent, parts = refs[:count], refs[count:-4]

    def other(name, chunk):
        array, first = places[name]
        return sent[array].at[(first + chunk) * CELLS : (first + chunk + 1) * CELLS]

    loads = io.get((low_own, lows.at[0, 0]), (grad_own, lows.at[1, 0]))
    for side, name in enumerate(("low", "grad")):
        for half in range(2):
            target = lows.at[side, 1, :, half * HID : (half + 1) * HID]
            loads.append(io.start(other(name, half), target))
    later = []
    for j in range(NZ):
        step = []
        for side, (value, name) in enumerate(((before_own, "before"), (hidden_own, "hidden"))):
            step.append(io.start(value.at[j], right.at[j, side, 0:CELLS]))
            step.append(io.start(other(name, j), right.at[j, side, CELLS : 2 * CELLS]))
        later.append(step)
    wait(loads)
    for side in range(2):
        for half in range(2):
            left[side, :, half * CELLS : (half + 1) * CELLS] = lows[side, half].T
    for j in range(NZ):
        wait(later[j])
        for side in range(2):
            product[j, side] = dot(left[side], right[j, side]).astype(bf16)
        for q in range(4):
            if len(parts) == 1:
                rows, part = slice(q * QUARTER, (q + 1) * QUARTER), parts[0].at[q]
            else:
                rows, part = at(((ids[2] // 2) ^ q) * QUARTER, QUARTER), parts[q]
            io.put(product.at[j, :, rows], part.at[j])


def plane_sum_body(ids, io, k1, k2, k3, k0, t0, t1, t2, t3, own):
    wait(io.get((k0, own)))
    for m, out in enumerate((t0, t1, t2, t3)):
        part = own[m].astype(f32) + k1[m].astype(f32)
        part = part + (k2[m].astype(f32) + k3[m].astype(f32))
        out[...] = part.astype(out.dtype)


def all_sum_body(ids, io, parts, out, held):
    loads = [io.start(parts.at[:, m], held.at[:, m]) for m in range(NZ)]
    for m in range(NZ):
        loads[m].wait()
        part = held[0, m].astype(f32) + held[1, m].astype(f32)
        part = part + (held[2, m].astype(f32) + held[3, m].astype(f32))
        out[ids[1] ^ m] = part.astype(bf16)


def output_body(ids, io, o0, ms_in, o3, o2, o1, out, held, wide, ms):
    z = ids[1]
    first = io.get((ms_in, ms))
    loads = [io.start(o, held.at[m]) for m, o in enumerate((o0, o1, o2, o3))]
    wait(first)
    for m in range(NZ):
        loads[m].wait()
        here = at((z ^ m) * CELLS, CELLS)
        wide[m] = (held[m].astype(f32).T + ms[0:1, here]).astype(bf16)
        io.put(wide.at[m], out.at[:, here])


def weights_out_body(layer, ids, io, *refs):
    core, chip = ids[0], ids[2] // 2
    pieces = refs[:8]
    up, down, both, result = refs[-4:]
    for e, piece in enumerate(pieces):
        rows, lanes = at((chip ^ (e // 2)) * QUARTER, QUARTER), at((core ^ (e % 2)) * HID, HID)
        both[:, rows, lanes] = piece[...]
    result[0] = both[0].astype(f32)
    io.put(result.at[0], up.at[layer])
    result[1] = both[1].T.astype(f32)
    io.put(result.at[1], down.at[layer])


def small_body(
    ids, io, left, right, gain_out, shift_out, mix_out, mix_bias_out, up_out, down_out,
    total, gain, shift, mix_bias, up, down,
):
    total[...] = left[...] + right[...]
    size = 2 * CH + 8
    first, zero, one = VROWS + 2 * size, VROWS // 2, 0
    blocks = (VROWS + size, VROWS)
    for l in range(LAYERS):
        for j in range(2):
            for part in range(2):
                here = blocks[l] + (2 * j + part) * BS
                io.put(total.at[here : here + BS], mix_out.at[l, j, part])
                here = blocks[l] + 2 * CH + 2 * j + part
                mix_bias[l, j, part : part + 1, :] = total[here : here + 1, :]
    for place, out, rows in (
        ((0, 0), gain, first), ((0, 1), gain, zero), ((1, 0), gain, zero + 3), ((1, 1), gain, one),
        ((0, 0), shift, first + 1), ((0, 1), shift, zero + 1), ((1, 0), shift, zero + 4),
        ((1, 1), shift, one + 1),
    ):
        l, j = place
        out[l, j : j + 1, :] = total[rows : rows + 1, :]
    for l, here in enumerate((zero, one)):
        down[l : l + 1, :] = total[here + 2 : here + 3, :]
        for q in range(NZ):
            up[l : l + 1, q * CH : (q + 1) * CH] = total[here + 8 + q : here + 9 + q, :]
    for source, out in (
        (gain, gain_out), (shift, shift_out), (mix_bias, mix_bias_out), (up, up_out),
        (down, down_out),
    ):
        io.put(source, out)


def swap(value, axis, mask):
    pairs = [(source, source ^ mask) for source in range(lax.axis_size(axis))]
    return lax.ppermute(value, axis, pairs)


def after(values, *done):
    values = list(values)
    return list(lax.optimization_barrier((*values, *done))[: len(values)])


def exchange(pieces):
    return [pieces[0]] + [swap(pieces[m], "narrow", m) for m in range(1, NZ)]


def in_order(pieces):
    return [pieces[m] for m in ORDER]


def spread(value):
    return lax.all_to_all(value, "narrow", 0, 0)


def chips():
    return [
        [8 * g + 2 * chip + core for chip in range(4)]
        for g in range(lax.axis_size("wide") // 8)
        for core in range(2)
    ]


def wide_total(value, mask, end):
    while mask < end:
        value = value + swap(value, "wide", mask)
        mask *= 2
    return value


def shards(
    field,
    noise,
    norm_gain,
    norm_bias,
    mix_weight,
    mix_bias,
    up_weight,
    up_bias,
    down_weight,
    down_bias,
    out_grad,
):
    wide, z = lax.axis_index("wide"), lax.axis_index("narrow")
    core, place = wide % 2, wide % 8
    ids = jnp.stack([core, z, place]).astype(jnp.int32)
    table, doubled, table_back, doubled_back = width_tables()
    height, height_back = height_tables()

    weight_turned = jnp.swapaxes(mix_weight, 3, 4)

    line_low, pair = vm((CH, LINE), bf16), vm((2, LINE), f32)
    params_two = vm((LAYERS, 2, CH), bf16)
    square_low, square_f32 = vm((D, D), bf16), vm((D, D), f32)
    chunks = vm((NZ, CELLS, D), bf16)
    store = vm((NZ, 2, D, D), bf16)
    up_rows, vector_rows = vm((NZ, D), f32), vm((10, D), f32)
    shift_rows = vm((LAYERS, NZ, D), f32)
    small_vm, two_scales = vm((NZ, VROWS // 2, CH), f32), vm((2, CELLS, CH), f32)
    piece_vm, group_vm = vm((CELLS, CH), bf16), vm((NZ, D, CH), bf16)
    modes_vm, share_vm = vm((NMODE, 2 * CH), bf16), vm((HALF, 2 * CH), bf16)
    mix_sums = (2 * CH + 8, CH)
    table_vms = [vm((1, 2 * MODES, 2 * GRID), bf16), vm((1, GRID, 2 * MODES), bf16)]
    table_vms.append(vm((LAYERS, 2, 2, BS, CH), bf16))


    own_piece, piece, far_piece = [kind((CELLS, CH), bf16) for kind in (auto, sds, far)]
    group = auto((NZ, D, CH), bf16)
    far_modes = far((NMODE, 2 * CH), bf16)
    far_low, far_f32, far_thin = far((CELLS, D), bf16), far((CELLS, D), f32), far((CELLS, CH), f32)
    halves, whole = far((NZ, CELLS, HID), bf16), far((NZ, CELLS, D), bf16)
    send = far(((NZ + 2) * CELLS, HID), bf16)
    parts = far((NZ, 2, QUARTER, HID), bf16)
    line_sums = auto((2, LINE), f32)
    far_small = far((NZ, VROWS // 2, CH), f32)

    def mix(layer, cells, own, other):
        outs = launch(
            lambda *refs: mix_body(layer, cells, *refs),
            "mix",
            ids,
            [own, other, height, height_back, weight_turned, mix_bias],
            [],
            ([own_piece] + [piece] * 3 if cells else [group]) + [far_modes] * 4,
            [modes_vm] * 4,
            16,
        )
        pieces = list(outs[:-4])
        return pieces[:1] + pieces[:0:-1], outs[-4:]

    def mix_back(layer, cells, own, other, saved):
        tables = [height, height_back, weight_turned]
        outs = launch(
            lambda *refs: mix_back_body(layer, cells, *refs),
            "mix_back",
            ids,
            [own, other] + (tables if cells else []),
            [*saved] + ([] if cells else tables),
            ([own_piece] + [piece] * 3 if cells else [group]) + [far(mix_sums, f32)],
            [share_vm, share_vm, modes_vm, modes_vm, modes_vm, modes_vm, vm(mix_sums, f32)]
            + ([] if cells else table_vms),
            16,
        )
        pieces = list(outs[:-1])
        return pieces[:1] + pieces[:0:-1], outs[-1]

    def first_step(arrived):
        others = [lax.dynamic_index_in_dim(arrived, z ^ m, 0, False) for m in range(1, NZ)]
        ups = jnp.stack([r[:SLICE] for r in others])
        downs = jnp.stack([r[SLICE : 2 * SLICE] for r in others])
        return ups, downs, swap(ups, "wide", 2), swap(downs, "wide", 4)

    def second_step(ups, downs, ups_near, downs_near):
        ups, downs = jnp.stack([ups, ups_near]), jnp.stack([downs, downs_near])
        return ups, downs, swap(ups, "wide", 4), swap(downs, "wide", 2)

    def third_step(ups, downs, ups_far, downs_far):
        held = jnp.stack(
            [jnp.concatenate([ups, ups_far]), jnp.concatenate([downs, downs_far])]
        )
        return held, swap(held, "wide", 1)

    def fan(arrived):
        sent = launch(
            fan_body, "fan", ids, [], [Arrived(arrived)], [far((4, 3, 2 * SLICE, D), bf16)],
            [vm((3, 2 * SLICE, D), bf16)], 12,
        )[0]
        return sent

    own, mine = launch(
        stats_body,
        "stats",
        ids,
        [],
        [field, noise, norm_gain, norm_bias, down_bias, up_bias, up_weight, down_weight],
        [line_sums, far((NZ, 2 * SLICE + PARAMS, D), bf16)],
        [line_low, line_low, params_two, params_two, vm((LAYERS, CH), bf16)]
        + [vm((LAYERS, D), bf16), vm((PARAMS, D), bf16), vm((2 * SLICE, D), bf16)],
        12,
    )
    first_sums = [own] + [swap(own, "narrow", m) for m in range(1, NZ)]
    zero = spread(after([mine], *first_sums[1:])[0])

    modes, ms, *late, mine_one = launch(
        first_body,
        "first",
        ids,
        first_sums,
        [field, noise, norm_gain, norm_bias, table, up_weight, down_weight, out_grad],
        [group, far((2, LINE), f32)]
        + [far((CH, CELLS), bf16)] * NZ
        + [far((NZ, 2 * SLICE, D), bf16)],
        [line_low, line_low, params_two, params_two, square_low, pair]
        + [vm((NZ, CH, CELLS), bf16), vm((2 * SLICE, D), bf16)],
        16,
    )
    (modes,), saved_zero = mix(0, False, modes, swap(modes, "wide", 1))
    spread_zero = second_step(*first_step(after([zero], modes)[0]))
    late = exchange([late[0], *after(late[1:], modes)])
    p3, p2, p1, p0 = launch(
        second_body,
        "second",
        ids,
        [modes],
        [ms, field, noise, norm_gain, norm_bias, doubled_back],
        [piece] * 3 + [far_piece],
        [line_low, line_low, params_two, params_two, pair, square_low, group_vm, piece_vm],
        16,
    )
    p1, p2, p3 = after([p1, p2, p3], *late[1:])
    state = exchange([p0, p1, p2, p3])
    ups_zero, downs_zero = after(spread_zero[2:], *state[1:])
    weights_zero = third_step(*spread_zero[:2], ups_zero, downs_zero)

    one = spread(after([mine_one], *state[1:])[0])

    (
        a0, a3, a2, a1, vectors, up_shift, base, unit_one, scale_one, unit_two, scale_two, slope,
        low_zero, hidden_zero, send_zero, grad_one,
    ) = launch(
        cells_one_body,
        "cells_one",
        ids,
        [],
        [state[0], *map(Arrived, state[:0:-1]), late[0], *map(Arrived, late[:0:-1]), Arrived(zero), up_weight, down_weight, *map(Arrived, weights_zero), table],
        [own_piece]
        + [piece] * 3
        + [far((10, D), f32), far((LAYERS, NZ, D), f32)]
        + [far_f32, far_low, far_thin, far_low, far_thin, whole]
        + [far_low, halves, send, far_low],
        [store, square_low, vm((NZ, PARAMS, CH), bf16), square_low, square_low, square_f32]
        + [chunks, vector_rows, shift_rows, square_f32, square_low, square_low, two_scales]
        + [chunks, square_low, vm((NZ, CH, CELLS), bf16)],
        28,
    )

    sent_one = fan(after([one], a0)[0])
    own = jnp.stack(after(in_order(exchange([a0, a1, a2, a3])), sent_one))
    near_one = lax.all_to_all(sent_one, "wide", 0, 0, axis_index_groups=chips())
    modes, saved_one = mix(1, True, own, swap(own, "wide", 1))
    ready = modes[0]
    modes = jnp.stack(after(in_order(exchange(modes)), near_one))
    near_one = after([near_one], modes)[0]
    weights_one = [near_one, swap(near_one, "wide", 1)]
    first_other = swap(after([send_zero], ready)[0], "wide", 1)
    base = after([base], first_other)[0]

    (
        a0, a3, a2, a1, o0, o1, o2, o3, small, grad, low_one, hidden_one, before_one,
        send_one,
    ) = launch(
        cells_two_body,
        "cells_two",
        ids,
        [modes],
        [base, vectors, up_shift, grad_one, up_weight, down_weight]
        + [*map(Arrived, weights_one), doubled_back, doubled],
        [own_piece]
        + [piece] * 3
        + [far_piece] * 4
        + [far_small, far_f32, far_low, halves, halves]
        + [far(((2 * NZ + 4) * CELLS, HID), bf16)],
        [store, square_low, square_low, square_low, square_low, square_low]
        + [square_f32] * 3
        + [chunks, chunks, up_rows, square_f32, vector_rows, shift_rows, small_vm, square_f32]
        + [square_low],
        34,
    )

    def finish_weights(result, *done):
        mask = 8
        while mask < lax.axis_size("wide"):
            result = result + swap(result.astype(bf16), "wide", mask).astype(f32)
            mask *= 2
        result = result.astype(bf16)
        pieces = []
        for value in [result] + [swap(result, "wide", q) for q in (2, 4, 6)]:
            pieces += [value, swap(after([value], *done)[0], "wide", 1)]
        return pieces

    def weight_parts(name, places, operands, outs):
        return launch(
            lambda *refs: weights_body(places, *refs),
            name,
            ids,
            [],
            operands,
            outs,
            [vm((2, 2, CELLS, D), bf16), vm((2, D, 2 * CELLS), bf16)]
            + [vm((NZ, 2, 2 * CELLS, HID), bf16), vm((NZ, 2, D, HID), bf16)],
            20,
        )

    own = exchange([a0, a1, a2, a3])
    parts_one = weight_parts(
        "weights_one",
        {"hidden": (0, 0), "before": (0, NZ), "low": (0, 2 * NZ), "grad": (0, 2 * NZ + 2)},
        [low_one, grad_one, hidden_one, before_one, Arrived(swap(send_one, "wide", 1))],
        [parts] * 4,
    )
    own = jnp.stack(after(in_order(own), parts_one[0]))
    modes, mix_one = mix_back(1, True, own, swap(own, "wide", 1), saved_one)
    own_part, *other_parts = [parts_one[0], *after(parts_one[1:], modes[0])]
    modes = exchange(modes)
    other_parts[2] = after([other_parts[2]], *modes[1:])[0]
    other_parts = [swap(other_parts[q - 1], "wide", 2 * q) for q in (1, 2, 3)]

    g0, g3, g2, g1, grad_zero, before_zero, last_send = launch(
        cells_three_body,
        "cells_three",
        ids,
        in_order(modes),
        [grad, unit_one, scale_one, unit_two, scale_two, vectors, small, slope]
        + [up_weight, down_weight, *map(Arrived, weights_zero), table_back],
        [auto((CELLS + 2 * VROWS, CH), bf16)]
        + [sds((CELLS + 2 * VROWS, CH), bf16)] * 3
        + [far_low, halves, send],
        [store, square_low, square_low, square_low, square_f32, square_f32, chunks, up_rows]
        + [small_vm, square_f32, square_low, square_low, two_scales, vector_rows, small_vm]
        + [chunks],
        28,
    )
    last_send = after([last_send], *other_parts[:2])[0]
    last_other = swap(last_send, "wide", 1)
    gradient = exchange([g0, g1, g2, g3])
    (parts_zero,) = weight_parts(
        "weights_zero",
        {"hidden": (0, 0), "low": (0, NZ), "before": (1, 0), "grad": (1, NZ)},
        [low_zero, grad_zero, hidden_zero, before_zero, *map(Arrived, (first_other, last_other))],
        [far((4, NZ, 2, QUARTER, HID), bf16)],
    )
    gradient = [after([gradient[0]], parts_zero)[0]] + gradient[1:]
    parts_zero = after([parts_zero], other_parts[2])[0]
    parts_zero = lax.all_to_all(parts_zero, "wide", 0, 0, axis_index_groups=chips())
    modes, small, cells = launch(
        return_body,
        "return",
        ids,
        in_order(gradient),
        [doubled],
        [group, far((VROWS, CH), f32), far((NZ, D, CH), bf16)],
        [square_low, vm((VROWS, CH), f32), group_vm],
        12,
    )
    outs = exchange([o0, *after([o1, o2, o3], modes)])
    (modes,), mix_zero = mix_back(0, False, modes, swap(modes, "wide", 1), saved_zero)
    total_one = launch(
        plane_sum_body,
        "plane_sum",
        ids,
        other_parts,
        after([own_part], modes, *outs[1:]),
        [auto((2, QUARTER, HID), f32)] + [sds((2, QUARTER, HID), bf16)] * 3,
        [vm((NZ, 2, QUARTER, HID), bf16)],
        12,
    )
    total_one = exchange(total_one)
    size = VROWS + 2 * (2 * CH + 8) + 8
    base, sums, tail = launch(
        last_body,
        "last",
        ids,
        [modes],
        [cells, ms, small, mix_one, mix_zero, field, noise, norm_gain, table_back],
        [auto((CH, LINE), f32), line_sums, auto((size, CH), f32)],
        [line_low, line_low, params_two, pair, square_low, group_vm],
        20,
    )
    total_zero = launch(
        all_sum_body,
        "plane_sum_zero",
        ids,
        [],
        [Arrived(parts_zero)],
        [auto((NZ, 2, QUARTER, HID), bf16)],
        [vm((4, NZ, 2, QUARTER, HID), bf16)],
        12,
    )[0]
    output = launch(
        output_body,
        "output",
        ids,
        [],
        [outs[0], ms, *map(Arrived, after(outs[:0:-1], total_zero))],
        [far((CH, LINE), bf16)],
        [vm((NZ, CELLS, CH), bf16), vm((NZ, CH, CELLS), bf16), pair],
        12,
    )[0]
    sums = sums + swap(sums, "narrow", 1)
    grad_field = launch(
        close_body,
        "close",
        ids,
        after([base], total_zero) + [sums, swap(sums, "narrow", 2)],
        [ms, field, noise],
        [far((CH, LINE), f32)],
        [line_low, line_low, pair, vm((CH, LINE), f32)],
        16,
    )[0]
    tail = wide_total(tail, 1, 4)
    sums_zero = spread(after([total_zero], tail, *total_one[1:])[0])
    result_one = total_one[0]
    for value in total_one[:0:-1]:
        result_one = result_one + value.astype(f32)
    last_mask = lax.axis_size("wide") // 2
    tail = wide_total(tail, 4, last_mask)
    result_zero = jnp.sum(sums_zero.astype(f32), axis=0)
    small_shapes = [
        (LAYERS, 2, CH), (LAYERS, 2, CH), (LAYERS, 2, 2, BS, CH), (LAYERS, 2, 2, CH), (LAYERS, D),
        (LAYERS, CH),
    ]
    small = launch(
        small_body,
        "small",
        ids,
        [tail, swap(tail, "wide", last_mask)],
        [],
        [far(shape, f32) for shape in small_shapes],
        [vm((size, CH), f32)] + [vm(small_shapes[place], f32) for place in (0, 1, 3, 4, 5)],
        12,
    )
    grad_gain, grad_shift, grad_mix, grad_mix_bias, grad_up_bias, grad_down_bias = small
    grad_mix = grad_mix.swapaxes(3, 4)
    pieces_one = finish_weights(after([result_one], total_zero)[0])
    grads = launch(
        lambda *refs: weights_out_body(1, *refs),
        "weights_out_one",
        ids,
        pieces_one,
        [],
        [far((LAYERS, D, D), f32)] * 2,
        [vm((2, D, D), bf16), vm((2, D, D), f32)],
        12,
    )
    pieces_zero = finish_weights(result_zero, grad_field, output, grads[0], small[0])
    grad_up, grad_down = launch(
        lambda *refs: weights_out_body(0, *refs),
        "weights_out_zero",
        ids,
        pieces_zero,
        grads,
        [far((LAYERS, D, D), f32)] * 2,
        [vm((2, D, D), bf16), vm((2, D, D), f32)],
        12,
        {9: 0, 10: 1},
    )
    return (
        output,
        grad_field,
        grad_gain,
        grad_shift,
        grad_mix,
        grad_mix_bias,
        grad_up,
        grad_up_bias,
        grad_down,
        grad_down_bias,
    )


def solution(mesh):
    placed = (
        P("narrow", "wide"),
        P("narrow", "wide"),
        P(None, None, "narrow"),
        P(None, None, "narrow"),
        P(None, None, None, "narrow", None),
        P(None, None, None, "narrow"),
        P(None, None, "narrow"),
        P(None, "narrow"),
        P(None, "narrow", None),
        P(None, "narrow"),
        P("narrow", "wide"),
    )
    return jax.shard_map(
        shards,
        mesh=mesh,
        in_specs=placed,
        out_specs=(
            P("narrow", "wide"),
            P("narrow", "wide"),
            P(None, None, "narrow"),
            P(None, None, "narrow"),
            P(None, None, None, "narrow", None),
            P(None, None, None, "narrow"),
            P(None, None, "narrow"),
            P(None, "narrow"),
            P(None, "narrow", None),
            P(None, "narrow"),
        ),
        check_vma=False,
    )
```
